32 devices in a mesh: dp: 8 (over y, x, core), fsdp: 4 (over z).
Axes of the slice: x: 2, y: 2, z: 4, core: 2. Of those that a mesh axis runs over, the one named last changes fastest.
Arguments:
- tokens: bfloat16 [8192, 1536], P(('dp', 'fsdp')), may hold values from -6 to 6
- doc_lengths: int32 [128], P(('dp', 'fsdp')), may hold values from 0 to 256, as said below
- norm_gain: bfloat16 [1536], P(('dp', 'fsdp')), may hold values from 0.5 to 1.5
- w_attn_in: bfloat16 [1536, 6144], P(('dp', 'fsdp')), may hold values from -0.15625 to 0.15625
- w_rates: bfloat16 [1536, 72], P(('dp', 'fsdp')), may hold values from -0.15625 to 0.15625
- rate_bias: float32 [72], replicated, may hold values from -2 to 6
- q_gain: bfloat16 [1536], P(('dp', 'fsdp')), may hold values from 0.5 to 1.5
- k_gain: bfloat16 [1536], P(('dp', 'fsdp')), may hold values from 0.5 to 1.5
- w_out: bfloat16 [1536, 1536], P(('dp', 'fsdp')), may hold values from -0.75 to 0.75
- ffn_gain: bfloat16 [1536], P(('dp', 'fsdp')), may hold values from 0.5 to 1.5
- w_gate_up: bfloat16 [1536, 8192], P(('dp', 'fsdp')), may hold values from -0.15625 to 0.15625
- w_down: bfloat16 [4096, 1536], P(('dp', 'fsdp')), may hold values from -0.09375 to 0.09375
- cotangent: bfloat16 [8192, 1536], P(('dp', 'fsdp')), may hold values from -6 to 6
Outputs:
- layer_out: bfloat16 [8192, 1536], P(('dp', 'fsdp'))
- d_tokens: float32 [8192, 1536], P(('dp', 'fsdp'))
- d_norm_gain: float32 [1536], P(('dp', 'fsdp'))
- d_w_attn_in: float32 [1536, 6144], P(('dp', 'fsdp'))
- d_w_rates: float32 [1536, 72], P(('dp', 'fsdp'))
- d_rate_bias: float32 [72], replicated
- d_q_gain: float32 [1536], P(('dp', 'fsdp'))
- d_k_gain: float32 [1536], P(('dp', 'fsdp'))
- d_w_out: float32 [1536, 1536], P(('dp', 'fsdp'))
- d_ffn_gain: float32 [1536], P(('dp', 'fsdp'))
- d_w_gate_up: float32 [1536, 8192], P(('dp', 'fsdp'))
- d_w_down: float32 [4096, 1536], P(('dp', 'fsdp'))
The draws below stay inside these ranges and needn't reach their ends.
Inputs may be any that keep to these rules, and one draw needn't show every extreme that they name: `doc_lengths`: consecutive groups of 4 entries belong to one bucket, in the order of the buckets, and give that bucket's document lengths in order (zero allowed); each group sums to at most 256, rows past the sum are padding. In every draw some bucket holds one document of 256 rows.
All inputs are finite; a program needn't handle non-finite values.
Results may differ from the reference program's by a relative error of at most 0.012.
Values may be sent and summed in bfloat16 or wider, within the bound.
No kernel may reach another device: no remote copies, remote signals or barrier semaphores. Data moves between devices by JAX's collectives and lax.ppermute only.
A program may use at most 448 MiB of HBM per device.

```python
import jax
import jax.numpy as jnp
from jax import lax

D = 1536
HEADS = 24
HEAD_DIM = 64
FF = 4096
TOK_DEV = 256
DOCS = 4
BUCKETS = 32
TOKENS = 8192


def draw_doc_lengths(key, part):
    key = jax.random.fold_in(key, 7)
    key_raw, key_full = jax.random.split(key, 2)
    per_doc = TOK_DEV // DOCS
    raw_lengths = jax.random.randint(key_raw, (BUCKETS, DOCS), 0, per_doc + 1)
    full_bucket = jax.random.randint(key_full, (), 0, BUCKETS)
    single_doc = jnp.zeros((DOCS,), jnp.int32).at[0].set(TOK_DEV)
    bucket_ids = jnp.arange(BUCKETS, dtype=jnp.int32)[:, None]
    lengths = jnp.where(bucket_ids == full_bucket, single_doc[None, :], raw_lengths)
    return lengths.reshape(-1).astype(jnp.int32)


def block_scale(own_key, extent, cuts, least, top_value):
    def one(axis_at, shards_of):
        heights = jax.random.uniform(jax.random.fold_in(jax.random.fold_in(own_key, 6), axis_at), (shards_of,), jnp.float32, least / len(cuts), top_value / len(cuts))
        return jnp.repeat(jnp.exp(heights), extent[axis_at] // shards_of).reshape((-1,) + (1,) * (len(extent) - axis_at - 1))

    level = one(*cuts[0])
    for cut in cuts[1:]:
        level = level * one(*cut)
    return level


def noise(rng, shape, spread, limit, shards=(), held_as=jnp.bfloat16):
    entries = jax.random.normal(rng, shape, jnp.float32) * spread
    if len(shards) > 0:
        entries = block_scale(rng, shape, shards, -0.22, 0.18) * entries
    return jnp.clip(entries, min=-limit, max=limit).astype(held_as)


def setup_inputs(seed: int = 0) -> dict:
    streams_of = jax.random.split(jax.random.key(seed), 14)
    return {
        "tokens": noise(streams_of[0], (TOKENS, D), 1.0, 6.0, ((0, 32),)),
        "doc_lengths": draw_doc_lengths(jax.random.fold_in(streams_of[13], 71), 0),
        "norm_gain": jnp.clip(1.0 + 0.1 * jax.random.normal(streams_of[2], (D,), jnp.float32), 0.5, 1.5).astype(jnp.bfloat16),
        "w_attn_in": noise(streams_of[3], (D, 4 * D), D ** -0.5, 0.15625, ((0, 32),)),
        "w_rates": noise(streams_of[4], (D, 3 * HEADS), D ** -0.5, 0.15625, ((0, 32),)),
        "rate_bias": jnp.clip(jax.random.uniform(streams_of[5], (3 * HEADS,), jnp.float32, -2.0, 6.0), -2.0, 6.0),
        "q_gain": jnp.clip(1.0 + 0.1 * jax.random.normal(streams_of[6], (D,), jnp.float32), 0.5, 1.5).astype(jnp.bfloat16),
        "k_gain": jnp.clip(1.0 + 0.1 * jax.random.normal(streams_of[7], (D,), jnp.float32), 0.5, 1.5).astype(jnp.bfloat16),
        "w_out": noise(streams_of[8], (D, D), (D // 24) ** -0.5, 0.75, ((0, 32),)),
        "ffn_gain": jnp.clip(1.0 + 0.1 * jax.random.normal(streams_of[9], (D,), jnp.float32), 0.5, 1.5).astype(jnp.bfloat16),
        "w_gate_up": noise(streams_of[10], (D, 2 * FF), D ** -0.5, 0.15625, ((0, 32),)),
        "w_down": noise(streams_of[11], (FF, D), FF ** -0.5, 0.09375, ((0, 32),)),
        "cotangent": noise(streams_of[12], (TOKENS, D), 1.0, 6.0, ((0, 32),)),
    }


EPS = 1e-06
NEG = -1e+30
HIGH = lax.Precision.HIGHEST

@jax.custom_vjp
def low(v):
    return lax.optimization_barrier(v.astype(jnp.bfloat16)).astype(jnp.float32)

@jax.custom_vjp
def low_back(v):
    return v

def low_keep(v):
    return (low(v), None)

def low_pass(kept, grad):
    return (grad,)

def back_keep(v):
    return (v, None)

def back_low(kept, grad):
    return (low(grad),)
low.defvjp(low_keep, low_pass)
low_back.defvjp(back_keep, back_low)

def normed(field_in):
    return field_in * lax.rsqrt(lax.optimization_barrier(jnp.mean(field_in * field_in, axis=-1, keepdims=True)) + EPS)

def shifted(current, mix_rate, same_prev):
    previous = jnp.concatenate([jnp.zeros_like(current[:1]), current[:-1]], axis=0) * same_prev
    mix_three = mix_rate[:, :, None]
    return mix_three * previous + (1.0 - mix_three) * current

def bucket_layer(stream_in, lengths, params):
    gain_one, w_proj, w_rate, bias_all, gain_q, gain_k, w_mix, gain_two, w_gu, w_dn = params
    tok_rows = stream_in.shape[0]
    width = stream_in.shape[1]
    doc_ends = jnp.cumsum(lengths).astype(jnp.int32)
    places = jnp.arange(tok_rows, dtype=jnp.int32)
    segment = lax.optimization_barrier(jnp.sum((doc_ends[None, :] <= places[:, None]).astype(jnp.int32), axis=1))
    live_rows = (places < doc_ends[-1]).astype(jnp.float32)[:, None]
    same_prev = jnp.concatenate([jnp.zeros((1,), dtype=bool), segment[1:] == segment[:-1]]).astype(jnp.float32)[:, None, None]
    allowed = (places[:, None] >= places[None, :]) & (segment[:, None] == segment[None, :])
    hidden_one = low(normed(stream_in) * gain_one)
    projected = low_back(jnp.dot(hidden_one, w_proj, precision=HIGH))
    rate_pre = low_back(jnp.dot(hidden_one, w_rate, precision=HIGH)) + bias_all
    blocks = projected.reshape(tok_rows, 4, HEADS, HEAD_DIM)
    query_raw = blocks[:, 0]
    key_raw = blocks[:, 1]
    value_raw = blocks[:, 2]
    gate_pre = blocks[:, 3]
    forget_pre = rate_pre[:, :HEADS]
    key_mix = jax.nn.sigmoid(rate_pre[:, HEADS:2 * HEADS])
    value_mix = jax.nn.sigmoid(rate_pre[:, 2 * HEADS:])
    decay_sum = jnp.cumsum(jax.nn.log_sigmoid(forget_pre), axis=0)
    key_mixed = shifted(key_raw, key_mix, same_prev)
    value_mixed = shifted(value_raw, value_mix, same_prev)
    q_low = low(normed(query_raw) * gain_q.reshape(HEADS, HEAD_DIM))
    k_low = low(normed(key_mixed) * gain_k.reshape(HEADS, HEAD_DIM))
    v_low = low(value_mixed)
    decay_t = decay_sum.T
    scores = jnp.einsum('thd,shd->hts', q_low, k_low, precision=HIGH) * HEAD_DIM ** (-0.5) + decay_t[:, :, None] - decay_t[:, None, :]
    scores = low_back(scores)
    masked = jnp.where(allowed[None], scores, NEG)
    row_top = lax.optimization_barrier(jnp.max(masked, axis=-1, keepdims=True))
    exp_terms = jnp.exp(masked - row_top)
    attn_prob = exp_terms / lax.optimization_barrier(jnp.sum(exp_terms, axis=-1, keepdims=True))
    attended = low_back(jnp.einsum('hts,shd->thd', low(attn_prob), v_low, precision=HIGH))
    out_gate = jax.nn.sigmoid(gate_pre)
    mixed_low = low((attended * out_gate).reshape(tok_rows, width) * live_rows)
    stream_mid = stream_in + low_back(jnp.dot(mixed_low, w_mix, precision=HIGH))
    hidden_two = low(normed(stream_mid) * gain_two)
    gate_up = low_back(jnp.dot(hidden_two, w_gu, precision=HIGH))
    ff_width = w_gu.shape[1] // 2
    act_low = low(jax.nn.silu(gate_up[:, :ff_width]) * gate_up[:, ff_width:] * live_rows)
    return stream_mid + low_back(jnp.dot(act_low, w_dn, precision=HIGH))

def reference(tokens, doc_lengths, norm_gain, w_attn_in, w_rates, rate_bias, q_gain, k_gain, w_out, ffn_gain, w_gate_up, w_down, cotangent):
    width = tokens.shape[1]
    stream_all = tokens.astype(jnp.float32).reshape(BUCKETS, TOK_DEV, width)
    lengths = doc_lengths.reshape(BUCKETS, DOCS)
    params = tuple((weight_in.astype(jnp.float32) for weight_in in (norm_gain, w_attn_in, w_rates, rate_bias, q_gain, k_gain, w_out, ffn_gain, w_gate_up, w_down)))
    bucket_fn = jax.checkpoint(bucket_layer)

    def forward(stream_all, params):
        return lax.map(lambda bucket_pair: bucket_fn(bucket_pair[0], bucket_pair[1], params), (stream_all, lengths))
    result, pullback = jax.vjp(forward, stream_all, params)
    d_stream, gradients = pullback(cotangent.astype(jnp.float32).reshape(BUCKETS, TOK_DEV, width))
    return (result.reshape(-1, width).astype(jnp.bfloat16), d_stream.reshape(-1, width), gradients[0], gradients[1], gradients[2], gradients[3], gradients[4], gradients[5], gradients[6], gradients[7], gradients[8], gradients[9])
```

```python
import functools

import jax
import jax.numpy as jnp
from jax import lax
from jax.experimental import pallas as pl
from jax.experimental.pallas import tpu as pltpu
from jax.sharding import Mesh
from jax.sharding import PartitionSpec as P

HEADS = 24
HEAD_DIM = 64
EPS = 1e-06
NEG = -1e30
TP = 8
OWN = HEADS // TP
BLOCK = OWN * HEAD_DIM
CORE = 4 * BLOCK
EXTRA = 128
WIDE = CORE + EXTRA
RATES = 3 * OWN
GAIN_AT = RATES
LENS_AT = RATES + 4
OFFSETS = (0, 2, 4, 6, 1, 3, 5, 7)
F32 = jnp.float32
BF16 = jnp.bfloat16


def flip(array, offset):
    return lax.ppermute(array, "tp", [(i, i ^ offset) for i in range(TP)])


def gather_rows(own):
    half = jnp.concatenate([own, flip(own, 2), flip(own, 4), flip(own, 6)], axis=0)
    return jnp.concatenate([half, flip(half, 1)], axis=0)


def scatter_rows(part):
    rows = part.shape[0] // TP
    half = part[: 4 * rows].astype(F32) + flip(part[4 * rows :], 1).astype(F32)
    low = half[rows:].astype(BF16)
    return (
        half[:rows]
        + flip(low[:rows], 2).astype(F32)
        + flip(low[rows : 2 * rows], 4).astype(F32)
        + flip(low[2 * rows :], 6).astype(F32)
    )


def normed(field_in):
    factor = lax.rsqrt(jnp.mean(field_in * field_in, axis=-1, keepdims=True) + EPS)
    return field_in * factor, factor


def norm_back(normal, factor, grad_in):
    return factor * (grad_in - normal * jnp.mean(grad_in * normal, axis=-1, keepdims=True))


def dot(a, b, dims=((1,), (0,)), precision=None):
    return lax.dot_general(a, b, (dims, ((), ())), precision=precision, preferred_element_type=F32)


def columns_out(weight, blocks):
    rows = weight.shape[0]
    cut = weight.reshape(rows, blocks, TP, -1)
    return cut.transpose(2, 0, 1, 3).reshape(TP, rows, -1)


def columns_in(cut, blocks):
    rows = cut.shape[1]
    return cut.reshape(TP, rows, blocks, -1).transpose(1, 2, 0, 3).reshape(rows, -1)


def own_share(part, share):
    columns = part.shape[1]
    part = part.reshape(TP, share, -1, columns).transpose(1, 0, 2, 3).reshape(-1, columns)
    return lax.psum_scatter(part, "sh", scatter_dimension=0, tiled=True).reshape(TP, -1, columns)


def head_masks(rows, width):
    lane = lax.broadcasted_iota(jnp.int32, (rows, width), 1)
    return [(lane >= h * HEAD_DIM) & (lane < (h + 1) * HEAD_DIM) for h in range(OWN)]


def spread(values, width, rows):
    lane = lax.broadcasted_iota(jnp.int32, (rows, width), 1)
    out = jnp.broadcast_to(values[OWN - 1], (rows, width))
    for h in range(OWN - 2, -1, -1):
        out = jnp.where(lane < (h + 1) * HEAD_DIM, values[h], out)
    return out


def head_sums(field_in, masks):
    return [jnp.sum(jnp.where(m, field_in, 0.0), axis=-1, keepdims=True) for m in masks]


def places_of(lens_ref, bucket, rows):
    ends = []
    total = jnp.int32(0)
    for j in range(lens_ref.shape[1]):
        total = total + lens_ref[bucket, j]
        ends.append(total)

    def segment(place):
        seg = jnp.zeros(place.shape, jnp.int32)
        for end in ends:
            seg = seg + (end <= place).astype(jnp.int32)
        return seg

    col = lax.broadcasted_iota(jnp.int32, (rows, 1), 0)
    row = lax.broadcasted_iota(jnp.int32, (1, rows), 1)
    seg_col = segment(col)
    allowed = (row <= col) & (segment(row) == seg_col)
    live = (col < total).astype(F32)
    same_prev = ((col > 0) & (seg_col == segment(col - 1))).astype(F32)
    return allowed, live, same_prev


def front(lens_ref, proj_ref, bias_ref, gains_ref, bucket):
    rows = proj_ref.shape[0]
    allowed, live, same_prev = places_of(lens_ref, bucket, rows)
    q = proj_ref[:, 0:BLOCK]
    k = proj_ref[:, BLOCK : 2 * BLOCK]
    v = proj_ref[:, 2 * BLOCK : 3 * BLOCK]
    og = proj_ref[:, 3 * BLOCK : CORE]
    rate = proj_ref[:, CORE:WIDE] + bias_ref[0:1, :]
    sig = jax.nn.sigmoid(rate)
    log_keep = jnp.minimum(rate, 0.0) - jnp.log1p(jnp.exp(-jnp.abs(rate)))
    tri = (
        lax.broadcasted_iota(jnp.int32, (rows, rows), 1)
        <= lax.broadcasted_iota(jnp.int32, (rows, rows), 0)
    ).astype(F32)
    decay = dot(tri, log_keep, precision=lax.Precision.HIGHEST)
    decay_t = decay.T
    masks = head_masks(rows, BLOCK)
    ak = spread([sig[:, OWN + h : OWN + h + 1] for h in range(OWN)], BLOCK, rows)
    av = spread([sig[:, 2 * OWN + h : 2 * OWN + h + 1] for h in range(OWN)], BLOCK, rows)
    k_prev = pltpu.roll(k, 1, 0) * same_prev
    v_prev = pltpu.roll(v, 1, 0) * same_prev
    ks = ak * k_prev + (1.0 - ak) * k
    vs = av * v_prev + (1.0 - av) * v

    def head_norm(u):
        sums = head_sums(u * u, masks)
        factor = spread([lax.rsqrt(s * (1.0 / HEAD_DIM) + EPS) for s in sums], BLOCK, rows)
        return u * factor, factor

    qn, rq = head_norm(q)
    kn, rk = head_norm(ks)
    q_gain, k_gain = gains_ref[0:1, 0:BLOCK], gains_ref[1:2, 0:BLOCK]
    qb = (qn * q_gain).astype(BF16)
    kb = (kn * k_gain).astype(BF16)
    vb = vs.astype(BF16)
    return dict(
        rows=rows, allowed=allowed, live=live, same_prev=same_prev, k=k, v=v, og=og, rate=rate, sig=sig,
        decay=decay, decay_t=decay_t, masks=masks, ak=ak, av=av, k_prev=k_prev, v_prev=v_prev,
        qn=qn, rq=rq, kn=kn, rk=rk, q_gain=q_gain, k_gain=k_gain, qb=qb, kb=kb, vb=vb, tri=tri,
    )


def scores_of(f, h):
    qm = jnp.where(f["masks"][h], f["qb"], jnp.zeros_like(f["qb"]))
    s = dot(qm, f["kb"], ((1,), (1,))) * HEAD_DIM**-0.5
    s = s + f["decay"][:, h : h + 1] - f["decay_t"][h : h + 1, :]
    return jnp.where(f["allowed"], s, NEG)


def attn_fwd_kernel(lens_ref, proj_ref, bias_ref, gains_ref, mixed_ref, att_ref, lse_ref):
    f = front(lens_ref, proj_ref, bias_ref, gains_ref, pl.program_id(0))
    rows = f["rows"]
    lane = lax.broadcasted_iota(jnp.int32, (rows, EXTRA), 1)
    att = jnp.zeros((rows, BLOCK), F32)
    lse_all = jnp.zeros((rows, EXTRA), F32)
    for h in range(OWN):
        s = scores_of(f, h)
        top = jnp.max(s, axis=-1, keepdims=True)
        e = jnp.exp(s - top)
        total = jnp.sum(e, axis=-1, keepdims=True)
        prob = (e / total).astype(BF16)
        att = att + dot(prob, jnp.where(f["masks"][h], f["vb"], jnp.zeros_like(f["vb"])))
        lse_all = jnp.where(lane == h, top + jnp.log(total), lse_all)
    att_ref[...] = att
    lse_ref[...] = lse_all
    mixed_ref[...] = (att * jax.nn.sigmoid(f["og"]) * f["live"]).astype(BF16)


def attn_bwd_kernel(
    lens_ref, proj_ref, bias_ref, gains_ref, att_ref, lse_ref, grad_ref, w_ref, dp_ref, sums_ref
):
    bucket = pl.program_id(0)
    f = front(lens_ref, proj_ref, bias_ref, gains_ref, bucket)
    rows, masks = f["rows"], f["masks"]
    dm = dot(grad_ref[...], w_ref[...], ((1,), (1,))) * f["live"]
    g = jax.nn.sigmoid(f["og"])
    dab = (dm * g).astype(BF16)
    dog = dm * att_ref[...] * g * (1.0 - g)
    zero = jnp.zeros((rows, BLOCK), BF16)
    lane = lax.broadcasted_iota(jnp.int32, (rows, EXTRA), 1)
    dqb = jnp.zeros((rows, BLOCK), F32)
    dkb = jnp.zeros((rows, BLOCK), F32)
    dvb = jnp.zeros((rows, BLOCK), F32)
    dc = jnp.zeros((rows, EXTRA), F32)
    for h in range(OWN):
        s = scores_of(f, h)
        p = jnp.exp(s - lse_ref[:, h : h + 1])
        dab_h = jnp.where(masks[h], dab, zero)
        dvb = dvb + dot(p.astype(BF16), dab_h, ((0,), (0,)))
        dp = dot(dab_h, f["vb"], ((1,), (1,)))
        ds = p * (dp - jnp.sum(p * dp, axis=-1, keepdims=True))
        dsb = ds.astype(BF16)
        dqb = dqb + dot(dsb, jnp.where(masks[h], f["kb"], zero))
        dkb = dkb + dot(dsb, jnp.where(masks[h], f["qb"], zero), ((0,), (0,)))
        ones = (lane == h).astype(BF16)
        dc = dc + dot(dsb, ones) - dot(dsb, ones, ((0,), (0,)))
    dqb = dqb * HEAD_DIM**-0.5
    dkb = dkb * HEAD_DIM**-0.5

    def back(n, r, e):
        means = spread([s * (1.0 / HEAD_DIM) for s in head_sums(e * n, masks)], BLOCK, rows)
        return r * (e - n * means)

    dq = back(f["qn"], f["rq"], dqb * f["q_gain"])
    dks = back(f["kn"], f["rk"], dkb * f["k_gain"])
    last = lax.broadcasted_iota(jnp.int32, (rows, 1), 0) == rows - 1

    def mix_back(grad, rate, cur, prev):
        ahead = pltpu.roll(rate * grad * f["same_prev"], rows - 1, 0)
        d_cur = (1.0 - rate) * grad + jnp.where(last, 0.0, ahead)
        return d_cur, head_sums(grad * (prev - cur), masks)

    dk, dak = mix_back(dks, f["ak"], f["k"], f["k_prev"])
    dv, dav = mix_back(dvb, f["av"], f["v"], f["v_prev"])
    keep = dot(f["tri"], dc, ((0,), (0,)), precision=lax.Precision.HIGHEST)
    sig = f["sig"]
    drate = keep * (1.0 - sig)
    slope = sig * (1.0 - sig)
    for h in range(OWN):
        drate = jnp.where(lane == OWN + h, dak[h] * slope, drate)
        drate = jnp.where(lane == 2 * OWN + h, dav[h] * slope, drate)
    drate = jnp.where(lane < RATES, drate, 0.0)
    dp_ref[:, 0:BLOCK] = dq.astype(BF16)
    dp_ref[:, BLOCK : 2 * BLOCK] = dk.astype(BF16)
    dp_ref[:, 2 * BLOCK : 3 * BLOCK] = dv.astype(BF16)
    dp_ref[:, 3 * BLOCK : CORE] = dog.astype(BF16)
    dp_ref[:, CORE:WIDE] = drate.astype(BF16)

    @pl.when(bucket == 0)
    def _():
        sums_ref[...] = jnp.zeros_like(sums_ref)

    sums_ref[0:1, 0:BLOCK] += jnp.sum(dqb * f["qn"], axis=0, keepdims=True)
    sums_ref[1:2, 0:BLOCK] += jnp.sum(dkb * f["kn"], axis=0, keepdims=True)
    sums_ref[2:3, 0:EXTRA] += jnp.sum(drate, axis=0, keepdims=True)


SMEM = pl.BlockSpec(memory_space=pltpu.SMEM)


def rows_spec(rows, width):
    return pl.BlockSpec((rows, width), lambda i: (i, 0))


def whole_spec(shape):
    return pl.BlockSpec(shape, lambda i: (0,) * len(shape))


def attn_fwd(lens, proj, bias, gains):
    buckets = lens.shape[0]
    rows = proj.shape[0] // buckets
    total = proj.shape[0]
    return pl.pallas_call(
        attn_fwd_kernel,
        grid=(buckets,),
        in_specs=[SMEM, rows_spec(rows, WIDE), whole_spec(bias.shape), whole_spec(gains.shape)],
        out_specs=[rows_spec(rows, BLOCK), rows_spec(rows, BLOCK), rows_spec(rows, EXTRA)],
        out_shape=[
            jax.ShapeDtypeStruct((total, BLOCK), BF16),
            jax.ShapeDtypeStruct((total, BLOCK), F32),
            jax.ShapeDtypeStruct((total, EXTRA), F32),
        ],
        compiler_params=pltpu.CompilerParams(vmem_limit_bytes=40 * 2**20),
        name="attn_fwd",
    )(lens, proj, bias, gains)


def attn_bwd(lens, proj, bias, gains, att, lse, grad, weight):
    buckets = lens.shape[0]
    rows = proj.shape[0] // buckets
    total = proj.shape[0]
    return pl.pallas_call(
        attn_bwd_kernel,
        grid=(buckets,),
        in_specs=[
            SMEM,
            rows_spec(rows, WIDE),
            whole_spec(bias.shape),
            whole_spec(gains.shape),
            rows_spec(rows, BLOCK),
            rows_spec(rows, EXTRA),
            rows_spec(rows, grad.shape[1]),
            whole_spec(weight.shape),
        ],
        out_specs=[rows_spec(rows, WIDE), whole_spec((8, 2 * EXTRA))],
        out_shape=[
            jax.ShapeDtypeStruct((total, WIDE), BF16),
            jax.ShapeDtypeStruct((8, 2 * EXTRA), F32),
        ],
        compiler_params=pltpu.CompilerParams(vmem_limit_bytes=40 * 2**20),
        name="attn_bwd",
    )(lens, proj, bias, gains, att, lse, grad, weight)


def body(
    tokens,
    doc_lengths,
    norm_gain,
    w_attn_in,
    w_rates,
    rate_bias,
    q_gain,
    k_gain,
    w_out,
    ffn_gain,
    w_gate_up,
    w_down,
    cotangent,
):
    place = lax.axis_index("tp")
    share = lax.axis_size("sh")
    tok_rows, width = tokens.shape
    own_rows = w_attn_in.shape[0]
    ff_own = w_gate_up.shape[1] // (2 * TP)
    offsets = jnp.array(OFFSETS, jnp.int32)

    gains = jnp.stack([norm_gain, q_gain, k_gain, ffn_gain], axis=1)
    lens_pad = jnp.zeros((own_rows, doc_lengths.shape[0]), BF16).at[0].set(doc_lengths.astype(BF16))
    beside = jnp.concatenate([gains, lens_pad], axis=1)
    beside = jnp.broadcast_to(beside[None], (TP,) + beside.shape)
    pad = EXTRA - RATES - beside.shape[2]
    out_in = jnp.concatenate(
        [
            columns_out(w_attn_in, 4),
            columns_out(w_rates, 3),
            beside,
            jnp.zeros((TP, own_rows, pad), BF16),
        ],
        axis=2,
    )
    got_in = lax.all_to_all(out_in, "tp", 0, 0, tiled=True)
    w_in = lax.all_gather(got_in, "sh", axis=1).reshape(width, WIDE)
    w_mix = lax.all_gather(w_out, "sh", axis=0, tiled=True)
    got_gu = lax.all_to_all(columns_out(w_gate_up, 2), "tp", 0, 0, tiled=True)
    w_gu = lax.all_gather(got_gu, "sh", axis=1).reshape(width, 2 * ff_own)
    w_dn = lax.all_gather(w_down, "sh", axis=0, tiled=True)

    lens_all = got_in[:, 0, CORE + LENS_AT : CORE + LENS_AT + doc_lengths.shape[0]].astype(jnp.int32)
    lens = lens_all[place ^ offsets]
    gains_all = w_in[:, CORE + GAIN_AT : CORE + GAIN_AT + 4].astype(F32).T
    gain_one = gains_all[0:1]
    gain_two = gains_all[3:4]
    gain_heads = lax.dynamic_slice(gains_all[1:3], (0, place * BLOCK), (2, BLOCK))
    gain_heads = jnp.pad(gain_heads, ((0, 6), (0, 2 * EXTRA - BLOCK)))
    bias = lax.dynamic_index_in_dim(rate_bias.reshape(3, TP, OWN), place, 1, False).reshape(1, RATES)
    bias = jnp.pad(bias, ((0, 7), (0, EXTRA - RATES)))

    tok_all = gather_rows(tokens)
    cot_all = gather_rows(cotangent)
    n1_all, _ = normed(tok_all.astype(F32))
    h1_all = (n1_all * gain_one).astype(BF16)
    proj = dot(h1_all, w_in)
    mixed, att, lse = attn_fwd(lens, proj, bias, gain_heads)
    x2 = tokens.astype(F32) + scatter_rows(dot(mixed, w_mix).astype(BF16))
    n2, r2 = normed(x2)
    h2_all = gather_rows((n2 * gain_two).astype(BF16))

    ends = jnp.sum(lens, axis=1)
    live = (jnp.arange(tok_rows)[None, :] < ends[:, None]).astype(F32).reshape(-1, 1)
    gu = dot(h2_all, w_gu)
    gate, up = gu[:, :ff_own], gu[:, ff_own:]
    sg = jax.nn.sigmoid(gate)
    ab = (gate * sg * up * live).astype(BF16)
    da = dot(cot_all, w_dn, ((1,), (1,))) * live
    dgu = jnp.concatenate([da * up * sg * (1.0 + gate * (1.0 - sg)), da * gate * sg], axis=1).astype(BF16)
    dh2 = scatter_rows(dot(dgu, w_gu, ((1,), (1,))).astype(BF16))
    layer_out = (x2 + scatter_rows(dot(ab, w_dn).astype(BF16))).astype(BF16)
    dw_dn = dot(ab, cot_all, ((0,), (0,))).astype(BF16)
    dw_gu = dot(h2_all, dgu, ((0,), (0,))).astype(BF16)
    d_w_down = lax.psum_scatter(dw_dn, "sh", scatter_dimension=0, tiled=True).astype(F32)
    dw_gu = own_share(dw_gu, share)
    d_w_gate_up = columns_in(lax.all_to_all(dw_gu, "tp", 0, 0, tiled=True), 2).astype(F32)

    dx2 = cotangent.astype(F32) + norm_back(n2, r2, dh2 * gain_two)
    dxb_all = gather_rows(dx2.astype(BF16))
    dw_mix = dot(mixed, dxb_all, ((0,), (0,))).astype(BF16)
    d_w_out = lax.psum_scatter(dw_mix, "sh", scatter_dimension=0, tiled=True).astype(F32)
    dp, sums = attn_bwd(lens, proj, bias, gain_heads, att, lse, dxb_all, w_mix)
    dw_in = dot(h1_all, dp, ((0,), (0,))).astype(BF16)

    at_row = jnp.arange(width)
    in_own = (at_row // BLOCK == place)[:, None]
    qk_sums = jnp.tile(sums[0:2, 0:BLOCK].T, (TP, 1))
    qk_sums = jnp.where(in_own, qk_sums, 0.0)
    bias_sums = jnp.pad(sums[2, 0:RATES], (0, own_rows - RATES))
    bias_sums = jnp.tile(bias_sums[:, None], (width // own_rows, 1))
    beside = jnp.concatenate([qk_sums, bias_sums], axis=1).astype(BF16)
    dw_in = jnp.concatenate(
        [dw_in[:, : CORE + RATES], beside, jnp.zeros((width, EXTRA - RATES - 3), BF16)], axis=1
    )
    dw_in = own_share(dw_in, share)
    dw_in = lax.all_to_all(dw_in, "tp", 0, 0, tiled=True)
    d_w_attn_in = columns_in(dw_in[:, :, :CORE], 4).astype(F32)
    d_w_rates = columns_in(dw_in[:, :, CORE : CORE + RATES], 3).astype(F32)
    small = dw_in[:, :, CORE + RATES : CORE + RATES + 3].astype(F32)
    d_q_gain = jnp.sum(small[:, :, 0], axis=0)
    d_k_gain = jnp.sum(small[:, :, 1], axis=0)
    d_rate_bias = small[:, :RATES, 2].reshape(TP, 3, OWN).transpose(1, 0, 2).reshape(-1)

    dh1 = scatter_rows(dot(dp, w_in, ((1,), (1,))).astype(BF16))
    n1, r1 = normed(tokens.astype(F32))
    d_tokens = dx2 + norm_back(n1, r1, dh1 * gain_one)

    d_norm_gain = (
        jnp.sum(w_attn_in.astype(F32) * d_w_attn_in, axis=1)
        + jnp.sum(w_rates.astype(F32) * d_w_rates, axis=1)
    ) / norm_gain.astype(F32)
    d_ffn_gain = jnp.sum(w_gate_up.astype(F32) * d_w_gate_up, axis=1) / ffn_gain.astype(F32)
    return (
        layer_out,
        d_tokens,
        d_norm_gain,
        d_w_attn_in,
        d_w_rates,
        d_rate_bias,
        d_q_gain,
        d_k_gain,
        d_w_out,
        d_ffn_gain,
        d_w_gate_up,
        d_w_down,
    )


def solution(mesh):
    devices = mesh.devices.reshape(TP, -1)
    grid = Mesh(devices, ("tp", "sh"))
    rows = P(("tp", "sh"), None)
    flat = P(("tp", "sh"))
    in_specs = (rows, flat, flat, rows, rows, P(), flat, flat, rows, flat, rows, rows, rows)
    out_specs = (rows, rows, flat, rows, rows, P(), flat, flat, rows, flat, rows, rows)
    return jax.shard_map(body, mesh=grid, in_specs=in_specs, out_specs=out_specs, check_vma=False)
```

```python
import jax
import jax.numpy as jnp
import numpy as np
from jax import lax
from jax.experimental import pallas as pl
from jax.experimental.pallas import tpu as pltpu
from jax.sharding import Mesh
from jax.sharding import PartitionSpec as P

HEADS = 24
HEAD_DIM = 64
EPS = 1e-06
NEG = -1e30
TP = 8
OWN = HEADS // TP
BLOCK = OWN * HEAD_DIM
CORE = 4 * BLOCK
EXTRA = 128
WIDE = CORE + EXTRA
RATES = 3 * OWN
GAIN_AT = RATES
LENS_AT = RATES + 4
OFFSETS = (0, 2, 4, 6, 1, 3, 5, 7)
F32 = jnp.float32
BF16 = jnp.bfloat16


def flip(array, offset):
    return lax.ppermute(array, "tp", [(i, i ^ offset) for i in range(TP)])


def sides(own):
    return flip(own, 2), flip(own, 4)


def diagonal(two, four):
    cut = two.shape[0] // 2
    return flip(two[:cut], 4), flip(four[cut:], 2)


def others(own):
    return [flip(own, d) for d in (2, 4, 6)]


def both_cores(near, far_flipped):
    rows = near.shape[0] // 4
    sums = [near[i * rows : (i + 1) * rows].astype(F32) + far_flipped[i * rows : (i + 1) * rows].astype(F32) for i in range(4)]
    return sums[0], [x.astype(BF16) for x in sums[1:]]


def send(blocks):
    return [flip(x, d) for x, d in zip(blocks, (2, 4, 6))]


def relay_six(blocks):
    two, four, six = blocks
    cut = six.shape[0] // 2
    return two, four, flip(six[:cut], 2), flip(six[cut:], 4)


def add_six(blocks):
    two, four, over_two, over_four = blocks
    cut = over_two.shape[0]
    two = jnp.concatenate([two[:cut], (two[cut:].astype(F32) + over_four.astype(F32)).astype(BF16)], axis=0)
    four = jnp.concatenate([(four[:cut].astype(F32) + over_two.astype(F32)).astype(BF16), four[cut:]], axis=0)
    return two, four


def gather_shares(own):
    share = lax.axis_size("sh")
    return [own] + [lax.ppermute(own, "sh", [(i, (i + k) % share) for i in range(share)]) for k in range(1, share)]


def in_order(pieces):
    here = lax.axis_index("sh")
    share = len(pieces)
    out = jnp.zeros((share,) + pieces[0].shape, pieces[0].dtype)
    for k, piece in enumerate(pieces):
        out = lax.dynamic_update_index_in_dim(out, piece, (here - k) % share, 0)
    return out.reshape((-1,) + pieces[0].shape[1:])


def to_shares(part):
    share = lax.axis_size("sh")
    here = lax.axis_index("sh")
    blocks = part.reshape(share, -1, part.shape[1])
    picked = [lax.dynamic_index_in_dim(blocks, (here + k) % share, 0, False) for k in range(share)]
    return picked[:1] + [
        lax.ppermute(picked[k], "sh", [(i, (i + k) % share) for i in range(share)]) for k in range(1, share)
    ]


def total_of(parts):
    return sum(term.astype(F32) for term in parts)


def phase(*values):
    return lax.optimization_barrier(values)


def normed(field_in):
    factor = lax.rsqrt(jnp.mean(field_in * field_in, axis=-1, keepdims=True) + EPS)
    return field_in * factor, factor


def norm_back(normal, factor, grad_in):
    return factor * (grad_in - normal * jnp.mean(grad_in * normal, axis=-1, keepdims=True))


def dot(a, b, dims=((1,), (0,)), precision=None):
    return lax.dot_general(a, b, (dims, ((), ())), precision=precision, preferred_element_type=F32)


def iota(shape, dim):
    return lax.broadcasted_iota(jnp.int32, shape, dim)


def settings(us, mib):
    cost = pl.CostEstimate(flops=int(us * 1e7), bytes_accessed=int(us * 1e4), transcendentals=0)
    return dict(compiler_params=pltpu.CompilerParams(vmem_limit_bytes=mib * 2**20), cost_estimate=cost)


SMEM = pl.BlockSpec(memory_space=pltpu.SMEM)
VMEM = pl.BlockSpec(memory_space=pltpu.VMEM)


def shape(dims, dtype):
    return jax.ShapeDtypeStruct(dims, dtype)


def rate_picks(t, rows, columns, flipped=False):
    whole, own = iota((rows, columns), 1 if flipped else 0), iota((rows, columns), 0 if flipped else 1)
    kind, head = own // OWN, own % OWN
    return ((own < RATES) & (whole == kind * HEADS + t * OWN + head)).astype(BF16)


def pack_in_kernel(lens_ref, w_ref, rates_ref, gains_ref, out_ref):
    rows, width = w_ref.shape[0], w_ref.shape[1] // 4
    picks = (iota((4, EXTRA), 1) == GAIN_AT + iota((4, EXTRA), 0)).astype(BF16)
    beside = dot(gains_ref[...], picks, ((0,), (0,)))
    lane, row = iota((rows, EXTRA), 1), iota((rows, EXTRA), 0)
    for j in range(lens_ref.shape[0]):
        beside = jnp.where((lane == LENS_AT + j) & (row == 0), lens_ref[j].astype(F32), beside)
    for t in range(TP):
        for b in range(4):
            at = b * width + t * BLOCK
            out_ref[t, :, b * BLOCK : (b + 1) * BLOCK] = w_ref[:, at : at + BLOCK]
        rates = dot(rates_ref[...], rate_picks(t, rates_ref.shape[1], EXTRA))
        out_ref[t, :, CORE:WIDE] = (rates + beside).astype(BF16)


def pack_in(lens, w, rates, gains):
    return pl.pallas_call(
        pack_in_kernel,
        in_specs=[SMEM, VMEM, VMEM, VMEM],
        out_specs=VMEM,
        out_shape=shape((TP, w.shape[0], WIDE), BF16),
        **settings(3, 16),
        name="pack_in",
    )(lens, w, rates, gains)


def pack_gu_kernel(w_ref, out_ref):
    ff = w_ref.shape[1] // 2
    own = ff // TP
    for t in range(TP):
        out_ref[t, :, :own] = w_ref[:, t * own : (t + 1) * own]
        out_ref[t, :, own:] = w_ref[:, ff + t * own : ff + (t + 1) * own]


def pack_gu(w):
    return pl.pallas_call(
        pack_gu_kernel,
        in_specs=[VMEM],
        out_specs=VMEM,
        out_shape=shape((TP, w.shape[0], w.shape[1] // TP), BF16),
        **settings(2, 16),
        name="pack_gu",
    )(w)


def join_ffn(got, down):
    columns = got.shape[2]
    top, rows = got.shape[0] * got.shape[1], down.shape[0]
    half = rows // 2

    def kernel(got_ref, down_ref, out_ref):
        for t in range(TP):
            out_ref[t * got.shape[1] : (t + 1) * got.shape[1], :] = got_ref[t]
        out_ref[top : top + rows, :] = down_ref[:, :columns]
        out_ref[top + rows :, : columns // 2] = down_ref[:half, columns:]
        out_ref[top + rows :, columns // 2 :] = down_ref[half:, columns:]

    return pl.pallas_call(
        kernel,
        in_specs=[VMEM, VMEM],
        out_specs=VMEM,
        out_shape=shape((top + rows + half, columns), BF16),
        **settings(2, 16),
        name="join_ffn",
    )(got, down)


def open_ffn(joined, down_rows, width):
    share, _, columns = joined.shape
    own_rows = width // (TP * share)
    top = TP * own_rows
    half = down_rows // 2

    def kernel(in_ref, gu_ref, down_ref):
        for z in range(share):
            for t in range(TP):
                at = (t * share + z) * own_rows
                gu_ref[at : at + own_rows, :] = in_ref[z, t * own_rows : (t + 1) * own_rows, :]
            at = z * down_rows
            down_ref[at : at + down_rows, :columns] = in_ref[z, top : top + down_rows, :]
            down_ref[at : at + half, columns:] = in_ref[z, top + down_rows :, : columns // 2]
            down_ref[at + half : at + down_rows, columns:] = in_ref[z, top + down_rows :, columns // 2 :]

    return pl.pallas_call(
        kernel,
        in_specs=[VMEM],
        out_specs=[VMEM, VMEM],
        out_shape=[shape((width, columns), BF16), shape((share * down_rows, width), BF16)],
        **settings(4, 16),
        name="open_ffn",
    )(joined)


def join_rows(*pieces):
    pieces = [x if isinstance(x, tuple) else (x, 0) for x in pieces]
    total = sum(x.shape[0] - first for x, first in pieces)

    def kernel(*refs):
        at = 0
        for ref, (x, first) in zip(refs, pieces):
            more = x.shape[0] - first
            refs[-1][at : at + more, :] = ref[first:, :]
            at += more

    return pl.pallas_call(
        kernel,
        in_specs=[VMEM] * len(pieces),
        out_specs=VMEM,
        out_shape=shape((total, pieces[0][0].shape[1]), pieces[0][0].dtype),
        **settings(2, 24),
        name="join_rows",
    )(*[x for x, _ in pieces])


def unpack_in_kernel(got_ref, w_ref, rates_ref, gain_ref, dw_ref, drates_ref, small_ref):
    rows, width = w_ref.shape[0], w_ref.shape[1] // 4
    along = jnp.zeros((rows, 1), F32)
    drates = jnp.zeros((rows, EXTRA), F32)
    sums = jnp.zeros((rows, EXTRA), F32)
    bias = jnp.zeros((rows, EXTRA), F32)
    lane, row = iota((rows, EXTRA), 1), iota((rows, EXTRA), 0)
    for t in range(TP):
        for b in range(4):
            at = b * width + t * BLOCK
            piece = got_ref[t, :, b * BLOCK : (b + 1) * BLOCK].astype(F32)
            dw_ref[:, at : at + BLOCK] = piece
            along = along + jnp.sum(piece * w_ref[:, at : at + BLOCK].astype(F32), axis=1, keepdims=True)
        extra = got_ref[t, :, CORE:WIDE]
        drates = drates + dot(extra, rate_picks(t, EXTRA, EXTRA, True))
        extra = extra.astype(F32)
        sums = sums + extra
        spot = (row // OWN) * HEADS + t * OWN + row % OWN
        bias = bias + jnp.where((lane == spot) & (row < RATES), extra[:, RATES + 2 : RATES + 3], 0.0)
    columns = rates_ref.shape[1]
    drates_ref[...] = drates[:, :columns]
    along = along + jnp.sum(drates[:, :columns] * rates_ref[...].astype(F32), axis=1, keepdims=True)
    turned = jnp.where(lane == 0, along, 0.0) + jnp.where(lane == 1, sums[:, RATES : RATES + 1], 0.0)
    turned = turned + jnp.where(lane == 2, sums[:, RATES + 1 : RATES + 2], 0.0)
    pick = (iota((rows, EXTRA), 0) == iota((rows, EXTRA), 1)).astype(F32)
    turned = dot(turned, pick, ((0,), (0,)), lax.Precision.HIGHEST)
    small_ref[0:1, :] = turned[0:1, :] / gain_ref[...]
    small_ref[1:3, :] = turned[1:3, :]
    small_ref[3:4, :] = jnp.sum(bias, axis=0, keepdims=True)
    small_ref[4:8, :] = jnp.zeros((4, EXTRA), F32)


def unpack_in(got, w, rates, gain):
    rows = w.shape[0]
    gain = jnp.pad(gain.astype(F32)[None], ((0, 0), (0, EXTRA - rows)), constant_values=1.0)
    return pl.pallas_call(
        unpack_in_kernel,
        in_specs=[VMEM] * 4,
        out_specs=[VMEM] * 3,
        out_shape=[shape(w.shape, F32), shape(rates.shape, F32), shape((8, EXTRA), F32)],
        **settings(5, 16),
        name="unpack_in",
    )(got, w, rates, gain)


def unpack_gu_kernel(got_ref, w_ref, gain_ref, dw_ref, small_ref):
    rows, ff = w_ref.shape[0], w_ref.shape[1] // 2
    own = ff // TP
    along = jnp.zeros((rows, 1), F32)
    for t in range(TP):
        for half in range(2):
            at = half * ff + t * own
            piece = got_ref[t, :, half * own : (half + 1) * own].astype(F32)
            dw_ref[:, at : at + own] = piece
            along = along + jnp.sum(piece * w_ref[:, at : at + own].astype(F32), axis=1, keepdims=True)
    lane = iota((rows, EXTRA), 1)
    pick = (iota((rows, EXTRA), 0) == lane).astype(F32)
    turned = dot(jnp.where(lane == 0, along, 0.0), pick, ((0,), (0,)), lax.Precision.HIGHEST)
    small_ref[...] = turned[0:8, :] / gain_ref[...]


def unpack_gu(got, w, gain):
    rows = w.shape[0]
    gain = jnp.pad(gain.astype(F32)[None], ((0, 0), (0, EXTRA - rows)), constant_values=1.0)
    return pl.pallas_call(
        unpack_gu_kernel,
        in_specs=[VMEM] * 3,
        out_specs=[VMEM] * 2,
        out_shape=[shape(w.shape, F32), shape((8, EXTRA), F32)],
        **settings(3, 16),
        name="unpack_gu",
    )(got, w, gain)


def fold(block):
    cut = block.shape[0] // 2
    tail = jnp.concatenate([block[:cut, EXTRA:], block[cut:, EXTRA:]], axis=1)
    return jnp.concatenate([block[:, :EXTRA], tail], axis=0)


def unfold(block):
    rows = 2 * block.shape[0] // 3
    tail = block[rows:]
    tail = jnp.concatenate([tail[:, : BLOCK - EXTRA], tail[:, BLOCK - EXTRA :]], axis=0)
    return jnp.concatenate([block[:rows], tail], axis=1)


def split(field_in, count):
    terms = []
    for _ in range(count):
        terms.append(field_in.astype(BF16))
        field_in = field_in - terms[-1].astype(F32)
    return terms


def dot_split(field_in, picks, count):
    return sum(dot(term, picks) for term in split(field_in, count))


TAIL = 64
SPAN = BLOCK + TAIL
TERMS = 3


def tail_lane(h, term):
    return 8 * h + term


def constants():
    head = np.arange(BLOCK) // HEAD_DIM
    same = head[:, None] == head[None, :]
    extra = np.arange(EXTRA)
    key_lanes = extra[:, None] == OWN + head[None, :]
    value_lanes = extra[:, None] == 2 * OWN + head[None, :]
    to_query = np.zeros((TERMS, EXTRA, TAIL))
    to_key = np.zeros((TERMS, EXTRA, TAIL))
    from_tail = np.zeros((TAIL, EXTRA))
    for h in range(OWN):
        for term in range(TERMS):
            to_query[term, h, tail_lane(h, term)] = 1
            to_key[term, h, tail_lane(h, TERMS + term)] = -1
        from_tail[tail_lane(h, TERMS), h] = 1
    wide = np.concatenate([same, key_lanes, value_lanes], axis=0)
    tails = np.concatenate([to_query.reshape(-1, TAIL), to_key.reshape(-1, TAIL)], axis=0)
    backs = np.concatenate([key_lanes.T, value_lanes.T, from_tail], axis=0)
    return tuple(jnp.asarray(x, BF16) for x in (wide, tails, backs))


def places_of(lens_ref, bucket, rows):
    ends = []
    total = jnp.int32(0)
    for j in range(lens_ref.shape[1]):
        total = total + lens_ref[bucket, j]
        ends.append(total)

    def segment(place):
        seg = jnp.zeros(place.shape, jnp.int32)
        for end in ends:
            seg = seg + (end <= place).astype(jnp.int32)
        return seg

    col = iota((rows, 1), 0)
    row = iota((1, rows), 1)
    seg_col = segment(col)
    allowed = (col <= row) & (segment(row) == seg_col)
    live = (col < total).astype(F32)
    same_prev = ((col > 0) & (seg_col == segment(col - 1))).astype(F32)
    return allowed, live, same_prev


def front(lens_ref, proj, bias_ref, gains_ref, wide_ref, tails_ref, bucket):
    rows = proj.shape[0]
    allowed, live, same_prev = places_of(lens_ref, bucket, rows)
    q = proj[:, 0:BLOCK]
    k = proj[:, BLOCK : 2 * BLOCK]
    v = proj[:, 2 * BLOCK : 3 * BLOCK]
    og = proj[:, 3 * BLOCK : CORE]
    rate = proj[:, CORE:WIDE] + bias_ref[0:1, :]
    sig = jax.nn.sigmoid(rate)
    log_keep = jnp.minimum(rate, 0.0) - jnp.log1p(jnp.exp(-jnp.abs(rate)))
    upto = (iota((rows, rows), 1) <= iota((rows, rows), 0)).astype(BF16)
    decay = sum(dot(upto, term) for term in split(log_keep, TERMS))
    same_head = wide_ref[0:BLOCK]
    ak = dot_split(sig, wide_ref[BLOCK : BLOCK + EXTRA], 2)
    av = dot_split(sig, wide_ref[BLOCK + EXTRA :], 2)
    k_prev = pltpu.roll(k, 1, 0) * same_prev
    v_prev = pltpu.roll(v, 1, 0) * same_prev
    ks = ak * k_prev + (1.0 - ak) * k
    vs = av * v_prev + (1.0 - av) * v

    def head_norm(u):
        factor = lax.rsqrt(dot_split(u * u, same_head, 2) * (1.0 / HEAD_DIM) + EPS)
        return u * factor, factor

    qn, rq = head_norm(q)
    kn, rk = head_norm(ks)
    q_gain, k_gain = gains_ref[0:1, 0:BLOCK], gains_ref[1:2, 0:BLOCK]
    qb = (qn * q_gain).astype(BF16) * jnp.asarray(HEAD_DIM**-0.5, BF16)
    kb = (kn * k_gain).astype(BF16)

    terms = split(decay, TERMS)
    lane = iota((1, TAIL), 1)
    ones_q = ((lane % 8 >= TERMS) & (lane % 8 < 2 * TERMS)).astype(F32)
    ones_k = (lane % 8 < TERMS).astype(F32)
    q_tail = ones_q + sum(dot(terms[t], tails_ref[t * EXTRA : (t + 1) * EXTRA]) for t in range(TERMS))
    k_tail = ones_k + sum(
        dot(terms[t], tails_ref[(TERMS + t) * EXTRA : (TERMS + t + 1) * EXTRA]) for t in range(TERMS)
    )
    qx = jnp.concatenate([qb, q_tail.astype(BF16)], axis=1)
    kx = jnp.concatenate([kb, k_tail.astype(BF16)], axis=1)
    span = iota((rows, SPAN), 1)
    masks = []
    for h in range(OWN):
        feature = (span >= h * HEAD_DIM) & (span < (h + 1) * HEAD_DIM)
        masks.append(feature | ((span >= BLOCK + 8 * h) & (span < BLOCK + 8 * (h + 1))))
    return dict(
        rows=rows, allowed=allowed, live=live, same_prev=same_prev, k=k, v=v, og=og, sig=sig, masks=masks,
        same_head=same_head, ak=ak, av=av, k_prev=k_prev, v_prev=v_prev, qn=qn, rq=rq, kn=kn, rk=rk,
        q_gain=q_gain, k_gain=k_gain, qx=qx, kx=kx, ks_low=kb, vs=vs,
    )


def scores_of(f, h):
    qh = jnp.where(f["masks"][h], f["qx"], jnp.zeros_like(f["qx"]))
    return jnp.where(f["allowed"], dot(f["kx"], qh, ((1,), (1,))), NEG), qh


def head_rows(h):
    return slice(h * HEAD_DIM, (h + 1) * HEAD_DIM)


def attn_fwd_kernel(
    lens_ref, spots_ref, near_ref, far_ref, w_ref, bias_ref, wide_ref, tails_ref,
    h1_ref, proj_ref, mixed_ref, att_ref, lse_ref, gains_ref, heads_ref,
):
    picks = (iota((8, EXTRA), 1) == GAIN_AT + iota((8, EXTRA), 0)) & (iota((8, EXTRA), 0) < 4)
    picks = picks.astype(BF16)
    gains = dot(picks, w_ref[:, CORE:WIDE], ((1,), (1,)))
    gains_ref[...] = gains
    at = pl.multiple_of(spots_ref[0] * BLOCK, BLOCK)
    heads = dot(picks, w_ref[pl.ds(at, BLOCK), CORE:WIDE], ((1,), (1,)))
    heads_ref[0:1, 0:BLOCK] = heads[1:2]
    heads_ref[1:2, 0:BLOCK] = heads[2:3]
    tok = jnp.where(pl.program_id(0) < 4, near_ref[...], far_ref[...]).astype(F32)
    h1 = (normed(tok)[0] * gains[0:1]).astype(BF16)
    h1_ref[...] = h1
    proj_ref[...] = dot(h1, w_ref[...])
    f = front(lens_ref, proj_ref, bias_ref, heads_ref, wide_ref, tails_ref, pl.program_id(0))
    vt = f["vs"].T.astype(BF16)
    att = []
    for h in range(OWN):
        s, _ = scores_of(f, h)
        top = jnp.max(s, axis=0, keepdims=True)
        e = jnp.exp(s - top)
        total = jnp.sum(e, axis=0, keepdims=True)
        prob = (e * (1.0 / total)).astype(BF16)
        att.append(dot(vt[head_rows(h)], prob))
        lse_ref[h : h + 1, :] = top + jnp.log(total)
    att = jnp.concatenate(att, axis=0).T
    att_ref[...] = att
    mixed_ref[0] = fold(att * jax.nn.sigmoid(f["og"]) * f["live"]).astype(BF16)


def attn_bwd_kernel(
    lens_ref, spots_ref, proj_ref, bias_ref, gains_ref, wide_ref, tails_ref, backs_ref, w_ref,
    att_ref, lse_ref, dm_ref, dp_ref, sums_ref, near_ref, far_ref,
):
    bucket = pl.program_id(0)
    f = front(lens_ref, proj_ref, bias_ref, gains_ref, wide_ref, tails_ref, bucket)
    rows, same_head = f["rows"], f["same_head"]
    dm = unfold(dm_ref[0].astype(F32)) * f["live"]
    g = jax.nn.sigmoid(f["og"])
    dab = (dm * g).astype(BF16)
    dog = dm * att_ref[...] * g * (1.0 - g)
    vb = f["vs"].astype(BF16)
    kt = f["kx"][:, :BLOCK].astype(F32).T.astype(BF16)
    zero = jnp.zeros((rows, BLOCK), BF16)
    dkx = jnp.zeros((rows, SPAN), F32)
    dvb = jnp.zeros((rows, BLOCK), F32)
    tail = jnp.zeros((TAIL, rows), F32)
    dqt = []
    for h in range(OWN):
        s, qh = scores_of(f, h)
        p = jnp.exp(s - lse_ref[h : h + 1, :])
        dab_h = jnp.where(f["masks"][h][:, :BLOCK], dab, zero)
        dvb = dvb + dot(p.astype(BF16), dab_h)
        dp = dot(vb, dab_h, ((1,), (1,)))
        ds = p * (dp - jnp.sum(p * dp, axis=0, keepdims=True))
        dsb = ds.astype(BF16)
        dqt.append(dot(kt[head_rows(h)], dsb))
        dkx = dkx + dot(dsb, qh)
        along = jnp.sum(dsb.astype(F32), axis=0, keepdims=True)
        tail = jnp.where(iota((TAIL, rows), 0) == tail_lane(h, TERMS), along, tail)
    dqx = jnp.concatenate(dqt + [tail], axis=0).T
    dqb = dqx[:, :BLOCK] * HEAD_DIM**-0.5
    dkb = dkx[:, :BLOCK]

    def back(n, r, e):
        return r * (e - n * (dot_split(e * n, same_head, 2) * (1.0 / HEAD_DIM)))

    dq = back(f["qn"], f["rq"], dqb * f["q_gain"])
    dks = back(f["kn"], f["rk"], dkb * f["k_gain"])
    last = iota((rows, 1), 0) == rows - 1

    def mix_back(grad, rate, cur, prev):
        ahead = pltpu.roll(rate * grad * f["same_prev"], rows - 1, 0)
        return (1.0 - rate) * grad + jnp.where(last, 0.0, ahead), grad * (prev - cur)

    dk, dak = mix_back(dks, f["ak"], f["k"], f["k_prev"])
    dv, dav = mix_back(dvb, f["av"], f["v"], f["v_prev"])

    onward = (iota((rows, rows), 1) >= iota((rows, rows), 0)).astype(BF16)
    keep = sum(dot(onward, term) for term in split(dqx[:, BLOCK:] - dkx[:, BLOCK:], TERMS))
    sig = f["sig"]
    drate = (
        dot_split(dak, backs_ref[0:BLOCK], 2)
        + dot_split(dav, backs_ref[BLOCK : 2 * BLOCK], 2)
        + dot_split(keep, backs_ref[2 * BLOCK :], 2)
    )
    lane = iota((rows, EXTRA), 1)
    drate = drate * (1.0 - sig) * jnp.where(lane < OWN, 1.0, sig)
    drate = jnp.where(lane < RATES, drate, 0.0)
    grads = jnp.concatenate([dq, dk, dv, dog, drate], axis=1).astype(BF16)
    dp_ref[...] = grads
    dh1 = dot(grads, w_ref[...], ((1,), (1,))).astype(BF16)

    @pl.when(bucket < 4)
    def _():
        near_ref[...] = dh1

    @pl.when(bucket >= 4)
    def _():
        far_ref[...] = dh1

    @pl.when(bucket == 0)
    def _():
        sums_ref[...] = jnp.zeros_like(sums_ref)

    sums_ref[0:1, 0:BLOCK] += jnp.sum(dqb * f["qn"], axis=0, keepdims=True)
    sums_ref[1:2, 0:BLOCK] += jnp.sum(dkb * f["kn"], axis=0, keepdims=True)
    sums_ref[2:3, 0:EXTRA] += jnp.sum(drate, axis=0, keepdims=True)


def rows_spec(rows, width):
    return pl.BlockSpec((rows, width), lambda i, lens, spots: (i, 0))


def whole_spec(dims):
    return pl.BlockSpec(dims, lambda i, lens, spots: (0,) * len(dims))


def spot_spec(rows):
    return pl.BlockSpec((1, rows * 3 // 2, EXTRA), lambda i, lens, spots: (spots[i], 0, 0))


def attn_fwd(lens, spots, near, far, w, bias, wide, tails):
    buckets = lens.shape[0]
    width = near.shape[1]
    total = 2 * near.shape[0]
    rows = total // buckets
    return pl.pallas_call(
        attn_fwd_kernel,
        grid_spec=pltpu.PrefetchScalarGridSpec(
            num_scalar_prefetch=2,
            grid=(buckets,),
            in_specs=[
                near_spec(rows, width),
                far_spec(rows, width),
                whole_spec(w.shape),
                whole_spec(bias.shape),
                whole_spec(wide.shape),
                whole_spec(tails.shape),
            ],
            out_specs=[
                rows_spec(rows, width),
                rows_spec(rows, WIDE),
                spot_spec(rows),
                rows_spec(rows, BLOCK),
                rows_spec(8, rows),
                whole_spec((8, width)),
                whole_spec((8, 2 * EXTRA)),
            ],
        ),
        out_shape=[
            shape((total, width), BF16),
            shape((total, WIDE), F32),
            shape((buckets, rows * 3 // 2, EXTRA), BF16),
            shape((total, BLOCK), F32),
            shape((8 * buckets, rows), F32),
            shape((8, width), F32),
            shape((8, 2 * EXTRA), F32),
        ],
        **settings(20, 60),
        name="attn_fwd",
    )(lens, spots, near, far, w, bias, wide, tails)


def near_spec(rows, width):
    return pl.BlockSpec((rows, width), lambda i, lens, spots: (jnp.minimum(i, 3), 0))


def far_spec(rows, width):
    return pl.BlockSpec((rows, width), lambda i, lens, spots: (jnp.maximum(i - 4, 0), 0))


def attn_bwd(lens, spots, proj, bias, gains, wide, tails, backs, w, att, lse, dm):
    buckets = lens.shape[0]
    total = proj.shape[0]
    width = w.shape[0]
    rows = total // buckets
    return pl.pallas_call(
        attn_bwd_kernel,
        grid_spec=pltpu.PrefetchScalarGridSpec(
            num_scalar_prefetch=2,
            grid=(buckets,),
            in_specs=[rows_spec(rows, WIDE)]
            + [whole_spec(x.shape) for x in (bias, gains, wide, tails, backs, w)]
            + [rows_spec(rows, BLOCK), rows_spec(8, rows), spot_spec(rows)],
            out_specs=[
                rows_spec(rows, WIDE),
                whole_spec((8, 2 * EXTRA)),
                near_spec(rows, width),
                far_spec(rows, width),
            ],
        ),
        out_shape=[shape((total, WIDE), BF16), shape((8, 2 * EXTRA), F32)]
        + [shape((total // 2, width), BF16)] * 2,
        **settings(24, 60),
        name="attn_bwd",
    )(lens, spots, proj, bias, gains, wide, tails, backs, w, att, lse, dm)


def mid_fwd_kernel(spots_ref, got_ref, tok_ref, gain_ref, *refs):
    x2_ref, h2_ref = refs[TP:]
    acc = tok_ref[...].astype(F32)
    for i in range(TP):
        acc = acc + dot(unfold(got_ref[spots_ref[i]]), refs[i][0:BLOCK, :])
    x2_ref[...] = acc
    h2_ref[...] = (normed(acc)[0] * gain_ref[...]).astype(BF16)


def mid_fwd(spots, got, w, tok, gain):
    return pl.pallas_call(
        mid_fwd_kernel,
        in_specs=[SMEM] + [VMEM] * (3 + TP),
        out_specs=[VMEM, VMEM],
        out_shape=[shape(tok.shape, F32), shape(tok.shape, BF16)],
        **settings(6, 40),
        name="mid_fwd",
    )(spots, got, tok, gain, *w)


def mid_bwd_kernel(
    spots_ref, a_ref, b_ref, c_ref, d_ref, x2_ref, cot_ref, gain_ref, *refs
):
    dx2_ref, dxb_ref, dm_ref = refs[TP:]
    dh2 = a_ref[...] + b_ref[...].astype(F32) + c_ref[...].astype(F32) + d_ref[...].astype(F32)
    n2, r2 = normed(x2_ref[...])
    dx2 = cot_ref[...].astype(F32) + norm_back(n2, r2, dh2 * gain_ref[...])
    dx2_ref[...] = dx2
    dxb = dx2.astype(BF16)
    dxb_ref[...] = dxb
    for i in range(TP):
        dm = dot(dxb, refs[i][0:BLOCK, :], ((1,), (1,)))
        dm_ref[spots_ref[i]] = fold(dm).astype(BF16)


def mid_bwd(spots, parts, x2, cot, gain, w):
    rows, width = x2.shape
    return pl.pallas_call(
        mid_bwd_kernel,
        in_specs=[SMEM] + [VMEM] * (7 + TP),
        out_specs=[VMEM] * 3,
        out_shape=[shape((rows, width), F32), shape((rows, width), BF16), shape((TP, rows * 3 // 2, EXTRA), BF16)],
        **settings(8, 40),
        name="mid_bwd",
    )(spots, *parts, x2, cot, gain, *w)


def grad_mix_kernel(spots_ref, got_ref, dxb_ref, near_ref, far_ref):
    for i in range(TP):
        out_ref = near_ref if i < 4 else far_ref
        piece = dot(unfold(got_ref[spots_ref[i]]), dxb_ref[...], ((0,), (0,)))
        out_ref[(i % 4) * BLOCK : (i % 4 + 1) * BLOCK, :] = piece.astype(BF16)


def grad_mix(spots, got, dxb):
    width = dxb.shape[1]
    return pl.pallas_call(
        grad_mix_kernel,
        in_specs=[SMEM, VMEM, VMEM],
        out_specs=[VMEM, VMEM],
        out_shape=[shape((4 * BLOCK, width), BF16)] * 2,
        **settings(4, 40),
        name="grad_mix",
    )(spots, got, dxb)


def ffn_kernel(lens_ref, h2_ref, cot_ref, gu_ref, dn_ref, ab_ref, dgu_ref, out_ref, dh2_ref):
    rows, ff = h2_ref.shape[0], dn_ref.shape[0]
    total = jnp.int32(0)
    for j in range(lens_ref.shape[1]):
        total = total + lens_ref[pl.program_id(0), j]
    live = (iota((rows, 1), 0) < total).astype(F32)
    gu = dot(h2_ref[...], gu_ref[...])
    da = dot(cot_ref[...], dn_ref[...], ((1,), (1,))) * live
    gate, up = gu[:, :ff], gu[:, ff:]
    sg = jax.nn.sigmoid(gate)
    act = gate * sg
    ab = (act * up * live).astype(BF16)
    dgate = (da * up * sg * (1.0 + gate * (1.0 - sg))).astype(BF16)
    dup = (da * act).astype(BF16)
    ab_ref[...] = ab
    dgu_ref[:, :ff] = dgate
    dgu_ref[:, ff:] = dup
    dh2 = dot(dgate, gu_ref[:, :ff], ((1,), (1,))) + dot(dup, gu_ref[:, ff:], ((1,), (1,)))
    dh2_ref[...] = dh2.astype(BF16)
    out_ref[...] = dot(ab, dn_ref[...]).astype(BF16)


def ffn(lens, h2, cot, gu, dn):
    buckets = lens.shape[0]
    total, width = h2.shape
    rows = total // buckets
    ff = dn.shape[0]

    def block(columns):
        return pl.BlockSpec((rows, columns), lambda i: (i, 0))

    def whole(dims):
        return pl.BlockSpec(dims, lambda i: (0, 0))

    outs = (ff, 2 * ff, width, width)
    return pl.pallas_call(
        ffn_kernel,
        grid=(buckets,),
        in_specs=[SMEM, block(width), block(width), whole(gu.shape), whole(dn.shape)],
        out_specs=[block(c) for c in outs],
        out_shape=[shape((total, c), BF16) for c in outs],
        **settings(4 * buckets, 40),
        name="ffn",
    )(lens, h2, cot, gu, dn)


def grad_down(ab, cot):
    ff, width = ab[0].shape[1], cot[0].shape[1]
    steps = 4
    columns = width // steps

    def kernel(ab0_ref, ab1_ref, cot0_ref, cot1_ref, out_ref):
        res = dot(ab0_ref[...], cot0_ref[...], ((0,), (0,))) + dot(ab1_ref[...], cot1_ref[...], ((0,), (0,)))
        out_ref[...] = res.astype(BF16)

    return pl.pallas_call(
        kernel,
        grid=(steps,),
        in_specs=[pl.BlockSpec(x.shape, lambda i: (0, 0)) for x in ab]
        + [pl.BlockSpec((x.shape[0], columns), lambda i: (0, i)) for x in cot],
        out_specs=pl.BlockSpec((ff, columns), lambda i: (0, i)),
        out_shape=shape((ff, width), BF16),
        **settings(6, 60),
        name="grad_down",
    )(*ab, *cot)


def grad_gu(h2, dgu, share):
    rows, width = h2[0].shape
    own_rows = width // (TP * share)
    columns = dgu[0].shape[1]
    steps = TP // 2

    def kernel(left0_ref, left1_ref, right0_ref, right1_ref, out_ref):
        res = dot(left0_ref[...], right0_ref[...], ((0,), (0,)))
        res = res + dot(left1_ref[...], right1_ref[...], ((0,), (0,)))
        for k in range(2):
            for z in range(share):
                at = (k * share + z) * own_rows
                out_ref[z, k] = res[at : at + own_rows].astype(BF16)

    return pl.pallas_call(
        kernel,
        grid=(steps,),
        in_specs=[pl.BlockSpec((rows, width // steps), lambda i: (0, i))] * 2
        + [pl.BlockSpec((rows, columns), lambda i: (0, 0))] * 2,
        out_specs=pl.BlockSpec((share, 2, own_rows, columns), lambda i: (0, i, 0, 0)),
        out_shape=shape((share, TP, own_rows, columns), BF16),
        **settings(11, 60),
        name="grad_gu",
    )(*h2, *dgu)


def grad_in(place, sums, left, right, share):
    own_rows = left.shape[1] // (TP * share)
    columns = right.shape[1]
    steps = TP // 2

    def kernel(place_ref, sums_ref, left_ref, right_ref, out_ref):
        res = dot(left_ref[...], right_ref[...], ((0,), (0,)))
        lane, row = iota((BLOCK, EXTRA), 1), iota((BLOCK, EXTRA), 0)
        turned = sums_ref[...].T[0:BLOCK]
        bias = jnp.where((lane == row % own_rows) & (lane < RATES), sums_ref[2:3, 0:EXTRA], 0.0)
        bias = jnp.sum(bias, axis=1, keepdims=True)
        for k in range(2):
            mine = (pl.program_id(0) * 2 + k == place_ref[0]).astype(F32)
            extra = res[k * BLOCK : (k + 1) * BLOCK, CORE:WIDE]
            extra = jnp.where(lane == RATES, turned[:, 0:1] * mine, extra)
            extra = jnp.where(lane == RATES + 1, turned[:, 1:2] * mine, extra)
            extra = jnp.where(lane == RATES + 2, bias, extra)
            for z in range(share):
                at = z * own_rows
                rest = k * BLOCK + at
                out_ref[z, k, :, :CORE] = res[rest : rest + own_rows, :CORE].astype(BF16)
                out_ref[z, k, :, CORE:] = extra[at : at + own_rows].astype(BF16)

    return pl.pallas_call(
        kernel,
        grid=(steps,),
        in_specs=[
            SMEM,
            pl.BlockSpec(sums.shape, lambda i: (0, 0)),
            pl.BlockSpec((left.shape[0], left.shape[1] // steps), lambda i: (0, i)),
            pl.BlockSpec(right.shape, lambda i: (0, 0)),
        ],
        out_specs=pl.BlockSpec((share, 2, own_rows, columns), lambda i: (0, i, 0, 0)),
        out_shape=shape((share, TP, own_rows, columns), BF16),
        **settings(11, 60),
        name="grad_in",
    )(place, sums, left, right)


def own_share(part):
    columns = part.shape[-1]
    summed = lax.psum_scatter(part.reshape(-1, columns), "sh", scatter_dimension=0, tiled=True)
    return summed.reshape(TP, -1, columns)


def swap(blocks):
    return lax.all_to_all(blocks, "tp", 0, 0, tiled=True)


def body(
    tokens,
    doc_lengths,
    norm_gain,
    w_attn_in,
    w_rates,
    rate_bias,
    q_gain,
    k_gain,
    w_out,
    ffn_gain,
    w_gate_up,
    w_down,
    cotangent,
):
    place = lax.axis_index("tp")
    share = lax.axis_size("sh")
    width = tokens.shape[1]
    own_rows = w_attn_in.shape[0]
    spots = place ^ jnp.array(OFFSETS, jnp.int32)

    gains = jnp.stack([norm_gain, q_gain, k_gain, ffn_gain])
    packed, w_mix = phase(pack_in(doc_lengths, w_attn_in, w_rates, gains), w_out)
    got_in, w_mix = phase(swap(packed), gather_shares(w_mix))
    w_in = lax.all_gather(got_in, "sh", axis=1).reshape(width, WIDE)
    lens_all = got_in[:, 0, CORE + LENS_AT : CORE + LENS_AT + doc_lengths.shape[0]].astype(jnp.int32)
    lens = lens_all[spots]
    bias = lax.dynamic_index_in_dim(rate_bias.reshape(3, TP, OWN), place, 1, False).reshape(1, RATES)
    bias = jnp.pad(bias, ((0, 7), (0, EXTRA - RATES)))

    tok, w_gu, _ = phase(tokens, w_gate_up, got_in)
    two_four = sides(tok)
    tok = join_rows(tok, *two_four, *diagonal(*two_four))
    tok, packed = phase(tok, pack_gu(w_gu))
    joined = join_ffn(swap(packed), w_down)
    far = flip(tok, 1)
    w_gu, w_dn = open_ffn(lax.all_gather(joined, "sh", axis=0), w_down.shape[0], width)

    wide, tails, backs = constants()
    beside = phase(join_rows(in_order(w_mix), cotangent), joined)[0]
    two_four = sides(beside)
    h1, proj, mixed, att, lse, gains, gain_heads = attn_fwd(lens, spots, tok, far, w_in, bias, wide, tails)
    gain_one, gain_two = gains[0:1], gains[3:4]
    mixed, two_four = phase(mixed, two_four)
    near = [beside, *two_four]
    six = diagonal(*two_four)
    got_mixed, six, far = phase(swap(mixed), six, [flip(x, 1) for x in near])
    far = [*far, *[flip(x, 1) for x in six]]
    near = [*near, *six]
    x2, h2 = mid_fwd(spots, got_mixed, near[:4] + far[:4], tokens, gain_two)

    h2, near, far = phase(h2, near, far)
    w_mix = near[:4] + far[:4]
    two_four = sides(h2)
    cot = [join_rows(*[(x, BLOCK) for x in half[:4]], half[4]) for half in (near, far)]
    two_four, cot = phase(two_four, cot)
    h2 = join_rows(h2, *two_four, *diagonal(*two_four))
    h2_far, found_near = phase(flip(h2, 1), ffn(lens[:4], h2, cot[0], w_gu, w_dn))
    h2 = h2, h2_far
    found_far = ffn(lens[4:], h2_far, cot[1], w_gu, w_dn)
    ab, dgu, out, dh2 = phase(*zip(found_near, found_far))
    dh2_far, dw_dn, out_far = phase(flip(dh2[1], 1), grad_down(ab, cot), flip(out[1], 1))
    own, low = both_cores(dh2[0], dh2_far)
    dw_dn = lax.psum_scatter(dw_dn, "sh", scatter_dimension=0, tiled=True)
    own, low, dgu, out_far = phase(own, low, dgu, out_far)
    layer_own, layer_low = both_cores(out[0], out_far)
    dh2, dw_gu, dw_dn, own, layer_low = phase(send(low), grad_gu(h2, dgu, share), dw_dn, own, layer_low)
    dw_gu = own_share(dw_gu)

    dx2, dxb, dm = mid_bwd(spots, [own] + dh2, x2, cotangent, gain_two, w_mix)
    dxb, dm = phase(dxb, dm)
    got_dm, mix, layer_low = phase(swap(dm), grad_mix(spots, got_mixed, dxb), layer_low)
    layer, mix_far, found, dw_gu = phase(
        send(layer_low),
        flip(mix[1], 1),
        attn_bwd(lens, spots, proj, bias, gain_heads, wide, tails, backs, w_in, att, lse, got_dm),
        dw_gu,
    )
    dp, sums, dh1_near, dh1_far = found
    layer_out = (x2 + total_of([layer_own] + layer)).astype(BF16)

    mix_own, low = both_cores(mix[0], mix_far)
    dh1_far, low, dw_in, got_gu = phase(
        flip(dh1_far, 1), relay_six(low), grad_in(place.reshape(1), sums, h1, dp, share), swap(dw_gu)
    )
    dw_in = own_share(dw_in)
    low = add_six(low)
    dh1_own, dh1_low = both_cores(dh1_near, dh1_far)
    low, dh1_low = phase(low, dh1_low)
    dh1, mix, dw_in = phase(send(dh1_low), (flip(low[0], 2), flip(low[1], 4)), dw_in)
    got_in_grad, mix = phase(swap(dw_in), to_shares(total_of((mix_own, *mix)).astype(BF16)))
    n1, r1 = normed(tokens.astype(F32))
    d_tokens = dx2 + norm_back(n1, r1, total_of([dh1_own] + dh1) * gain_one)

    d_w_attn_in, d_w_rates, small = unpack_in(got_in_grad, w_attn_in, w_rates, norm_gain)
    d_w_gate_up, small_gu = unpack_gu(got_gu, w_gate_up, ffn_gain)
    d_ffn_gain = small_gu[0, :own_rows]
    d_w_out = total_of(mix)
    return (
        layer_out,
        d_tokens,
        small[0, :own_rows],
        d_w_attn_in,
        d_w_rates,
        small[3, : w_rates.shape[1]],
        small[1, :own_rows],
        small[2, :own_rows],
        d_w_out,
        d_ffn_gain,
        d_w_gate_up,
        dw_dn.astype(F32),
    )


def solution(mesh):
    devices = mesh.devices.reshape(TP, -1)
    grid = Mesh(devices, ("tp", "sh"))
    rows = P(("tp", "sh"), None)
    flat = P(("tp", "sh"))
    in_specs = (rows, flat, flat, rows, rows, P(), flat, flat, rows, flat, rows, rows, rows)
    out_specs = (rows, rows, flat, rows, rows, P(), flat, flat, rows, flat, rows, rows)
    return jax.shard_map(body, mesh=grid, in_specs=in_specs, out_specs=out_specs, check_vma=False)
```

```python
import jax
import jax.numpy as jnp
import numpy as np
from jax import lax
from jax.experimental import pallas as pl
from jax.experimental.pallas import tpu as pltpu
from jax.sharding import Mesh
from jax.sharding import PartitionSpec as P

HEADS = 24
HEAD_DIM = 64
EPS = 1e-06
NEG = -1e30
TP = 8
OWN = HEADS // TP
BLOCK = OWN * HEAD_DIM
CORE = 4 * BLOCK
EXTRA = 128
WIDE = CORE + EXTRA
RATES = 3 * OWN
GAIN_AT = RATES
LENS_AT = RATES + 4
OFFSETS = (0, 2, 4, 6, 1, 3, 5, 7)
F32 = jnp.float32
BF16 = jnp.bfloat16


def flip(array, offset):
    return lax.ppermute(array, "tp", [(i, i ^ offset) for i in range(TP)])


def sides(own):
    return flip(own, 2), flip(own, 4)


def diagonal(two, four):
    cut = two.shape[0] // 2
    return flip(two[:cut], 4), flip(four[cut:], 2)


def others(own):
    return [flip(own, d) for d in (2, 4, 6)]


def both_cores(near, far):
    sums = [x.astype(F32) + y.astype(F32) for x, y in zip(near, far)]
    return sums[0], [x.astype(BF16) for x in sums[1:]]


def quarters(array):
    rows = array.shape[0] // 4
    return [array[i * rows : (i + 1) * rows] for i in range(4)]


def send(blocks):
    return [flip(x, d) for x, d in zip(blocks, (2, 4, 6))]


def relay_six(blocks):
    two, four, six = blocks
    cut = six.shape[0] // 2
    return two, four, flip(six[:cut], 2), flip(six[cut:], 4)


def add_six(blocks):
    two, four, over_two, over_four = blocks
    cut = over_two.shape[0]
    two = jnp.concatenate([two[:cut], (two[cut:].astype(F32) + over_four.astype(F32)).astype(BF16)], axis=0)
    four = jnp.concatenate([(four[:cut].astype(F32) + over_two.astype(F32)).astype(BF16), four[cut:]], axis=0)
    return two, four


def gather_shares(own):
    share = lax.axis_size("sh")
    return [own] + [lax.ppermute(own, "sh", [(i, (i + k) % share) for i in range(share)]) for k in range(1, share)]


def in_order(pieces):
    here = lax.axis_index("sh")
    share = len(pieces)
    out = jnp.zeros((share,) + pieces[0].shape, pieces[0].dtype)
    for k, piece in enumerate(pieces):
        out = lax.dynamic_update_index_in_dim(out, piece, (here - k) % share, 0)
    return out.reshape((-1,) + pieces[0].shape[1:])


def to_shares(part):
    share = lax.axis_size("sh")
    here = lax.axis_index("sh")
    blocks = part.reshape(share, -1, part.shape[1])
    picked = [lax.dynamic_index_in_dim(blocks, (here + k) % share, 0, False) for k in range(share)]
    return picked[:1] + [
        lax.ppermute(picked[k], "sh", [(i, (i + k) % share) for i in range(share)]) for k in range(1, share)
    ]


def total_of(parts):
    return sum(term.astype(F32) for term in parts)


def phase(*values):
    return lax.optimization_barrier(values)


def normed(field_in):
    factor = lax.rsqrt(jnp.mean(field_in * field_in, axis=-1, keepdims=True) + EPS)
    return field_in * factor, factor


def norm_back(normal, factor, grad_in):
    return factor * (grad_in - normal * jnp.mean(grad_in * normal, axis=-1, keepdims=True))


def dot(a, b, dims=((1,), (0,)), precision=None):
    return lax.dot_general(a, b, (dims, ((), ())), precision=precision, preferred_element_type=F32)


def iota(shape, dim):
    return lax.broadcasted_iota(jnp.int32, shape, dim)


def settings(us, mib):
    cost = pl.CostEstimate(flops=int(us * 1e7), bytes_accessed=int(us * 1e4), transcendentals=0)
    return dict(compiler_params=pltpu.CompilerParams(vmem_limit_bytes=mib * 2**20), cost_estimate=cost)


SMEM = pl.BlockSpec(memory_space=pltpu.SMEM)
VMEM = pl.BlockSpec(memory_space=pltpu.VMEM)


def shape(dims, dtype):
    return jax.ShapeDtypeStruct(dims, dtype)


def rate_picks(t, rows, columns, flipped=False):
    whole, own = iota((rows, columns), 1 if flipped else 0), iota((rows, columns), 0 if flipped else 1)
    kind, head = own // OWN, own % OWN
    return ((own < RATES) & (whole == kind * HEADS + t * OWN + head)).astype(BF16)


def pack_in_kernel(lens_ref, w_ref, rates_ref, gains_ref, out_ref):
    rows, width = w_ref.shape[0], w_ref.shape[1] // 4
    picks = (iota((4, EXTRA), 1) == GAIN_AT + iota((4, EXTRA), 0)).astype(BF16)
    beside = dot(gains_ref[...], picks, ((0,), (0,)))
    lane, row = iota((rows, EXTRA), 1), iota((rows, EXTRA), 0)
    for j in range(lens_ref.shape[0]):
        beside = jnp.where((lane == LENS_AT + j) & (row == 0), lens_ref[j].astype(F32), beside)
    for t in range(TP):
        for b in range(4):
            at = b * width + t * BLOCK
            out_ref[t, :, b * BLOCK : (b + 1) * BLOCK] = w_ref[:, at : at + BLOCK]
        rates = dot(rates_ref[...], rate_picks(t, rates_ref.shape[1], EXTRA))
        out_ref[t, :, CORE:WIDE] = (rates + beside).astype(BF16)


def pack_in(lens, w, rates, gains):
    return pl.pallas_call(
        pack_in_kernel,
        in_specs=[SMEM, VMEM, VMEM, VMEM],
        out_specs=VMEM,
        out_shape=shape((TP, w.shape[0], WIDE), BF16),
        **settings(3, 16),
        name="pack_in",
    )(lens, w, rates, gains)


def pack_gu_kernel(w_ref, out_ref):
    ff = w_ref.shape[1] // 2
    own = ff // TP
    for t in range(TP):
        out_ref[t, :, :own] = w_ref[:, t * own : (t + 1) * own]
        out_ref[t, :, own:] = w_ref[:, ff + t * own : ff + (t + 1) * own]


def pack_gu(w):
    return pl.pallas_call(
        pack_gu_kernel,
        in_specs=[VMEM],
        out_specs=VMEM,
        out_shape=shape((TP, w.shape[0], w.shape[1] // TP), BF16),
        **settings(2, 16),
        name="pack_gu",
    )(w)


def join_ffn(got, down):
    columns = got.shape[2]
    top, rows = got.shape[0] * got.shape[1], down.shape[0]
    half = rows // 2

    def kernel(got_ref, down_ref, out_ref):
        for t in range(TP):
            out_ref[t * got.shape[1] : (t + 1) * got.shape[1], :] = got_ref[t]
        out_ref[top : top + rows, :] = down_ref[:, :columns]
        out_ref[top + rows :, : columns // 2] = down_ref[:half, columns:]
        out_ref[top + rows :, columns // 2 :] = down_ref[half:, columns:]

    return pl.pallas_call(
        kernel,
        in_specs=[VMEM, VMEM],
        out_specs=VMEM,
        out_shape=shape((top + rows + half, columns), BF16),
        **settings(2, 16),
        name="join_ffn",
    )(got, down)


def open_ffn(joined, down_rows, width):
    share, _, columns = joined.shape
    own_rows = width // (TP * share)
    top = TP * own_rows
    half = down_rows // 2

    def kernel(in_ref, gu_ref, down_ref):
        for z in range(share):
            for t in range(TP):
                at = (t * share + z) * own_rows
                gu_ref[at : at + own_rows, :] = in_ref[z, t * own_rows : (t + 1) * own_rows, :]
            at = z * down_rows
            down_ref[at : at + down_rows, :columns] = in_ref[z, top : top + down_rows, :]
            down_ref[at : at + half, columns:] = in_ref[z, top + down_rows :, : columns // 2]
            down_ref[at + half : at + down_rows, columns:] = in_ref[z, top + down_rows :, columns // 2 :]

    return pl.pallas_call(
        kernel,
        in_specs=[VMEM],
        out_specs=[VMEM, VMEM],
        out_shape=[shape((width, columns), BF16), shape((share * down_rows, width), BF16)],
        **settings(4, 16),
        name="open_ffn",
    )(joined)


def join_rows(*pieces):
    pieces = [x if isinstance(x, tuple) else (x, 0) for x in pieces]
    total = sum(x.shape[0] - first for x, first in pieces)

    def kernel(*refs):
        at = 0
        for ref, (x, first) in zip(refs, pieces):
            more = x.shape[0] - first
            refs[-1][at : at + more, :] = ref[first:, :]
            at += more

    return pl.pallas_call(
        kernel,
        in_specs=[VMEM] * len(pieces),
        out_specs=VMEM,
        out_shape=shape((total, pieces[0][0].shape[1]), pieces[0][0].dtype),
        **settings(2, 24),
        name="join_rows",
    )(*[x for x, _ in pieces])


def unpack_in_kernel(got_ref, w_ref, rates_ref, gain_ref, dw_ref, drates_ref, small_ref):
    rows, width = w_ref.shape[0], w_ref.shape[1] // 4
    along = jnp.zeros((rows, 1), F32)
    drates = jnp.zeros((rows, EXTRA), F32)
    sums = jnp.zeros((rows, EXTRA), F32)
    bias = jnp.zeros((rows, EXTRA), F32)
    lane, row = iota((rows, EXTRA), 1), iota((rows, EXTRA), 0)
    for t in range(TP):
        for b in range(4):
            at = b * width + t * BLOCK
            piece = got_ref[t, :, b * BLOCK : (b + 1) * BLOCK].astype(F32)
            dw_ref[:, at : at + BLOCK] = piece
            along = along + jnp.sum(piece * w_ref[:, at : at + BLOCK].astype(F32), axis=1, keepdims=True)
        extra = got_ref[t, :, CORE:WIDE]
        drates = drates + dot(extra, rate_picks(t, EXTRA, EXTRA, True))
        extra = extra.astype(F32)
        sums = sums + extra
        spot = (row // OWN) * HEADS + t * OWN + row % OWN
        bias = bias + jnp.where((lane == spot) & (row < RATES), extra[:, RATES + 2 : RATES + 3], 0.0)
    columns = rates_ref.shape[1]
    drates_ref[...] = drates[:, :columns]
    along = along + jnp.sum(drates[:, :columns] * rates_ref[...].astype(F32), axis=1, keepdims=True)
    turned = jnp.where(lane == 0, along, 0.0) + jnp.where(lane == 1, sums[:, RATES : RATES + 1], 0.0)
    turned = turned + jnp.where(lane == 2, sums[:, RATES + 1 : RATES + 2], 0.0)
    pick = (iota((rows, EXTRA), 0) == iota((rows, EXTRA), 1)).astype(F32)
    turned = dot(turned, pick, ((0,), (0,)), lax.Precision.HIGHEST)
    small_ref[0:1, :] = turned[0:1, :] / gain_ref[...]
    small_ref[1:3, :] = turned[1:3, :]
    small_ref[3:4, :] = jnp.sum(bias, axis=0, keepdims=True)
    small_ref[4:8, :] = jnp.zeros((4, EXTRA), F32)


def unpack_in(got, w, rates, gain):
    rows = w.shape[0]
    gain = jnp.pad(gain.astype(F32)[None], ((0, 0), (0, EXTRA - rows)), constant_values=1.0)
    return pl.pallas_call(
        unpack_in_kernel,
        in_specs=[VMEM] * 4,
        out_specs=[VMEM] * 3,
        out_shape=[shape(w.shape, F32), shape(rates.shape, F32), shape((8, EXTRA), F32)],
        **settings(5, 16),
        name="unpack_in",
    )(got, w, rates, gain)


def unpack_gu_kernel(got_ref, w_ref, gain_ref, dw_ref, small_ref):
    rows, ff = w_ref.shape[0], w_ref.shape[1] // 2
    own = ff // TP
    along = jnp.zeros((rows, 1), F32)
    for t in range(TP):
        for half in range(2):
            at = half * ff + t * own
            piece = got_ref[t, :, half * own : (half + 1) * own].astype(F32)
            dw_ref[:, at : at + own] = piece
            along = along + jnp.sum(piece * w_ref[:, at : at + own].astype(F32), axis=1, keepdims=True)
    lane = iota((rows, EXTRA), 1)
    pick = (iota((rows, EXTRA), 0) == lane).astype(F32)
    turned = dot(jnp.where(lane == 0, along, 0.0), pick, ((0,), (0,)), lax.Precision.HIGHEST)
    small_ref[...] = turned[0:8, :] / gain_ref[...]


def unpack_gu(got, w, gain):
    rows = w.shape[0]
    gain = jnp.pad(gain.astype(F32)[None], ((0, 0), (0, EXTRA - rows)), constant_values=1.0)
    return pl.pallas_call(
        unpack_gu_kernel,
        in_specs=[VMEM] * 3,
        out_specs=[VMEM] * 2,
        out_shape=[shape(w.shape, F32), shape((8, EXTRA), F32)],
        **settings(3, 16),
        name="unpack_gu",
    )(got, w, gain)


def fold(block):
    cut = block.shape[0] // 2
    tail = jnp.concatenate([block[:cut, EXTRA:], block[cut:, EXTRA:]], axis=1)
    return jnp.concatenate([block[:, :EXTRA], tail], axis=0)


def unfold(block):
    rows = 2 * block.shape[0] // 3
    tail = block[rows:]
    tail = jnp.concatenate([tail[:, : BLOCK - EXTRA], tail[:, BLOCK - EXTRA :]], axis=0)
    return jnp.concatenate([block[:rows], tail], axis=1)


def split(field_in, count):
    terms = []
    for _ in range(count):
        terms.append(field_in.astype(BF16))
        field_in = field_in - terms[-1].astype(F32)
    return terms


def dot_split(field_in, picks, count):
    return sum(dot(term, picks) for term in split(field_in, count))


TAIL = 64
SPAN = BLOCK + TAIL
TERMS = 3


def tail_lane(h, term):
    return 8 * h + term


def constants():
    head = np.arange(BLOCK) // HEAD_DIM
    same = head[:, None] == head[None, :]
    extra = np.arange(EXTRA)
    key_lanes = extra[:, None] == OWN + head[None, :]
    value_lanes = extra[:, None] == 2 * OWN + head[None, :]
    to_query = np.zeros((TERMS, EXTRA, TAIL))
    to_key = np.zeros((TERMS, EXTRA, TAIL))
    from_tail = np.zeros((TAIL, EXTRA))
    for h in range(OWN):
        for term in range(TERMS):
            to_query[term, h, tail_lane(h, term)] = 1
            to_key[term, h, tail_lane(h, TERMS + term)] = -1
        from_tail[tail_lane(h, TERMS), h] = 1
    wide = np.concatenate([same, key_lanes, value_lanes], axis=0)
    tails = np.concatenate([to_query.reshape(-1, TAIL), to_key.reshape(-1, TAIL)], axis=0)
    backs = np.concatenate([key_lanes.T, value_lanes.T, from_tail], axis=0)
    return tuple(jnp.asarray(x, BF16) for x in (wide, tails, backs))


def places_of(lens_ref, bucket, rows):
    ends = []
    total = jnp.int32(0)
    for j in range(lens_ref.shape[1]):
        total = total + lens_ref[bucket, j]
        ends.append(total)

    def segment(place):
        seg = jnp.zeros(place.shape, jnp.int32)
        for end in ends:
            seg = seg + (end <= place).astype(jnp.int32)
        return seg

    col = iota((rows, 1), 0)
    row = iota((1, rows), 1)
    seg_col = segment(col)
    allowed = (col <= row) & (segment(row) == seg_col)
    live = (col < total).astype(F32)
    same_prev = ((col > 0) & (seg_col == segment(col - 1))).astype(F32)
    return allowed, live, same_prev


KEPT = ("qn", "kn", "rq", "rk", "ak", "av", "k", "v", "g")
KEPT_LOW = ("qx", "kx", "vb")


def front(proj, bias_ref, gains_ref, wide_ref, tails_ref, same_prev):
    rows = proj.shape[0]
    q = proj[:, 0:BLOCK]
    k = proj[:, BLOCK : 2 * BLOCK]
    v = proj[:, 2 * BLOCK : 3 * BLOCK]
    og = proj[:, 3 * BLOCK : CORE]
    rate = proj[:, CORE:WIDE] + bias_ref[0:1, :]
    sig = jax.nn.sigmoid(rate)
    log_keep = jnp.minimum(rate, 0.0) - jnp.log1p(jnp.exp(-jnp.abs(rate)))
    upto = (iota((rows, rows), 1) <= iota((rows, rows), 0)).astype(BF16)
    decay = sum(dot(upto, term) for term in split(log_keep, TERMS))
    same_head = wide_ref[0:BLOCK]
    ak = dot_split(sig, wide_ref[BLOCK : BLOCK + EXTRA], 2)
    av = dot_split(sig, wide_ref[BLOCK + EXTRA :], 2)
    ks = ak * shifted(k, same_prev) + (1.0 - ak) * k
    vs = av * shifted(v, same_prev) + (1.0 - av) * v

    def head_norm(u):
        factor = lax.rsqrt(dot_split(u * u, same_head, 2) * (1.0 / HEAD_DIM) + EPS)
        return u * factor, factor

    qn, rq = head_norm(q)
    kn, rk = head_norm(ks)
    q_gain, k_gain = gains_ref[0:1, 0:BLOCK], gains_ref[1:2, 0:BLOCK]
    qb = (qn * q_gain).astype(BF16) * jnp.asarray(HEAD_DIM**-0.5, BF16)
    kb = (kn * k_gain).astype(BF16)

    terms = split(decay, TERMS)
    lane = iota((1, TAIL), 1)
    ones_q = ((lane % 8 >= TERMS) & (lane % 8 < 2 * TERMS)).astype(F32)
    ones_k = (lane % 8 < TERMS).astype(F32)
    q_tail = ones_q + sum(dot(terms[t], tails_ref[t * EXTRA : (t + 1) * EXTRA]) for t in range(TERMS))
    k_tail = ones_k + sum(
        dot(terms[t], tails_ref[(TERMS + t) * EXTRA : (TERMS + t + 1) * EXTRA]) for t in range(TERMS)
    )
    qx = jnp.concatenate([qb, q_tail.astype(BF16)], axis=1)
    kx = jnp.concatenate([kb, k_tail.astype(BF16)], axis=1)
    return dict(
        qn=qn, kn=kn, rq=rq, rk=rk, ak=ak, av=av, k=k, v=v, g=jax.nn.sigmoid(og),
        qx=qx, kx=kx, vb=vs.astype(BF16), vs=vs, sig=sig,
    )


def shifted(array, same_prev):
    return pltpu.roll(array, 1, 0) * same_prev


def head_masks(rows):
    span = iota((rows, SPAN), 1)
    masks = []
    for h in range(OWN):
        feature = (span >= h * HEAD_DIM) & (span < (h + 1) * HEAD_DIM)
        masks.append(feature | ((span >= BLOCK + 8 * h) & (span < BLOCK + 8 * (h + 1))))
    return masks


def scores_of(qx, kx, mask, allowed):
    qh = jnp.where(mask, qx, jnp.zeros_like(qx))
    return jnp.where(allowed, dot(kx, qh, ((1,), (1,))), NEG), qh


def head_rows(h):
    return slice(h * HEAD_DIM, (h + 1) * HEAD_DIM)


def attn_fwd_kernel(
    lens_ref, spots_ref, near_ref, far_ref, w_ref, bias_ref, wide_ref, tails_ref,
    h1_ref, mixed_ref, att_ref, lse_ref, gains_ref, heads_ref, sig_ref, *kept_refs
):
    picks = (iota((8, EXTRA), 1) == GAIN_AT + iota((8, EXTRA), 0)) & (iota((8, EXTRA), 0) < 4)
    picks = picks.astype(BF16)
    gains = dot(picks, w_ref[:, CORE:WIDE], ((1,), (1,)))
    gains_ref[...] = gains
    at = pl.multiple_of(spots_ref[0] * BLOCK, BLOCK)
    heads = dot(picks, w_ref[pl.ds(at, BLOCK), CORE:WIDE], ((1,), (1,)))
    heads_ref[0:1, 0:BLOCK] = heads[1:2]
    heads_ref[1:2, 0:BLOCK] = heads[2:3]
    tok = jnp.where(pl.program_id(0) < 4, near_ref[...], far_ref[...]).astype(F32)
    h1 = (normed(tok)[0] * gains[0:1]).astype(BF16)
    h1_ref[...] = h1
    rows = h1.shape[0]
    allowed, live, same_prev = places_of(lens_ref, pl.program_id(0), rows)
    f = front(dot(h1, w_ref[...]), bias_ref, heads_ref, wide_ref, tails_ref, same_prev)
    sig_ref[...] = f["sig"]
    for name, ref in zip(KEPT + KEPT_LOW, kept_refs):
        ref[...] = f[name]
    vt = f["vs"].T.astype(BF16)
    att = []
    for h, mask in enumerate(head_masks(rows)):
        s, _ = scores_of(f["qx"], f["kx"], mask, allowed)
        top = jnp.max(s, axis=0, keepdims=True)
        e = jnp.exp(s - top)
        total = jnp.sum(e, axis=0, keepdims=True)
        prob = (e * (1.0 / total)).astype(BF16)
        att.append(dot(vt[head_rows(h)], prob))
        lse_ref[h : h + 1, :] = top + jnp.log(total)
    att = jnp.concatenate(att, axis=0).T
    att_ref[...] = att
    mixed_ref[0] = fold(att * f["g"] * live).astype(BF16)


def attn_bwd_kernel(
    lens_ref, spots_ref, gains_ref, wide_ref, backs_ref, w_ref, att_ref, lse_ref, dm_ref, sig_ref, *refs
):
    kept = KEPT + KEPT_LOW
    f = {name: ref[...] for name, ref in zip(kept, refs)}
    dp_ref, sums_ref, near_ref, far_ref = refs[len(kept) :]
    bucket = pl.program_id(0)
    rows = att_ref.shape[0]
    allowed, live, same_prev = places_of(lens_ref, bucket, rows)
    masks = head_masks(rows)
    same_head = wide_ref[0:BLOCK]
    q_gain, k_gain = gains_ref[0:1, 0:BLOCK], gains_ref[1:2, 0:BLOCK]
    dm = unfold(dm_ref[0].astype(F32)) * live
    g, vb = f["g"], f["vb"]
    dab = (dm * g).astype(BF16)
    dog = dm * att_ref[...] * g * (1.0 - g)
    kt = f["kx"][:, :BLOCK].astype(F32).T.astype(BF16)
    zero = jnp.zeros((rows, BLOCK), BF16)
    dkx = jnp.zeros((rows, SPAN), F32)
    dvb = jnp.zeros((rows, BLOCK), F32)
    tail = jnp.zeros((TAIL, rows), F32)
    dqt = []
    for h in range(OWN):
        s, qh = scores_of(f["qx"], f["kx"], masks[h], allowed)
        p = jnp.exp(s - lse_ref[h : h + 1, :])
        dab_h = jnp.where(masks[h][:, :BLOCK], dab, zero)
        dvb = dvb + dot(p.astype(BF16), dab_h)
        dp = dot(vb, dab_h, ((1,), (1,)))
        ds = p * (dp - jnp.sum(p * dp, axis=0, keepdims=True))
        dsb = ds.astype(BF16)
        dqt.append(dot(kt[head_rows(h)], dsb))
        dkx = dkx + dot(dsb, qh)
        along = jnp.sum(dsb.astype(F32), axis=0, keepdims=True)
        tail = jnp.where(iota((TAIL, rows), 0) == tail_lane(h, TERMS), along, tail)
    dqx = jnp.concatenate(dqt + [tail], axis=0).T
    dqb = dqx[:, :BLOCK] * HEAD_DIM**-0.5
    dkb = dkx[:, :BLOCK]

    def back(n, r, e):
        return r * (e - n * (dot_split(e * n, same_head, 2) * (1.0 / HEAD_DIM)))

    dq = back(f["qn"], f["rq"], dqb * q_gain)
    dks = back(f["kn"], f["rk"], dkb * k_gain)
    last = iota((rows, 1), 0) == rows - 1

    def mix_back(grad, rate, cur, prev):
        ahead = pltpu.roll(rate * grad * same_prev, rows - 1, 0)
        return (1.0 - rate) * grad + jnp.where(last, 0.0, ahead), grad * (prev - cur)

    dk, dak = mix_back(dks, f["ak"], f["k"], shifted(f["k"], same_prev))
    dv, dav = mix_back(dvb, f["av"], f["v"], shifted(f["v"], same_prev))

    onward = (iota((rows, rows), 1) >= iota((rows, rows), 0)).astype(BF16)
    keep = sum(dot(onward, term) for term in split(dqx[:, BLOCK:] - dkx[:, BLOCK:], TERMS))
    sig = sig_ref[...]
    drate = (
        dot_split(dak, backs_ref[0:BLOCK], 2)
        + dot_split(dav, backs_ref[BLOCK : 2 * BLOCK], 2)
        + dot_split(keep, backs_ref[2 * BLOCK :], 2)
    )
    lane = iota((rows, EXTRA), 1)
    drate = drate * (1.0 - sig) * jnp.where(lane < OWN, 1.0, sig)
    drate = jnp.where(lane < RATES, drate, 0.0)
    grads = jnp.concatenate([dq, dk, dv, dog, drate], axis=1).astype(BF16)
    dp_ref[...] = grads
    dh1 = dot(grads, w_ref[...], ((1,), (1,))).astype(BF16)

    @pl.when(bucket < 4)
    def _():
        near_ref[...] = dh1

    @pl.when(bucket >= 4)
    def _():
        far_ref[...] = dh1

    @pl.when(bucket == 0)
    def _():
        sums_ref[...] = jnp.zeros_like(sums_ref)

    sums_ref[0:1, 0:BLOCK] += jnp.sum(dqb * f["qn"], axis=0, keepdims=True)
    sums_ref[1:2, 0:BLOCK] += jnp.sum(dkb * f["kn"], axis=0, keepdims=True)
    sums_ref[2:3, 0:EXTRA] += jnp.sum(drate, axis=0, keepdims=True)


def rows_spec(rows, width):
    return pl.BlockSpec((rows, width), lambda i, lens, spots: (i, 0))


def whole_spec(dims):
    return pl.BlockSpec(dims, lambda i, lens, spots: (0,) * len(dims))


def spot_spec(rows):
    return pl.BlockSpec((1, rows * 3 // 2, EXTRA), lambda i, lens, spots: (spots[i], 0, 0))


def kept_specs(rows):
    return [rows_spec(rows, BLOCK) for _ in KEPT] + [rows_spec(rows, c) for c in (SPAN, SPAN, BLOCK)]


def attn_fwd(lens, spots, near, far, w, bias, wide, tails):
    buckets = lens.shape[0]
    width = near.shape[1]
    total = 2 * near.shape[0]
    rows = total // buckets
    return pl.pallas_call(
        attn_fwd_kernel,
        grid_spec=pltpu.PrefetchScalarGridSpec(
            num_scalar_prefetch=2,
            grid=(buckets,),
            in_specs=[
                near_spec(rows, width),
                far_spec(rows, width),
                whole_spec(w.shape),
                whole_spec(bias.shape),
                whole_spec(wide.shape),
                whole_spec(tails.shape),
            ],
            out_specs=[
                rows_spec(rows, width),
                spot_spec(rows),
                rows_spec(rows, BLOCK),
                rows_spec(8, rows),
                whole_spec((8, width)),
                whole_spec((8, 2 * EXTRA)),
                rows_spec(rows, EXTRA),
            ]
            + kept_specs(rows),
        ),
        out_shape=[
            shape((total, width), BF16),
            shape((buckets, rows * 3 // 2, EXTRA), BF16),
            shape((total, BLOCK), F32),
            shape((8 * buckets, rows), F32),
            shape((8, width), F32),
            shape((8, 2 * EXTRA), F32),
            shape((total, EXTRA), F32),
        ]
        + [shape((total, BLOCK), F32) for _ in KEPT]
        + [shape((total, c), BF16) for c in (SPAN, SPAN, BLOCK)],
        **settings(20, 60),
        name="attn_fwd",
    )(lens, spots, near, far, w, bias, wide, tails)


def near_spec(rows, width):
    return pl.BlockSpec((rows, width), lambda i, lens, spots: (jnp.minimum(i, 3), 0))


def far_spec(rows, width):
    return pl.BlockSpec((rows, width), lambda i, lens, spots: (jnp.maximum(i - 4, 0), 0))


def attn_bwd(lens, spots, gains, wide, backs, w, att, lse, dm, sig, *kept):
    buckets = lens.shape[0]
    total = att.shape[0]
    width = w.shape[0]
    rows = total // buckets
    return pl.pallas_call(
        attn_bwd_kernel,
        grid_spec=pltpu.PrefetchScalarGridSpec(
            num_scalar_prefetch=2,
            grid=(buckets,),
            in_specs=[whole_spec(x.shape) for x in (gains, wide, backs, w)]
            + [rows_spec(rows, BLOCK), rows_spec(8, rows), spot_spec(rows), rows_spec(rows, EXTRA)]
            + kept_specs(rows),
            out_specs=[
                rows_spec(rows, WIDE),
                whole_spec((8, 2 * EXTRA)),
                near_spec(rows, width),
                far_spec(rows, width),
            ],
        ),
        out_shape=[shape((total, WIDE), BF16), shape((8, 2 * EXTRA), F32)]
        + [shape((total // 2, width), BF16)] * 2,
        **settings(24, 60),
        name="attn_bwd",
    )(lens, spots, gains, wide, backs, w, att, lse, dm, sig, *kept)


def mid_fwd_kernel(spots_ref, got_ref, tok_ref, gain_ref, *refs):
    x2_ref, h2_ref = refs[TP:]
    acc = tok_ref[...].astype(F32)
    for i in range(TP):
        acc = acc + dot(unfold(got_ref[spots_ref[i]]), refs[i][...])
    x2_ref[...] = acc
    h2_ref[...] = (normed(acc)[0] * gain_ref[...]).astype(BF16)


def once(dims):
    return pl.BlockSpec(dims, lambda i: (0,) * len(dims))


def mix_specs(w):
    return [once((BLOCK, x.shape[1])) for x in w]


def mid_fwd(spots, got, w, tok, gain):
    rows, width = tok.shape
    return pl.pallas_call(
        mid_fwd_kernel,
        grid=(1,),
        in_specs=[SMEM, once(got.shape), once(tok.shape), once(gain.shape)] + mix_specs(w),
        out_specs=[once(tok.shape)] * 2,
        out_shape=[shape(tok.shape, F32), shape(tok.shape, BF16)],
        **settings(5, 40),
        name="mid_fwd",
    )(spots, got, tok, gain, *w)


def mid_bwd_kernel(spots_ref, a_ref, b_ref, c_ref, d_ref, x2_ref, cot_ref, gain_ref, got_ref, *refs):
    dx2_ref, dm_ref, near_ref, far_ref = refs[TP:]
    dh2 = a_ref[...] + b_ref[...].astype(F32) + c_ref[...].astype(F32) + d_ref[...].astype(F32)
    n2, r2 = normed(x2_ref[...])
    dx2 = cot_ref[...].astype(F32) + norm_back(n2, r2, dh2 * gain_ref[...])
    dx2_ref[...] = dx2
    dxb = dx2.astype(BF16)
    for i in range(TP):
        dm = dot(dxb, refs[i][...], ((1,), (1,)))
        dm_ref[spots_ref[i]] = fold(dm).astype(BF16)
        out_ref = near_ref if i < 4 else far_ref
        piece = dot(unfold(got_ref[spots_ref[i]]), dxb, ((0,), (0,)))
        out_ref[(i % 4) * BLOCK : (i % 4 + 1) * BLOCK, :] = piece.astype(BF16)


def mid_bwd(spots, parts, x2, cot, gain, got, w):
    rows, width = x2.shape
    arrays = (*parts, x2, cot, gain, got)
    outs = [
        shape((rows, width), F32),
        shape((TP, rows * 3 // 2, EXTRA), BF16),
        shape((4 * BLOCK, width), BF16),
        shape((4 * BLOCK, width), BF16),
    ]
    return pl.pallas_call(
        mid_bwd_kernel,
        grid=(1,),
        in_specs=[SMEM] + [once(x.shape) for x in arrays] + mix_specs(w),
        out_specs=[once(x.shape) for x in outs],
        out_shape=outs,
        **settings(9, 48),
        name="mid_bwd",
    )(spots, *arrays, *w)


def ffn_kernel(lens_ref, h2_ref, cot_ref, gu_ref, dn_ref, ab_ref, dgu_ref, *out_refs):
    rows, ff = h2_ref.shape[0], dn_ref.shape[0]
    total = jnp.int32(0)
    for j in range(lens_ref.shape[1]):
        total = total + lens_ref[pl.program_id(0), j]
    live = (iota((rows, 1), 0) < total).astype(F32)
    gu = dot(h2_ref[...], gu_ref[...])
    da = dot(cot_ref[...], dn_ref[...], ((1,), (1,))) * live
    gate, up = gu[:, :ff], gu[:, ff:]
    sg = jax.nn.sigmoid(gate)
    act = gate * sg
    ab = (act * up * live).astype(BF16)
    dgate = (da * up * sg * (1.0 + gate * (1.0 - sg))).astype(BF16)
    dup = (da * act).astype(BF16)
    ab_ref[...] = ab
    dgu_ref[:, :ff] = dgate
    dgu_ref[:, ff:] = dup
    dh2 = dot(dgate, gu_ref[:, :ff], ((1,), (1,))) + dot(dup, gu_ref[:, ff:], ((1,), (1,)))
    dh2 = dh2.astype(BF16)
    out = dot(ab, dn_ref[...]).astype(BF16)
    last = pl.program_id(0) == pl.num_programs(0) - 1

    @pl.when(jnp.logical_not(last))
    def _():
        out_refs[0][...] = out
        out_refs[1][...] = dh2

    @pl.when(last)
    def _():
        out_refs[2][...] = out
        out_refs[3][...] = dh2


def ffn(lens, h2, cot, gu, dn):
    buckets = lens.shape[0]
    total, width = h2.shape
    rows = total // buckets
    ff = dn.shape[0]

    def block(columns):
        return pl.BlockSpec((rows, columns), lambda i: (i, 0))

    def whole(dims):
        return pl.BlockSpec(dims, lambda i: (0, 0))

    most = pl.BlockSpec((rows, width), lambda i: (jnp.minimum(i, buckets - 2), 0))
    return pl.pallas_call(
        ffn_kernel,
        grid=(buckets,),
        in_specs=[SMEM, block(width), block(width), whole(gu.shape), whole(dn.shape)],
        out_specs=[block(ff), block(2 * ff), most, most, whole((rows, width)), whole((rows, width))],
        out_shape=[shape((total, ff), BF16), shape((total, 2 * ff), BF16)]
        + [shape((total - rows, width), BF16)] * 2
        + [shape((rows, width), BF16)] * 2,
        **settings(4 * buckets, 40),
        name="ffn",
    )(lens, h2, cot, gu, dn)


def grad_down(ab, cot):
    ff, width = ab[0].shape[1], cot[0].shape[1]
    steps = 4
    columns = width // steps

    def kernel(ab0_ref, ab1_ref, cot0_ref, cot1_ref, out_ref):
        res = dot(ab0_ref[...], cot0_ref[...], ((0,), (0,))) + dot(ab1_ref[...], cot1_ref[...], ((0,), (0,)))
        out_ref[...] = res.astype(BF16)

    return pl.pallas_call(
        kernel,
        grid=(steps,),
        in_specs=[pl.BlockSpec(x.shape, lambda i: (0, 0)) for x in ab]
        + [pl.BlockSpec((x.shape[0], columns), lambda i: (0, i)) for x in cot],
        out_specs=pl.BlockSpec((ff, columns), lambda i: (0, i)),
        out_shape=shape((ff, width), BF16),
        **settings(6, 60),
        name="grad_down",
    )(*ab, *cot)


def grad_gu(h2, dgu, share):
    rows, width = h2[0].shape
    own_rows = width // (TP * share)
    columns = dgu[0].shape[1]
    steps = TP // 2

    def kernel(left0_ref, left1_ref, right0_ref, right1_ref, out_ref):
        res = dot(left0_ref[...], right0_ref[...], ((0,), (0,)))
        res = res + dot(left1_ref[...], right1_ref[...], ((0,), (0,)))
        for k in range(2):
            for z in range(share):
                at = (k * share + z) * own_rows
                out_ref[z, k] = res[at : at + own_rows].astype(BF16)

    return pl.pallas_call(
        kernel,
        grid=(steps,),
        in_specs=[pl.BlockSpec((rows, width // steps), lambda i: (0, i))] * 2
        + [pl.BlockSpec((rows, columns), lambda i: (0, 0))] * 2,
        out_specs=pl.BlockSpec((share, 2, own_rows, columns), lambda i: (0, i, 0, 0)),
        out_shape=shape((share, TP, own_rows, columns), BF16),
        **settings(11, 60),
        name="grad_gu",
    )(*h2, *dgu)


def grad_in(place, sums, left, right, share):
    own_rows = left.shape[1] // (TP * share)
    columns = right.shape[1]
    steps = TP // 2

    def kernel(place_ref, sums_ref, left_ref, right_ref, out_ref):
        res = dot(left_ref[...], right_ref[...], ((0,), (0,)))
        lane, row = iota((BLOCK, EXTRA), 1), iota((BLOCK, EXTRA), 0)
        turned = sums_ref[...].T[0:BLOCK]
        bias = jnp.where((lane == row % own_rows) & (lane < RATES), sums_ref[2:3, 0:EXTRA], 0.0)
        bias = jnp.sum(bias, axis=1, keepdims=True)
        for k in range(2):
            mine = (pl.program_id(0) * 2 + k == place_ref[0]).astype(F32)
            extra = res[k * BLOCK : (k + 1) * BLOCK, CORE:WIDE]
            extra = jnp.where(lane == RATES, turned[:, 0:1] * mine, extra)
            extra = jnp.where(lane == RATES + 1, turned[:, 1:2] * mine, extra)
            extra = jnp.where(lane == RATES + 2, bias, extra)
            for z in range(share):
                at = z * own_rows
                rest = k * BLOCK + at
                out_ref[z, k, :, :CORE] = res[rest : rest + own_rows, :CORE].astype(BF16)
                out_ref[z, k, :, CORE:] = extra[at : at + own_rows].astype(BF16)

    return pl.pallas_call(
        kernel,
        grid=(steps,),
        in_specs=[
            SMEM,
            pl.BlockSpec(sums.shape, lambda i: (0, 0)),
            pl.BlockSpec((left.shape[0], left.shape[1] // steps), lambda i: (0, i)),
            pl.BlockSpec(right.shape, lambda i: (0, 0)),
        ],
        out_specs=pl.BlockSpec((share, 2, own_rows, columns), lambda i: (0, i, 0, 0)),
        out_shape=shape((share, TP, own_rows, columns), BF16),
        **settings(11, 60),
        name="grad_in",
    )(place, sums, left, right)


def own_share(part):
    columns = part.shape[-1]
    summed = lax.psum_scatter(part.reshape(-1, columns), "sh", scatter_dimension=0, tiled=True)
    return summed.reshape(TP, -1, columns)


def swap(blocks):
    return lax.all_to_all(blocks, "tp", 0, 0, tiled=True)


def body(
    tokens,
    doc_lengths,
    norm_gain,
    w_attn_in,
    w_rates,
    rate_bias,
    q_gain,
    k_gain,
    w_out,
    ffn_gain,
    w_gate_up,
    w_down,
    cotangent,
):
    place = lax.axis_index("tp")
    share = lax.axis_size("sh")
    width = tokens.shape[1]
    own_rows = w_attn_in.shape[0]
    spots = place ^ jnp.array(OFFSETS, jnp.int32)

    gains = jnp.stack([norm_gain, q_gain, k_gain, ffn_gain])
    packed, w_mix = phase(pack_in(doc_lengths, w_attn_in, w_rates, gains), w_out)
    got_in = swap(packed)
    w_in = lax.all_gather(got_in, "sh", axis=1).reshape(width, WIDE)
    lens_all = got_in[:, 0, CORE + LENS_AT : CORE + LENS_AT + doc_lengths.shape[0]].astype(jnp.int32)
    lens = lens_all[spots]
    bias = lax.dynamic_index_in_dim(rate_bias.reshape(3, TP, OWN), place, 1, False).reshape(1, RATES)
    bias = jnp.pad(bias, ((0, 7), (0, EXTRA - RATES)))

    tok, w_gu, w_mix, _ = phase(tokens, w_gate_up, w_mix, got_in)
    two_four, w_mix = phase(sides(tok), gather_shares(w_mix))
    tok = join_rows(tok, *two_four, *diagonal(*two_four))
    tok, packed = phase(tok, pack_gu(w_gu))
    joined = join_ffn(swap(packed), w_down)
    far = flip(tok, 1)
    w_gu, w_dn = open_ffn(lax.all_gather(joined, "sh", axis=0), w_down.shape[0], width)

    wide, tails, backs = constants()
    beside = phase(join_rows(in_order(w_mix), cotangent), joined)[0]
    two_four = sides(beside)
    h1, mixed, att, lse, gains, gain_heads, *kept = attn_fwd(lens, spots, tok, far, w_in, bias, wide, tails)
    gain_one, gain_two = gains[0:1], gains[3:4]
    mixed, two_four = phase(mixed, two_four)
    near = [beside, *two_four]
    six = diagonal(*two_four)
    got_mixed, six, far = phase(swap(mixed), six, [flip(x, 1) for x in near])
    far = [*far, *[flip(x, 1) for x in six]]
    near = [*near, *six]
    x2, h2 = mid_fwd(spots, got_mixed, near[:4] + far[:4], tokens, gain_two)

    first, second = (0, 2, 4, 1), (3, 5, 7, 6)
    lens_of = [jnp.stack([lens[OFFSETS.index(d)] for d in order]) for order in (first, second)]
    h2, near, far = phase(h2, near, far)
    w_mix = near[:4] + far[:4]
    two, four = sides(h2)
    one = flip(h2, 1)
    cot = [
        join_rows((near[0], BLOCK), (near[1], BLOCK), (near[2], BLOCK), (far[0], BLOCK)),
        join_rows((far[1], BLOCK), (far[2], BLOCK), (far[3], BLOCK), far[4], (near[3], BLOCK), near[4]),
    ]
    one, two, four, cot = phase(one, two, four, cot)
    six = diagonal(two, four)
    three, five = flip(two, 1), flip(four, 1)
    h2 = join_rows(h2, two, four, one)
    found = ffn(lens_of[0], h2, cot[0], w_gu, w_dn)
    found, six, three, five = phase(found, six, three, five)
    out_one, dh2_one = flip(found[4], 1), flip(found[5], 1)
    six = jnp.concatenate(six, axis=0)
    six, seven = phase(six, flip(six, 1))
    h2 = h2, join_rows(three, five, seven, six)
    found = [found, ffn(lens_of[1], h2[1], cot[1], w_gu, w_dn)]
    found, dh2_one, out_one = phase(found, dh2_one, out_one)
    ab, dgu, out, dh2, out_last, dh2_last = zip(*found)
    dh2_far, dw_dn, out_far = phase(flip(dh2[1], 1), grad_down(ab, cot), flip(out[1], 1))

    def folded(near, six, one, far):
        rows = six.shape[0]
        parts = [[x[i * rows : (i + 1) * rows] for i in range(3)] for x in (near, far)]
        return both_cores([*parts[0], six], [one, *parts[1]])

    own, low = folded(dh2[0], dh2_last[1], dh2_one, dh2_far)
    dw_dn = lax.psum_scatter(dw_dn, "sh", scatter_dimension=0, tiled=True)
    own, low, dgu, out_far = phase(own, low, dgu, out_far)
    layer_own, layer_low = folded(out[0], out_last[1], out_one, out_far)
    dh2, dw_gu, dw_dn, own, layer_low = phase(send(low), grad_gu(h2, dgu, share), dw_dn, own, layer_low)
    dw_gu = own_share(dw_gu)

    found, layer_low = phase(
        mid_bwd(spots, [own] + dh2, x2, cotangent, gain_two, got_mixed, w_mix), relay_six(layer_low)
    )
    dx2, dm, mix_near, mix_far = found
    mix_own, mix_low = both_cores(quarters(mix_near), quarters(flip(mix_far, 1)))
    got_dm, mix_own, mix_low, layer_low = phase(swap(dm), mix_own, mix_low, add_six(layer_low))
    layer, mix_low, found = phase(
        (flip(layer_low[0], 2), flip(layer_low[1], 4)),
        relay_six(mix_low),
        attn_bwd(lens, spots, gain_heads, wide, backs, w_in, att, lse, got_dm, *kept),
    )
    dp, sums, dh1_near, dh1_far = found
    layer_out = (x2 + total_of((layer_own, *layer))).astype(BF16)

    mix_low = add_six(mix_low)
    mix = flip(mix_low[0], 2), flip(mix_low[1], 4)
    dh1_far, dw_in, got_gu = phase(
        flip(dh1_far, 1), grad_in(place.reshape(1), sums, h1, dp, share), swap(dw_gu)
    )
    dw_in = own_share(dw_in)
    dh1_own, dh1_low = both_cores(quarters(dh1_near), quarters(dh1_far))
    dh1, dw_in, mix = phase(send(dh1_low), dw_in, mix)
    mix = to_shares(total_of((mix_own, *mix)).astype(BF16))
    n1, r1 = normed(tokens.astype(F32))
    d_tokens = dx2 + norm_back(n1, r1, total_of([dh1_own] + dh1) * gain_one)

    d_w_attn_in, d_w_rates, small = unpack_in(swap(dw_in), w_attn_in, w_rates, norm_gain)
    d_w_gate_up, small_gu = unpack_gu(got_gu, w_gate_up, ffn_gain)
    d_ffn_gain = small_gu[0, :own_rows]
    small, mix = phase(small, mix)
    d_w_out = total_of(mix)
    return (
        layer_out,
        d_tokens,
        small[0, :own_rows],
        d_w_attn_in,
        d_w_rates,
        small[3, : w_rates.shape[1]],
        small[1, :own_rows],
        small[2, :own_rows],
        d_w_out,
        d_ffn_gain,
        d_w_gate_up,
        dw_dn.astype(F32),
    )


def solution(mesh):
    devices = mesh.devices.reshape(TP, -1)
    grid = Mesh(devices, ("tp", "sh"))
    rows = P(("tp", "sh"), None)
    flat = P(("tp", "sh"))
    in_specs = (rows, flat, flat, rows, rows, P(), flat, flat, rows, flat, rows, rows, rows)
    out_specs = (rows, rows, flat, rows, rows, P(), flat, flat, rows, flat, rows, rows)
    return jax.shard_map(body, mesh=grid, in_specs=in_specs, out_specs=out_specs, check_vma=False)
```

```python
import jax
import jax.numpy as jnp
import numpy as np
from jax import lax
from jax.experimental import pallas as pl
from jax.experimental.pallas import tpu as pltpu
from jax.sharding import Mesh
from jax.sharding import PartitionSpec as P

HEADS = 24
HEAD_DIM = 64
EPS = 1e-06
NEG = -1e30
TP = 8
OWN = HEADS // TP
BLOCK = OWN * HEAD_DIM
CORE = 4 * BLOCK
EXTRA = 128
WIDE = CORE + EXTRA
RATES = 3 * OWN
GAIN_AT = RATES
LENS_AT = RATES + 4
OFFSETS = (0, 2, 4, 6, 1, 3, 5, 7)
F32 = jnp.float32
BF16 = jnp.bfloat16


def flip(array, offset):
    return lax.ppermute(array, "tp", [(i, i ^ offset) for i in range(TP)])


def sides(own):
    return flip(own, 2), flip(own, 4)


def diagonal(two, four):
    cut = two.shape[0] // 2
    return flip(two[:cut], 4), flip(four[cut:], 2)


def others(own):
    return [flip(own, d) for d in (2, 4, 6)]


def both_cores(near, far):
    sums = [x.astype(F32) + y.astype(F32) for x, y in zip(near, far)]
    return sums[0], [x.astype(BF16) for x in sums[1:]]


def two_sums(near, far):
    rows = near.shape[0] // 2
    return [near[i : i + rows].astype(F32) + far[i : i + rows].astype(F32) for i in (0, rows)]


def quarters(array):
    rows = array.shape[0] // 4
    return [array[i * rows : (i + 1) * rows] for i in range(4)]


def send(blocks):
    return [flip(x, d) for x, d in zip(blocks, (2, 4, 6))]


def relay_six(blocks):
    two, four, six = blocks
    cut = six.shape[0] // 2
    return two, four, flip(six[:cut], 2), flip(six[cut:], 4)


def add_six(blocks):
    two, four, over_two, over_four = blocks
    cut = over_two.shape[0]
    two = jnp.concatenate([two[:cut], (two[cut:].astype(F32) + over_four.astype(F32)).astype(BF16)], axis=0)
    four = jnp.concatenate([(four[:cut].astype(F32) + over_two.astype(F32)).astype(BF16), four[cut:]], axis=0)
    return two, four


def gather_shares(own):
    share = lax.axis_size("sh")
    return [own] + [lax.ppermute(own, "sh", [(i, (i + k) % share) for i in range(share)]) for k in range(1, share)]


def in_order(pieces):
    here = lax.axis_index("sh")
    share = len(pieces)
    out = jnp.zeros((share,) + pieces[0].shape, pieces[0].dtype)
    for k, piece in enumerate(pieces):
        out = lax.dynamic_update_index_in_dim(out, piece, (here - k) % share, 0)
    return out.reshape((-1,) + pieces[0].shape[1:])


def to_shares(part):
    share = lax.axis_size("sh")
    here = lax.axis_index("sh")
    blocks = part.reshape(share, -1, part.shape[1])
    picked = [lax.dynamic_index_in_dim(blocks, (here + k) % share, 0, False) for k in range(share)]
    return picked[:1] + [
        lax.ppermute(picked[k], "sh", [(i, (i + k) % share) for i in range(share)]) for k in range(1, share)
    ]


def total_of(parts):
    return sum(term.astype(F32) for term in parts)


def phase(*values):
    return lax.optimization_barrier(values)


def normed(field_in):
    factor = lax.rsqrt(jnp.mean(field_in * field_in, axis=-1, keepdims=True) + EPS)
    return field_in * factor, factor


def norm_back(normal, factor, grad_in):
    return factor * (grad_in - normal * jnp.mean(grad_in * normal, axis=-1, keepdims=True))


def dot(a, b, dims=((1,), (0,)), precision=None):
    return lax.dot_general(a, b, (dims, ((), ())), precision=precision, preferred_element_type=F32)


def iota(shape, dim):
    return lax.broadcasted_iota(jnp.int32, shape, dim)


def settings(us, mib):
    cost = pl.CostEstimate(flops=int(us * 1e7), bytes_accessed=int(us * 1e4), transcendentals=0)
    return dict(compiler_params=pltpu.CompilerParams(vmem_limit_bytes=mib * 2**20), cost_estimate=cost)


SMEM = pl.BlockSpec(memory_space=pltpu.SMEM)
VMEM = pl.BlockSpec(memory_space=pltpu.VMEM)


def shape(dims, dtype):
    return jax.ShapeDtypeStruct(dims, dtype)


def rate_picks(t, rows, columns, flipped=False):
    whole, own = iota((rows, columns), 1 if flipped else 0), iota((rows, columns), 0 if flipped else 1)
    kind, head = own // OWN, own % OWN
    return ((own < RATES) & (whole == kind * HEADS + t * OWN + head)).astype(BF16)


def pack_in_kernel(lens_ref, w_ref, rates_ref, gains_ref, out_ref):
    rows, width = w_ref.shape[0], w_ref.shape[1] // 4
    picks = (iota((4, EXTRA), 1) == GAIN_AT + iota((4, EXTRA), 0)).astype(BF16)
    beside = dot(gains_ref[...], picks, ((0,), (0,)))
    lane, row = iota((rows, EXTRA), 1), iota((rows, EXTRA), 0)
    for j in range(lens_ref.shape[0]):
        beside = jnp.where((lane == LENS_AT + j) & (row == 0), lens_ref[j].astype(F32), beside)
    for t in range(TP):
        for b in range(4):
            at = b * width + t * BLOCK
            out_ref[t, :, b * BLOCK : (b + 1) * BLOCK] = w_ref[:, at : at + BLOCK]
        rates = dot(rates_ref[...], rate_picks(t, rates_ref.shape[1], EXTRA))
        out_ref[t, :, CORE:WIDE] = (rates + beside).astype(BF16)


def pack_in(lens, w, rates, gains):
    return pl.pallas_call(
        pack_in_kernel,
        in_specs=[SMEM, VMEM, VMEM, VMEM],
        out_specs=VMEM,
        out_shape=shape((TP, w.shape[0], WIDE), BF16),
        **settings(3, 16),
        name="pack_in",
    )(lens, w, rates, gains)


def pack_gu_kernel(w_ref, out_ref):
    ff = w_ref.shape[1] // 2
    own = ff // TP
    for t in range(TP):
        out_ref[t, :, :own] = w_ref[:, t * own : (t + 1) * own]
        out_ref[t, :, own:] = w_ref[:, ff + t * own : ff + (t + 1) * own]


def pack_gu(w):
    return pl.pallas_call(
        pack_gu_kernel,
        in_specs=[VMEM],
        out_specs=VMEM,
        out_shape=shape((TP, w.shape[0], w.shape[1] // TP), BF16),
        **settings(2, 16),
        name="pack_gu",
    )(w)


def join_ffn(got, down):
    columns = got.shape[2]
    top, rows = got.shape[0] * got.shape[1], down.shape[0]
    half = rows // 2

    def kernel(got_ref, down_ref, out_ref):
        for t in range(TP):
            out_ref[t * got.shape[1] : (t + 1) * got.shape[1], :] = got_ref[t]
        out_ref[top : top + rows, :] = down_ref[:, :columns]
        out_ref[top + rows :, : columns // 2] = down_ref[:half, columns:]
        out_ref[top + rows :, columns // 2 :] = down_ref[half:, columns:]

    return pl.pallas_call(
        kernel,
        in_specs=[VMEM, VMEM],
        out_specs=VMEM,
        out_shape=shape((top + rows + half, columns), BF16),
        **settings(2, 16),
        name="join_ffn",
    )(got, down)


def open_ffn(joined, down_rows, width):
    share, _, columns = joined.shape
    own_rows = width // (TP * share)
    top = TP * own_rows
    half = down_rows // 2

    def kernel(in_ref, gu_ref, down_ref):
        for z in range(share):
            for t in range(TP):
                at = (t * share + z) * own_rows
                gu_ref[at : at + own_rows, :] = in_ref[z, t * own_rows : (t + 1) * own_rows, :]
            at = z * down_rows
            down_ref[at : at + down_rows, :columns] = in_ref[z, top : top + down_rows, :]
            down_ref[at : at + half, columns:] = in_ref[z, top + down_rows :, : columns // 2]
            down_ref[at + half : at + down_rows, columns:] = in_ref[z, top + down_rows :, columns // 2 :]

    return pl.pallas_call(
        kernel,
        in_specs=[VMEM],
        out_specs=[VMEM, VMEM],
        out_shape=[shape((width, columns), BF16), shape((share * down_rows, width), BF16)],
        **settings(4, 16),
        name="open_ffn",
    )(joined)


def join_rows(*pieces):
    pieces = [x if isinstance(x, tuple) else (x, 0) for x in pieces]
    total = sum(x.shape[0] - first for x, first in pieces)

    def kernel(*refs):
        at = 0
        for ref, (x, first) in zip(refs, pieces):
            more = x.shape[0] - first
            refs[-1][at : at + more, :] = ref[first:, :]
            at += more

    return pl.pallas_call(
        kernel,
        in_specs=[VMEM] * len(pieces),
        out_specs=VMEM,
        out_shape=shape((total, pieces[0][0].shape[1]), pieces[0][0].dtype),
        **settings(2, 24),
        name="join_rows",
    )(*[x for x, _ in pieces])


def unpack_in_kernel(got_ref, w_ref, rates_ref, gain_ref, dw_ref, drates_ref, small_ref):
    rows, width = w_ref.shape[0], w_ref.shape[1] // 4
    along = jnp.zeros((rows, 1), F32)
    drates = jnp.zeros((rows, EXTRA), F32)
    sums = jnp.zeros((rows, EXTRA), F32)
    bias = jnp.zeros((rows, EXTRA), F32)
    lane, row = iota((rows, EXTRA), 1), iota((rows, EXTRA), 0)
    for t in range(TP):
        for b in range(4):
            at = b * width + t * BLOCK
            piece = got_ref[t, :, b * BLOCK : (b + 1) * BLOCK].astype(F32)
            dw_ref[:, at : at + BLOCK] = piece
            along = along + jnp.sum(piece * w_ref[:, at : at + BLOCK].astype(F32), axis=1, keepdims=True)
        extra = got_ref[t, :, CORE:WIDE]
        drates = drates + dot(extra, rate_picks(t, EXTRA, EXTRA, True))
        extra = extra.astype(F32)
        sums = sums + extra
        spot = (row // OWN) * HEADS + t * OWN + row % OWN
        bias = bias + jnp.where((lane == spot) & (row < RATES), extra[:, RATES + 2 : RATES + 3], 0.0)
    columns = rates_ref.shape[1]
    drates_ref[...] = drates[:, :columns]
    along = along + jnp.sum(drates[:, :columns] * rates_ref[...].astype(F32), axis=1, keepdims=True)
    turned = jnp.where(lane == 0, along, 0.0) + jnp.where(lane == 1, sums[:, RATES : RATES + 1], 0.0)
    turned = turned + jnp.where(lane == 2, sums[:, RATES + 1 : RATES + 2], 0.0)
    pick = (iota((rows, EXTRA), 0) == iota((rows, EXTRA), 1)).astype(F32)
    turned = dot(turned, pick, ((0,), (0,)), lax.Precision.HIGHEST)
    small_ref[0:1, :] = turned[0:1, :] / gain_ref[...]
    small_ref[1:3, :] = turned[1:3, :]
    small_ref[3:4, :] = jnp.sum(bias, axis=0, keepdims=True)
    small_ref[4:8, :] = jnp.zeros((4, EXTRA), F32)


def unpack_in(got, w, rates, gain):
    rows = w.shape[0]
    gain = jnp.pad(gain.astype(F32)[None], ((0, 0), (0, EXTRA - rows)), constant_values=1.0)
    return pl.pallas_call(
        unpack_in_kernel,
        in_specs=[VMEM] * 4,
        out_specs=[VMEM] * 3,
        out_shape=[shape(w.shape, F32), shape(rates.shape, F32), shape((8, EXTRA), F32)],
        **settings(5, 16),
        name="unpack_in",
    )(got, w, rates, gain)


def unpack_gu_kernel(got_ref, w_ref, gain_ref, dw_ref, small_ref):
    rows, ff = w_ref.shape[0], w_ref.shape[1] // 2
    own = ff // TP
    along = jnp.zeros((rows, 1), F32)
    for t in range(TP):
        for half in range(2):
            at = half * ff + t * own
            piece = got_ref[t, :, half * own : (half + 1) * own].astype(F32)
            dw_ref[:, at : at + own] = piece
            along = along + jnp.sum(piece * w_ref[:, at : at + own].astype(F32), axis=1, keepdims=True)
    lane = iota((rows, EXTRA), 1)
    pick = (iota((rows, EXTRA), 0) == lane).astype(F32)
    turned = dot(jnp.where(lane == 0, along, 0.0), pick, ((0,), (0,)), lax.Precision.HIGHEST)
    small_ref[...] = turned[0:8, :] / gain_ref[...]


def unpack_gu(got, w, gain):
    rows = w.shape[0]
    gain = jnp.pad(gain.astype(F32)[None], ((0, 0), (0, EXTRA - rows)), constant_values=1.0)
    return pl.pallas_call(
        unpack_gu_kernel,
        in_specs=[VMEM] * 3,
        out_specs=[VMEM] * 2,
        out_shape=[shape(w.shape, F32), shape((8, EXTRA), F32)],
        **settings(3, 16),
        name="unpack_gu",
    )(got, w, gain)


def fold(block):
    cut = block.shape[0] // 2
    tail = jnp.concatenate([block[:cut, EXTRA:], block[cut:, EXTRA:]], axis=1)
    return jnp.concatenate([block[:, :EXTRA], tail], axis=0)


def unfold(block):
    rows = 2 * block.shape[0] // 3
    tail = block[rows:]
    tail = jnp.concatenate([tail[:, : BLOCK - EXTRA], tail[:, BLOCK - EXTRA :]], axis=0)
    return jnp.concatenate([block[:rows], tail], axis=1)


def split(field_in, count):
    terms = []
    for _ in range(count):
        terms.append(field_in.astype(BF16))
        field_in = field_in - terms[-1].astype(F32)
    return terms


def dot_split(field_in, picks, count):
    return sum(dot(term, picks) for term in split(field_in, count))


TAIL = 64
SPAN = BLOCK + TAIL
TERMS = 3


def tail_lane(h, term):
    return 8 * h + term


def constants():
    head = np.arange(BLOCK) // HEAD_DIM
    same = head[:, None] == head[None, :]
    extra = np.arange(EXTRA)
    key_lanes = extra[:, None] == OWN + head[None, :]
    value_lanes = extra[:, None] == 2 * OWN + head[None, :]
    to_query = np.zeros((TERMS, EXTRA, TAIL))
    to_key = np.zeros((TERMS, EXTRA, TAIL))
    from_tail = np.zeros((TAIL, EXTRA))
    for h in range(OWN):
        for term in range(TERMS):
            to_query[term, h, tail_lane(h, term)] = 1
            to_key[term, h, tail_lane(h, TERMS + term)] = -1
        from_tail[tail_lane(h, TERMS), h] = 1
    wide = np.concatenate([same, key_lanes, value_lanes], axis=0)
    tails = np.concatenate([to_query.reshape(-1, TAIL), to_key.reshape(-1, TAIL)], axis=0)
    backs = np.concatenate([key_lanes.T, value_lanes.T, from_tail], axis=0)
    return tuple(jnp.asarray(x, BF16) for x in (wide, tails, backs))


def places_of(lens_ref, bucket, rows):
    ends = []
    total = jnp.int32(0)
    for j in range(lens_ref.shape[1]):
        total = total + lens_ref[bucket, j]
        ends.append(total)

    def segment(place):
        seg = jnp.zeros(place.shape, jnp.int32)
        for end in ends:
            seg = seg + (end <= place).astype(jnp.int32)
        return seg

    col = iota((rows, 1), 0)
    row = iota((1, rows), 1)
    seg_col = segment(col)
    allowed = (col <= row) & (segment(row) == seg_col)
    live = (col < total).astype(F32)
    same_prev = ((col > 0) & (seg_col == segment(col - 1))).astype(F32)
    return allowed, live, same_prev


KEPT = ("qn", "kn", "rq", "rk", "ak", "av", "k", "v", "g")
KEPT_LOW = ("qx", "kx", "vb")


def front(proj, bias_ref, gains_ref, wide_ref, tails_ref, same_prev):
    rows = proj.shape[0]
    q = proj[:, 0:BLOCK]
    k = proj[:, BLOCK : 2 * BLOCK]
    v = proj[:, 2 * BLOCK : 3 * BLOCK]
    og = proj[:, 3 * BLOCK : CORE]
    rate = proj[:, CORE:WIDE] + bias_ref[0:1, :]
    sig = jax.nn.sigmoid(rate)
    log_keep = jnp.minimum(rate, 0.0) - jnp.log1p(jnp.exp(-jnp.abs(rate)))
    upto = (iota((rows, rows), 1) <= iota((rows, rows), 0)).astype(BF16)
    decay = sum(dot(upto, term) for term in split(log_keep, TERMS))
    same_head = wide_ref[0:BLOCK]
    ak = dot_split(sig, wide_ref[BLOCK : BLOCK + EXTRA], 2)
    av = dot_split(sig, wide_ref[BLOCK + EXTRA :], 2)
    ks = ak * shifted(k, same_prev) + (1.0 - ak) * k
    vs = av * shifted(v, same_prev) + (1.0 - av) * v

    def head_norm(u):
        factor = lax.rsqrt(dot_split(u * u, same_head, 2) * (1.0 / HEAD_DIM) + EPS)
        return u * factor, factor

    qn, rq = head_norm(q)
    kn, rk = head_norm(ks)
    q_gain, k_gain = gains_ref[0:1, 0:BLOCK], gains_ref[1:2, 0:BLOCK]
    qb = (qn * q_gain).astype(BF16) * jnp.asarray(HEAD_DIM**-0.5, BF16)
    kb = (kn * k_gain).astype(BF16)

    terms = split(decay, TERMS)
    lane = iota((1, TAIL), 1)
    ones_q = ((lane % 8 >= TERMS) & (lane % 8 < 2 * TERMS)).astype(F32)
    ones_k = (lane % 8 < TERMS).astype(F32)
    q_tail = ones_q + sum(dot(terms[t], tails_ref[t * EXTRA : (t + 1) * EXTRA]) for t in range(TERMS))
    k_tail = ones_k + sum(
        dot(terms[t], tails_ref[(TERMS + t) * EXTRA : (TERMS + t + 1) * EXTRA]) for t in range(TERMS)
    )
    qx = jnp.concatenate([qb, q_tail.astype(BF16)], axis=1)
    kx = jnp.concatenate([kb, k_tail.astype(BF16)], axis=1)
    return dict(
        qn=qn, kn=kn, rq=rq, rk=rk, ak=ak, av=av, k=k, v=v, g=jax.nn.sigmoid(og),
        qx=qx, kx=kx, vb=vs.astype(BF16), vs=vs, sig=sig,
    )


def shifted(array, same_prev):
    return pltpu.roll(array, 1, 0) * same_prev


def head_masks(rows):
    span = iota((rows, SPAN), 1)
    masks = []
    for h in range(OWN):
        feature = (span >= h * HEAD_DIM) & (span < (h + 1) * HEAD_DIM)
        masks.append(feature | ((span >= BLOCK + 8 * h) & (span < BLOCK + 8 * (h + 1))))
    return masks


def scores_of(qx, kx, mask, allowed):
    qh = jnp.where(mask, qx, jnp.zeros_like(qx))
    return jnp.where(allowed, dot(kx, qh, ((1,), (1,))), NEG), qh


def head_rows(h):
    return slice(h * HEAD_DIM, (h + 1) * HEAD_DIM)


def attn_fwd_kernel(
    lens_ref, spots_ref, near_ref, far_ref, w_ref, bias_ref, wide_ref, tails_ref,
    h1_ref, mixed_ref, att_ref, lse_ref, gains_ref, heads_ref, sig_ref, *kept_refs
):
    picks = (iota((8, EXTRA), 1) == GAIN_AT + iota((8, EXTRA), 0)) & (iota((8, EXTRA), 0) < 4)
    picks = picks.astype(BF16)
    gains = dot(picks, w_ref[:, CORE:WIDE], ((1,), (1,)))
    gains_ref[...] = gains
    at = pl.multiple_of(spots_ref[0] * BLOCK, BLOCK)
    heads = dot(picks, w_ref[pl.ds(at, BLOCK), CORE:WIDE], ((1,), (1,)))
    heads_ref[0:1, 0:BLOCK] = heads[1:2]
    heads_ref[1:2, 0:BLOCK] = heads[2:3]
    tok = jnp.where(pl.program_id(0) < 4, near_ref[...], far_ref[...]).astype(F32)
    h1 = (normed(tok)[0] * gains[0:1]).astype(BF16)
    h1_ref[...] = h1
    rows = h1.shape[0]
    allowed, live, same_prev = places_of(lens_ref, pl.program_id(0), rows)
    f = front(dot(h1, w_ref[...]), bias_ref, heads_ref, wide_ref, tails_ref, same_prev)
    sig_ref[...] = f["sig"]
    for name, ref in zip(KEPT + KEPT_LOW, kept_refs):
        ref[...] = f[name]
    vt = f["vs"].T.astype(BF16)
    att = []
    for h, mask in enumerate(head_masks(rows)):
        s, _ = scores_of(f["qx"], f["kx"], mask, allowed)
        top = jnp.max(s, axis=0, keepdims=True)
        e = jnp.exp(s - top)
        total = jnp.sum(e, axis=0, keepdims=True)
        prob = (e * (1.0 / total)).astype(BF16)
        att.append(dot(vt[head_rows(h)], prob))
        lse_ref[h : h + 1, :] = top + jnp.log(total)
    att = jnp.concatenate(att, axis=0).T
    att_ref[...] = att
    mixed_ref[0] = fold(att * f["g"] * live).astype(BF16)


def attn_bwd_kernel(
    lens_ref, spots_ref, gains_ref, wide_ref, backs_ref, w_ref, att_ref, lse_ref, dm_ref, sig_ref, *refs
):
    kept = KEPT + KEPT_LOW
    f = {name: ref[...] for name, ref in zip(kept, refs)}
    dp_ref, sums_ref, near_ref, far_ref = refs[len(kept) :]
    bucket = pl.program_id(0)
    rows = att_ref.shape[0]
    allowed, live, same_prev = places_of(lens_ref, bucket, rows)
    masks = head_masks(rows)
    same_head = wide_ref[0:BLOCK]
    q_gain, k_gain = gains_ref[0:1, 0:BLOCK], gains_ref[1:2, 0:BLOCK]
    dm = unfold(dm_ref[0].astype(F32)) * live
    g, vb = f["g"], f["vb"]
    dab = (dm * g).astype(BF16)
    dog = dm * att_ref[...] * g * (1.0 - g)
    kt = f["kx"][:, :BLOCK].astype(F32).T.astype(BF16)
    zero = jnp.zeros((rows, BLOCK), BF16)
    dkx = jnp.zeros((rows, SPAN), F32)
    dvb = jnp.zeros((rows, BLOCK), F32)
    tail = jnp.zeros((TAIL, rows), F32)
    dqt = []
    for h in range(OWN):
        s, qh = scores_of(f["qx"], f["kx"], masks[h], allowed)
        p = jnp.exp(s - lse_ref[h : h + 1, :])
        dab_h = jnp.where(masks[h][:, :BLOCK], dab, zero)
        dvb = dvb + dot(p.astype(BF16), dab_h)
        dp = dot(vb, dab_h, ((1,), (1,)))
        ds = p * (dp - jnp.sum(p * dp, axis=0, keepdims=True))
        dsb = ds.astype(BF16)
        dqt.append(dot(kt[head_rows(h)], dsb))
        dkx = dkx + dot(dsb, qh)
        along = jnp.sum(dsb.astype(F32), axis=0, keepdims=True)
        tail = jnp.where(iota((TAIL, rows), 0) == tail_lane(h, TERMS), along, tail)
    dqx = jnp.concatenate(dqt + [tail], axis=0).T
    dqb = dqx[:, :BLOCK] * HEAD_DIM**-0.5
    dkb = dkx[:, :BLOCK]

    def back(n, r, e):
        return r * (e - n * (dot_split(e * n, same_head, 2) * (1.0 / HEAD_DIM)))

    dq = back(f["qn"], f["rq"], dqb * q_gain)
    dks = back(f["kn"], f["rk"], dkb * k_gain)
    last = iota((rows, 1), 0) == rows - 1

    def mix_back(grad, rate, cur, prev):
        ahead = pltpu.roll(rate * grad * same_prev, rows - 1, 0)
        return (1.0 - rate) * grad + jnp.where(last, 0.0, ahead), grad * (prev - cur)

    dk, dak = mix_back(dks, f["ak"], f["k"], shifted(f["k"], same_prev))
    dv, dav = mix_back(dvb, f["av"], f["v"], shifted(f["v"], same_prev))

    onward = (iota((rows, rows), 1) >= iota((rows, rows), 0)).astype(BF16)
    keep = sum(dot(onward, term) for term in split(dqx[:, BLOCK:] - dkx[:, BLOCK:], TERMS))
    sig = sig_ref[...]
    drate = (
        dot_split(dak, backs_ref[0:BLOCK], 2)
        + dot_split(dav, backs_ref[BLOCK : 2 * BLOCK], 2)
        + dot_split(keep, backs_ref[2 * BLOCK :], 2)
    )
    lane = iota((rows, EXTRA), 1)
    drate = drate * (1.0 - sig) * jnp.where(lane < OWN, 1.0, sig)
    drate = jnp.where(lane < RATES, drate, 0.0)
    grads = jnp.concatenate([dq, dk, dv, dog, drate], axis=1).astype(BF16)
    dp_ref[...] = grads
    dh1 = dot(grads, w_ref[...], ((1,), (1,))).astype(BF16)

    @pl.when(bucket < 4)
    def _():
        near_ref[...] = dh1

    @pl.when(bucket >= 4)
    def _():
        far_ref[...] = dh1

    @pl.when(bucket == 0)
    def _():
        sums_ref[...] = jnp.zeros_like(sums_ref)

    sums_ref[0:1, 0:BLOCK] += jnp.sum(dqb * f["qn"], axis=0, keepdims=True)
    sums_ref[1:2, 0:BLOCK] += jnp.sum(dkb * f["kn"], axis=0, keepdims=True)
    sums_ref[2:3, 0:EXTRA] += jnp.sum(drate, axis=0, keepdims=True)


def rows_spec(rows, width):
    return pl.BlockSpec((rows, width), lambda i, lens, spots: (i, 0))


def whole_spec(dims):
    return pl.BlockSpec(dims, lambda i, lens, spots: (0,) * len(dims))


def spot_spec(rows):
    return pl.BlockSpec((1, rows * 3 // 2, EXTRA), lambda i, lens, spots: (spots[i], 0, 0))


def kept_specs(rows):
    return [rows_spec(rows, BLOCK) for _ in KEPT] + [rows_spec(rows, c) for c in (SPAN, SPAN, BLOCK)]


def attn_fwd(lens, spots, near, far, w, bias, wide, tails):
    buckets = lens.shape[0]
    width = near.shape[1]
    total = 2 * near.shape[0]
    rows = total // buckets
    return pl.pallas_call(
        attn_fwd_kernel,
        grid_spec=pltpu.PrefetchScalarGridSpec(
            num_scalar_prefetch=2,
            grid=(buckets,),
            in_specs=[
                near_spec(rows, width),
                far_spec(rows, width),
                whole_spec(w.shape),
                whole_spec(bias.shape),
                whole_spec(wide.shape),
                whole_spec(tails.shape),
            ],
            out_specs=[
                rows_spec(rows, width),
                spot_spec(rows),
                rows_spec(rows, BLOCK),
                rows_spec(8, rows),
                whole_spec((8, width)),
                whole_spec((8, 2 * EXTRA)),
                rows_spec(rows, EXTRA),
            ]
            + kept_specs(rows),
        ),
        out_shape=[
            shape((total, width), BF16),
            shape((buckets, rows * 3 // 2, EXTRA), BF16),
            shape((total, BLOCK), F32),
            shape((8 * buckets, rows), F32),
            shape((8, width), F32),
            shape((8, 2 * EXTRA), F32),
            shape((total, EXTRA), F32),
        ]
        + [shape((total, BLOCK), F32) for _ in KEPT]
        + [shape((total, c), BF16) for c in (SPAN, SPAN, BLOCK)],
        **settings(20, 60),
        name="attn_fwd",
    )(lens, spots, near, far, w, bias, wide, tails)


def near_spec(rows, width):
    return pl.BlockSpec((rows, width), lambda i, lens, spots: (jnp.minimum(i, 3), 0))


def far_spec(rows, width):
    return pl.BlockSpec((rows, width), lambda i, lens, spots: (jnp.maximum(i - 4, 0), 0))


def attn_bwd(lens, spots, gains, wide, backs, w, att, lse, dm, sig, *kept):
    buckets = lens.shape[0]
    total = att.shape[0]
    width = w.shape[0]
    rows = total // buckets
    return pl.pallas_call(
        attn_bwd_kernel,
        grid_spec=pltpu.PrefetchScalarGridSpec(
            num_scalar_prefetch=2,
            grid=(buckets,),
            in_specs=[whole_spec(x.shape) for x in (gains, wide, backs, w)]
            + [rows_spec(rows, BLOCK), rows_spec(8, rows), spot_spec(rows), rows_spec(rows, EXTRA)]
            + kept_specs(rows),
            out_specs=[
                rows_spec(rows, WIDE),
                whole_spec((8, 2 * EXTRA)),
                near_spec(rows, width),
                far_spec(rows, width),
            ],
        ),
        out_shape=[shape((total, WIDE), BF16), shape((8, 2 * EXTRA), F32)]
        + [shape((total // 2, width), BF16)] * 2,
        **settings(24, 60),
        name="attn_bwd",
    )(lens, spots, gains, wide, backs, w, att, lse, dm, sig, *kept)


def mid_fwd_kernel(spots_ref, got_ref, tok_ref, gain_ref, *refs):
    x2_ref, h2_ref = refs[TP:]
    acc = tok_ref[...].astype(F32)
    for i in range(TP):
        acc = acc + dot(unfold(got_ref[spots_ref[i]]), refs[i][...])
    x2_ref[...] = acc
    h2_ref[...] = (normed(acc)[0] * gain_ref[...]).astype(BF16)


def once(dims):
    return pl.BlockSpec(dims, lambda i: (0,) * len(dims))


def mix_specs(w):
    return [once((BLOCK, x.shape[1])) for x in w]


def mid_fwd(spots, got, w, tok, gain):
    rows, width = tok.shape
    return pl.pallas_call(
        mid_fwd_kernel,
        grid=(1,),
        in_specs=[SMEM, once(got.shape), once(tok.shape), once(gain.shape)] + mix_specs(w),
        out_specs=[once(tok.shape)] * 2,
        out_shape=[shape(tok.shape, F32), shape(tok.shape, BF16)],
        **settings(5, 40),
        name="mid_fwd",
    )(spots, got, tok, gain, *w)


def mid_bwd_kernel(spots_ref, a_ref, b_ref, c_ref, d_ref, x2_ref, cot_ref, gain_ref, got_ref, *refs):
    dx2_ref, dm_ref, near_ref, far_ref = refs[TP:]
    dh2 = a_ref[...] + b_ref[...].astype(F32) + c_ref[...].astype(F32) + d_ref[...].astype(F32)
    n2, r2 = normed(x2_ref[...])
    dx2 = cot_ref[...].astype(F32) + norm_back(n2, r2, dh2 * gain_ref[...])
    dx2_ref[...] = dx2
    dxb = dx2.astype(BF16)
    for i in range(TP):
        dm = dot(dxb, refs[i][...], ((1,), (1,)))
        dm_ref[spots_ref[i]] = fold(dm).astype(BF16)
        out_ref = near_ref if i < 4 else far_ref
        piece = dot(unfold(got_ref[spots_ref[i]]), dxb, ((0,), (0,)))
        out_ref[(i % 4) * BLOCK : (i % 4 + 1) * BLOCK, :] = piece.astype(BF16)


def mid_bwd(spots, parts, x2, cot, gain, got, w):
    rows, width = x2.shape
    arrays = (*parts, x2, cot, gain, got)
    outs = [
        shape((rows, width), F32),
        shape((TP, rows * 3 // 2, EXTRA), BF16),
        shape((4 * BLOCK, width), BF16),
        shape((4 * BLOCK, width), BF16),
    ]
    return pl.pallas_call(
        mid_bwd_kernel,
        grid=(1,),
        in_specs=[SMEM] + [once(x.shape) for x in arrays] + mix_specs(w),
        out_specs=[once(x.shape) for x in outs],
        out_shape=outs,
        **settings(9, 48),
        name="mid_bwd",
    )(spots, *arrays, *w)


def last_norm(tok, gain, dx2, *parts):
    rows, width = tok.shape
    steps = 4

    def kernel(tok_ref, gain_ref, dx2_ref, *refs):
        n1, r1 = normed(tok_ref[...].astype(F32))
        refs[-1][...] = dx2_ref[...] + norm_back(n1, r1, total_of([x[...] for x in refs[:-1]]) * gain_ref[...])

    block = pl.BlockSpec((rows // steps, width), lambda i: (i, 0))
    return pl.pallas_call(
        kernel,
        grid=(steps,),
        in_specs=[block, once(gain.shape), block] + [block] * len(parts),
        out_specs=block,
        out_shape=shape((rows, width), F32),
        **settings(3, 24),
        name="last_norm",
    )(tok, gain, dx2, *parts)


def ffn_kernel(lens_ref, h2_ref, cot_ref, gu_ref, dn_ref, ab_ref, dgu_ref, *out_refs):
    rows, ff = h2_ref.shape[0], dn_ref.shape[0]
    total = jnp.int32(0)
    for j in range(lens_ref.shape[1]):
        total = total + lens_ref[pl.program_id(0), j]
    live = (iota((rows, 1), 0) < total).astype(F32)
    gu = dot(h2_ref[...], gu_ref[...])
    da = dot(cot_ref[...], dn_ref[...], ((1,), (1,))) * live
    gate, up = gu[:, :ff], gu[:, ff:]
    sg = jax.nn.sigmoid(gate)
    act = gate * sg
    ab = (act * up * live).astype(BF16)
    dgate = (da * up * sg * (1.0 + gate * (1.0 - sg))).astype(BF16)
    dup = (da * act).astype(BF16)
    ab_ref[...] = ab
    dgu_ref[:, :ff] = dgate
    dgu_ref[:, ff:] = dup
    dh2 = dot(dgate, gu_ref[:, :ff], ((1,), (1,))) + dot(dup, gu_ref[:, ff:], ((1,), (1,)))
    dh2 = dh2.astype(BF16)
    out = dot(ab, dn_ref[...]).astype(BF16)
    near = pl.program_id(0) < pl.num_programs(0) // 2

    @pl.when(near)
    def _():
        out_refs[0][...] = out
        out_refs[1][...] = dh2

    @pl.when(jnp.logical_not(near))
    def _():
        out_refs[2][...] = out
        out_refs[3][...] = dh2


def ffn(lens, h2, cot, gu, dn):
    buckets = lens.shape[0]
    half = buckets // 2
    total, width = h2.shape
    rows = total // buckets
    ff = dn.shape[0]

    def block(columns):
        return pl.BlockSpec((rows, columns), lambda i: (i, 0))

    def whole(dims):
        return pl.BlockSpec(dims, lambda i: (0, 0))

    near = pl.BlockSpec((rows, width), lambda i: (jnp.minimum(i, half - 1), 0))
    far = pl.BlockSpec((rows, width), lambda i: (jnp.maximum(i - half, 0), 0))
    return pl.pallas_call(
        ffn_kernel,
        grid=(buckets,),
        in_specs=[SMEM, block(width), block(width), whole(gu.shape), whole(dn.shape)],
        out_specs=[block(ff), block(2 * ff), near, near, far, far],
        out_shape=[shape((total, ff), BF16), shape((total, 2 * ff), BF16)] + [shape((total // 2, width), BF16)] * 4,
        **settings(4 * buckets, 40),
        name="ffn",
    )(lens, h2, cot, gu, dn)


def sum_of_dots(lefts, rights):
    return sum(dot(x[...], y[...], ((0,), (0,))) for x, y in zip(lefts, rights))


def grad_down(ab, cot):
    ff, width = ab[0].shape[1], cot[0].shape[1]
    steps = 4
    columns = width // steps
    count = len(ab)

    def kernel(*refs):
        refs[-1][...] = sum_of_dots(refs[:count], refs[count : 2 * count]).astype(BF16)

    return pl.pallas_call(
        kernel,
        grid=(steps,),
        in_specs=[pl.BlockSpec(x.shape, lambda i: (0, 0)) for x in ab]
        + [pl.BlockSpec((x.shape[0], columns), lambda i: (0, i)) for x in cot],
        out_specs=pl.BlockSpec((ff, columns), lambda i: (0, i)),
        out_shape=shape((ff, width), BF16),
        **settings(6, 60),
        name="grad_down",
    )(*ab, *cot)


def grad_gu(h2, dgu, share):
    width = h2[0].shape[1]
    own_rows = width // (TP * share)
    columns = dgu[0].shape[1]
    steps = TP // 2
    count = len(h2)

    def kernel(*refs):
        res = sum_of_dots(refs[:count], refs[count : 2 * count])
        for k in range(2):
            for z in range(share):
                at = (k * share + z) * own_rows
                refs[-1][z, k] = res[at : at + own_rows].astype(BF16)

    return pl.pallas_call(
        kernel,
        grid=(steps,),
        in_specs=[pl.BlockSpec((x.shape[0], width // steps), lambda i: (0, i)) for x in h2]
        + [pl.BlockSpec(x.shape, lambda i: (0, 0)) for x in dgu],
        out_specs=pl.BlockSpec((share, 2, own_rows, columns), lambda i: (0, i, 0, 0)),
        out_shape=shape((share, TP, own_rows, columns), BF16),
        **settings(11, 60),
        name="grad_gu",
    )(*h2, *dgu)


def grad_in(place, sums, left, right, share):
    own_rows = left.shape[1] // (TP * share)
    columns = right.shape[1]
    steps = TP // 2

    def kernel(place_ref, sums_ref, left_ref, right_ref, out_ref):
        res = dot(left_ref[...], right_ref[...], ((0,), (0,)))
        lane, row = iota((BLOCK, EXTRA), 1), iota((BLOCK, EXTRA), 0)
        turned = sums_ref[...].T[0:BLOCK]
        bias = jnp.where((lane == row % own_rows) & (lane < RATES), sums_ref[2:3, 0:EXTRA], 0.0)
        bias = jnp.sum(bias, axis=1, keepdims=True)
        for k in range(2):
            mine = (pl.program_id(0) * 2 + k == place_ref[0]).astype(F32)
            extra = res[k * BLOCK : (k + 1) * BLOCK, CORE:WIDE]
            extra = jnp.where(lane == RATES, turned[:, 0:1] * mine, extra)
            extra = jnp.where(lane == RATES + 1, turned[:, 1:2] * mine, extra)
            extra = jnp.where(lane == RATES + 2, bias, extra)
            for z in range(share):
                at = z * own_rows
                rest = k * BLOCK + at
                out_ref[z, k, :, :CORE] = res[rest : rest + own_rows, :CORE].astype(BF16)
                out_ref[z, k, :, CORE:] = extra[at : at + own_rows].astype(BF16)

    return pl.pallas_call(
        kernel,
        grid=(steps,),
        in_specs=[
            SMEM,
            pl.BlockSpec(sums.shape, lambda i: (0, 0)),
            pl.BlockSpec((left.shape[0], left.shape[1] // steps), lambda i: (0, i)),
            pl.BlockSpec(right.shape, lambda i: (0, 0)),
        ],
        out_specs=pl.BlockSpec((share, 2, own_rows, columns), lambda i: (0, i, 0, 0)),
        out_shape=shape((share, TP, own_rows, columns), BF16),
        **settings(11, 60),
        name="grad_in",
    )(place, sums, left, right)


def own_share(part):
    columns = part.shape[-1]
    summed = lax.psum_scatter(part.reshape(-1, columns), "sh", scatter_dimension=0, tiled=True)
    return summed.reshape(TP, -1, columns)


def swap(blocks):
    return lax.all_to_all(blocks, "tp", 0, 0, tiled=True)


def body(
    tokens,
    doc_lengths,
    norm_gain,
    w_attn_in,
    w_rates,
    rate_bias,
    q_gain,
    k_gain,
    w_out,
    ffn_gain,
    w_gate_up,
    w_down,
    cotangent,
):
    place = lax.axis_index("tp")
    share = lax.axis_size("sh")
    width = tokens.shape[1]
    own_rows = w_attn_in.shape[0]
    spots = place ^ jnp.array(OFFSETS, jnp.int32)

    gains = jnp.stack([norm_gain, q_gain, k_gain, ffn_gain])
    packed, w_mix = phase(pack_in(doc_lengths, w_attn_in, w_rates, gains), w_out)
    got_in = swap(packed)
    w_in = lax.all_gather(got_in, "sh", axis=1).reshape(width, WIDE)
    lens_all = got_in[:, 0, CORE + LENS_AT : CORE + LENS_AT + doc_lengths.shape[0]].astype(jnp.int32)
    lens = lens_all[spots]
    bias = lax.dynamic_index_in_dim(rate_bias.reshape(3, TP, OWN), place, 1, False).reshape(1, RATES)
    bias = jnp.pad(bias, ((0, 7), (0, EXTRA - RATES)))

    tok, w_gu, w_mix, _ = phase(tokens, w_gate_up, w_mix, got_in)
    two_four, w_mix = phase(sides(tok), gather_shares(w_mix))
    tok = join_rows(tok, *two_four, *diagonal(*two_four))
    tok, packed = phase(tok, pack_gu(w_gu))
    joined = join_ffn(swap(packed), w_down)
    far = flip(tok, 1)
    w_gu, w_dn = open_ffn(lax.all_gather(joined, "sh", axis=0), w_down.shape[0], width)

    wide, tails, backs = constants()
    beside = phase(join_rows(in_order(w_mix), cotangent), joined)[0]
    two_four = sides(beside)
    h1, mixed, att, lse, gains, gain_heads, *kept = attn_fwd(lens, spots, tok, far, w_in, bias, wide, tails)
    gain_one, gain_two = gains[0:1], gains[3:4]
    mixed, two_four = phase(mixed, two_four)
    near = [beside, *two_four]
    got_mixed, mix_six, far = phase(
        swap(mixed), diagonal(*[x[:BLOCK] for x in two_four]), [flip(x, 1) for x in near]
    )
    mix_six = jnp.concatenate(mix_six, axis=0)
    w_mix = [*near, mix_six, *far, flip(mix_six, 1)]
    x2, h2 = mid_fwd(spots, got_mixed, w_mix, tokens, gain_two)

    orders = (2, 4, 3, 5), (0, 1), (6, 7)
    lens_of = [jnp.stack([lens[OFFSETS.index(d)] for d in order]) for order in orders]
    h2, near, far = phase(h2, near, far)
    cot = [
        join_rows(*[(half[i], BLOCK) for half in (near, far) for i in (1, 2)]),
        join_rows((near[0], BLOCK), (far[0], BLOCK)),
    ]
    (two, four), one, cot = phase(sides(h2), flip(h2, 1), cot)
    six = diagonal(two, four)
    two, four, three, five, one = phase(two, four, flip(two, 1), flip(four, 1), one)
    h2 = [join_rows(two, four, three, five), join_rows(h2, one)]
    found = [ffn(lens_of[0], h2[0], cot[0], w_gu, w_dn)]
    found, six, h2[1], cot_six = phase(found, six, h2[1], diagonal(*[x[BLOCK:] for x in near[1:3]]))
    six, cot_six = [jnp.concatenate(x, axis=0) for x in (six, cot_six)]
    seven, cot_seven, far, more = phase(
        flip(six, 1),
        flip(cot_six, 1),
        [flip(x, 1) for x in found[0][4:]],
        ffn(lens_of[1], h2[1], cot[1], w_gu, w_dn),
    )
    found.append(more)
    layer_side, side = [[x.astype(BF16) for x in two_sums(*pair)] for pair in zip(found[0][2:4], far)]
    h2.append(join_rows(six, seven))
    cot.append(join_rows(cot_six, cot_seven))
    side, layer_side, h2[2], cot[2], one = phase(side, layer_side, h2[2], cot[2], found[1][5])
    side = flip(side[0], 2), flip(side[1], 4)
    one, more = phase(flip(one, 1), ffn(lens_of[2], h2[2], cot[2], w_gu, w_dn))
    found.append(more)
    ab, dgu, out_near, dh2_near, out_far, dh2_far = zip(*found)
    seven, dw_gu, side = phase(flip(dh2_far[2], 1), grad_gu(h2, dgu, share), side)
    dw_gu = own_share(dw_gu)
    low = (dh2_near[2].astype(F32) + seven.astype(F32)).astype(BF16)
    low, ab, out_far = phase(low, ab, out_far)
    own = dh2_near[1].astype(F32) + one.astype(F32)
    six, dw_dn, out_far, own = phase(flip(low, 6), grad_down(ab, cot), [flip(x, 1) for x in out_far[1:]], own)
    dw_dn = lax.psum_scatter(dw_dn, "sh", scatter_dimension=0, tiled=True)
    layer_six = (out_near[2].astype(F32) + out_far[1].astype(F32)).astype(BF16)
    dh2, layer_low = phase((own, *side, six), (*layer_side, layer_six))

    found, layer_low = phase(
        mid_bwd(spots, dh2, x2, cotangent, gain_two, got_mixed, w_mix), relay_six(layer_low)
    )
    dx2, dm, mix_near, mix_far = found
    mix_own, mix_low = both_cores(quarters(mix_near), quarters(flip(mix_far, 1)))
    got_dm, mix_own, mix_low, layer_low = phase(swap(dm), mix_own, mix_low, add_six(layer_low))
    layer, mix_low, found, dw_gu = phase(
        (flip(layer_low[0], 2), flip(layer_low[1], 4)),
        relay_six(mix_low),
        attn_bwd(lens, spots, gain_heads, wide, backs, w_in, att, lse, got_dm, *kept),
        dw_gu,
    )
    dp, sums, dh1_near, dh1_far = found

    mix_low = add_six(mix_low)
    mix = flip(mix_low[0], 2), flip(mix_low[1], 4)
    dh1_far, dw_in, got_gu, dw_dn = phase(
        flip(dh1_far, 1), grad_in(place.reshape(1), sums, h1, dp, share), swap(dw_gu), dw_dn
    )
    dw_in = own_share(dw_in)
    dh1_own, dh1_low = both_cores(quarters(dh1_near), quarters(dh1_far))
    layer_own = out_near[1].astype(F32) + out_far[0].astype(F32)
    layer_out = (x2 + total_of((layer_own, *layer))).astype(BF16)
    dh1, mix, dw_in, layer_out = phase(send(dh1_low), mix, dw_in, layer_out)
    mix = to_shares(total_of((mix_own, *mix)).astype(BF16))
    d_tokens = last_norm(tokens, gain_one, dx2, dh1_own, *dh1)

    d_w_attn_in, d_w_rates, small = unpack_in(swap(dw_in), w_attn_in, w_rates, norm_gain)
    d_w_gate_up, small_gu = unpack_gu(got_gu, w_gate_up, ffn_gain)
    d_ffn_gain = small_gu[0, :own_rows]
    small, mix = phase(small, mix)
    d_w_out = total_of(mix)
    return (
        layer_out,
        d_tokens,
        small[0, :own_rows],
        d_w_attn_in,
        d_w_rates,
        small[3, : w_rates.shape[1]],
        small[1, :own_rows],
        small[2, :own_rows],
        d_w_out,
        d_ffn_gain,
        d_w_gate_up,
        dw_dn.astype(F32),
    )


def solution(mesh):
    devices = mesh.devices.reshape(TP, -1)
    grid = Mesh(devices, ("tp", "sh"))
    rows = P(("tp", "sh"), None)
    flat = P(("tp", "sh"))
    in_specs = (rows, flat, flat, rows, rows, P(), flat, flat, rows, flat, rows, rows, rows)
    out_specs = (rows, rows, flat, rows, rows, P(), flat, flat, rows, flat, rows, rows)
    return jax.shard_map(body, mesh=grid, in_specs=in_specs, out_specs=out_specs, check_vma=False)
```

```python
import jax
import jax.numpy as jnp
import numpy as np
from jax import lax
from jax.experimental import pallas as pl
from jax.experimental.pallas import tpu as pltpu
from jax.sharding import Mesh
from jax.sharding import PartitionSpec as P

HEADS = 24
HEAD_DIM = 64
EPS = 1e-06
NEG = -1e30
TP = 8
OWN = HEADS // TP
BLOCK = OWN * HEAD_DIM
CORE = 4 * BLOCK
EXTRA = 128
WIDE = CORE + EXTRA
RATES = 3 * OWN
GAIN_AT = RATES
LENS_AT = RATES + 4
OFFSETS = (0, 2, 4, 6, 1, 3, 5, 7)
F32 = jnp.float32
BF16 = jnp.bfloat16


def flip(array, offset):
    return lax.ppermute(array, "tp", [(i, i ^ offset) for i in range(TP)])


def sides(own):
    return flip(own, 2), flip(own, 4)


def diagonal(two, four):
    cut = two.shape[0] // 2
    return flip(two[:cut], 4), flip(four[cut:], 2)


def others(own):
    return [flip(own, d) for d in (2, 4, 6)]


def both_cores(near, far):
    sums = [x.astype(F32) + y.astype(F32) for x, y in zip(near, far)]
    return sums[0], [x.astype(BF16) for x in sums[1:]]


def two_sums(near, far):
    rows = near.shape[0] // 2
    return [near[i : i + rows].astype(F32) + far[i : i + rows].astype(F32) for i in (0, rows)]


def quarters(array):
    rows = array.shape[0] // 4
    return [array[i * rows : (i + 1) * rows] for i in range(4)]


def send(blocks):
    return [flip(x, d) for x, d in zip(blocks, (2, 4, 6))]


def relay_six(blocks):
    two, four, six = blocks
    cut = six.shape[0] // 2
    return two, four, flip(six[:cut], 2), flip(six[cut:], 4)


def add_six(blocks):
    two, four, over_two, over_four = blocks
    cut = over_two.shape[0]
    two = jnp.concatenate([two[:cut], (two[cut:].astype(F32) + over_four.astype(F32)).astype(BF16)], axis=0)
    four = jnp.concatenate([(four[:cut].astype(F32) + over_two.astype(F32)).astype(BF16), four[cut:]], axis=0)
    return two, four


def gather_shares(own):
    share = lax.axis_size("sh")
    return [own] + [lax.ppermute(own, "sh", [(i, (i + k) % share) for i in range(share)]) for k in range(1, share)]


def in_order(pieces):
    here = lax.axis_index("sh")
    share = len(pieces)
    out = jnp.zeros((share,) + pieces[0].shape, pieces[0].dtype)
    for k, piece in enumerate(pieces):
        out = lax.dynamic_update_index_in_dim(out, piece, (here - k) % share, 0)
    return out.reshape((-1,) + pieces[0].shape[1:])


def to_shares(part):
    share = lax.axis_size("sh")
    here = lax.axis_index("sh")
    blocks = part.reshape(share, -1, part.shape[1])
    picked = [lax.dynamic_index_in_dim(blocks, (here + k) % share, 0, False) for k in range(share)]
    return picked[:1] + [
        lax.ppermute(picked[k], "sh", [(i, (i + k) % share) for i in range(share)]) for k in range(1, share)
    ]


def total_of(parts):
    return sum(term.astype(F32) for term in parts)


def phase(*values):
    return lax.optimization_barrier(values)


def normed(field_in):
    factor = lax.rsqrt(jnp.mean(field_in * field_in, axis=-1, keepdims=True) + EPS)
    return field_in * factor, factor


def norm_back(normal, factor, grad_in):
    return factor * (grad_in - normal * jnp.mean(grad_in * normal, axis=-1, keepdims=True))


def dot(a, b, dims=((1,), (0,)), precision=None):
    return lax.dot_general(a, b, (dims, ((), ())), precision=precision, preferred_element_type=F32)


def iota(shape, dim):
    return lax.broadcasted_iota(jnp.int32, shape, dim)


def settings(us, mib):
    cost = pl.CostEstimate(flops=int(us * 1e7), bytes_accessed=int(us * 1e4), transcendentals=0)
    return dict(compiler_params=pltpu.CompilerParams(vmem_limit_bytes=mib * 2**20), cost_estimate=cost)


SMEM = pl.BlockSpec(memory_space=pltpu.SMEM)
VMEM = pl.BlockSpec(memory_space=pltpu.VMEM)


def shape(dims, dtype):
    return jax.ShapeDtypeStruct(dims, dtype)


def rate_picks(t, rows, columns, flipped=False):
    whole, own = iota((rows, columns), 1 if flipped else 0), iota((rows, columns), 0 if flipped else 1)
    kind, head = own // OWN, own % OWN
    return ((own < RATES) & (whole == kind * HEADS + t * OWN + head)).astype(BF16)


def pack_in_kernel(lens_ref, w_ref, rates_ref, gains_ref, out_ref):
    rows, width = w_ref.shape[0], w_ref.shape[1] // 4
    picks = (iota((4, EXTRA), 1) == GAIN_AT + iota((4, EXTRA), 0)).astype(BF16)
    beside = dot(gains_ref[...], picks, ((0,), (0,)))
    lane, row = iota((rows, EXTRA), 1), iota((rows, EXTRA), 0)
    for j in range(lens_ref.shape[0]):
        beside = jnp.where((lane == LENS_AT + j) & (row == 0), lens_ref[j].astype(F32), beside)
    for t in range(TP):
        for b in range(4):
            at = b * width + t * BLOCK
            out_ref[t, :, b * BLOCK : (b + 1) * BLOCK] = w_ref[:, at : at + BLOCK]
        rates = dot(rates_ref[...], rate_picks(t, rates_ref.shape[1], EXTRA))
        out_ref[t, :, CORE:WIDE] = (rates + beside).astype(BF16)


def pack_in(lens, w, rates, gains):
    return pl.pallas_call(
        pack_in_kernel,
        in_specs=[SMEM, VMEM, VMEM, VMEM],
        out_specs=VMEM,
        out_shape=shape((TP, w.shape[0], WIDE), BF16),
        **settings(3, 16),
        name="pack_in",
    )(lens, w, rates, gains)


def pack_gu_kernel(w_ref, out_ref):
    ff = w_ref.shape[1] // 2
    own = ff // TP
    for t in range(TP):
        out_ref[t, :, :own] = w_ref[:, t * own : (t + 1) * own]
        out_ref[t, :, own:] = w_ref[:, ff + t * own : ff + (t + 1) * own]


def pack_gu(w):
    return pl.pallas_call(
        pack_gu_kernel,
        in_specs=[VMEM],
        out_specs=VMEM,
        out_shape=shape((TP, w.shape[0], w.shape[1] // TP), BF16),
        **settings(2, 16),
        name="pack_gu",
    )(w)


def join_ffn(got, down):
    columns = got.shape[2]
    top, rows = got.shape[0] * got.shape[1], down.shape[0]
    half = rows // 2

    def kernel(got_ref, down_ref, out_ref):
        for t in range(TP):
            out_ref[t * got.shape[1] : (t + 1) * got.shape[1], :] = got_ref[t]
        out_ref[top : top + rows, :] = down_ref[:, :columns]
        out_ref[top + rows :, : columns // 2] = down_ref[:half, columns:]
        out_ref[top + rows :, columns // 2 :] = down_ref[half:, columns:]

    return pl.pallas_call(
        kernel,
        in_specs=[VMEM, VMEM],
        out_specs=VMEM,
        out_shape=shape((top + rows + half, columns), BF16),
        **settings(2, 16),
        name="join_ffn",
    )(got, down)


def open_ffn(joined, down_rows, width):
    share, _, columns = joined.shape
    own_rows = width // (TP * share)
    top = TP * own_rows
    half = down_rows // 2

    def kernel(in_ref, gu_ref, down_ref):
        for z in range(share):
            for t in range(TP):
                at = (t * share + z) * own_rows
                gu_ref[at : at + own_rows, :] = in_ref[z, t * own_rows : (t + 1) * own_rows, :]
            at = z * down_rows
            down_ref[at : at + down_rows, :columns] = in_ref[z, top : top + down_rows, :]
            down_ref[at : at + half, columns:] = in_ref[z, top + down_rows :, : columns // 2]
            down_ref[at + half : at + down_rows, columns:] = in_ref[z, top + down_rows :, columns // 2 :]

    return pl.pallas_call(
        kernel,
        in_specs=[VMEM],
        out_specs=[VMEM, VMEM],
        out_shape=[shape((width, columns), BF16), shape((share * down_rows, width), BF16)],
        **settings(4, 16),
        name="open_ffn",
    )(joined)


def join_rows(*pieces):
    pieces = [x if isinstance(x, tuple) else (x, 0) for x in pieces]
    total = sum(x.shape[0] - first for x, first in pieces)

    def kernel(*refs):
        at = 0
        for ref, (x, first) in zip(refs, pieces):
            more = x.shape[0] - first
            refs[-1][at : at + more, :] = ref[first:, :]
            at += more

    return pl.pallas_call(
        kernel,
        in_specs=[VMEM] * len(pieces),
        out_specs=VMEM,
        out_shape=shape((total, pieces[0][0].shape[1]), pieces[0][0].dtype),
        **settings(2, 24),
        name="join_rows",
    )(*[x for x, _ in pieces])


def unpack_in_kernel(got_ref, w_ref, rates_ref, gain_ref, dw_ref, drates_ref, small_ref):
    rows, width = w_ref.shape[0], w_ref.shape[1] // 4
    along = jnp.zeros((rows, 1), F32)
    drates = jnp.zeros((rows, EXTRA), F32)
    sums = jnp.zeros((rows, EXTRA), F32)
    bias = jnp.zeros((rows, EXTRA), F32)
    lane, row = iota((rows, EXTRA), 1), iota((rows, EXTRA), 0)
    for t in range(TP):
        for b in range(4):
            at = b * width + t * BLOCK
            piece = got_ref[t, :, b * BLOCK : (b + 1) * BLOCK].astype(F32)
            dw_ref[:, at : at + BLOCK] = piece
            along = along + jnp.sum(piece * w_ref[:, at : at + BLOCK].astype(F32), axis=1, keepdims=True)
        extra = got_ref[t, :, CORE:WIDE]
        drates = drates + dot(extra, rate_picks(t, EXTRA, EXTRA, True))
        extra = extra.astype(F32)
        sums = sums + extra
        spot = (row // OWN) * HEADS + t * OWN + row % OWN
        bias = bias + jnp.where((lane == spot) & (row < RATES), extra[:, RATES + 2 : RATES + 3], 0.0)
    columns = rates_ref.shape[1]
    drates_ref[...] = drates[:, :columns]
    along = along + jnp.sum(drates[:, :columns] * rates_ref[...].astype(F32), axis=1, keepdims=True)
    turned = jnp.where(lane == 0, along, 0.0) + jnp.where(lane == 1, sums[:, RATES : RATES + 1], 0.0)
    turned = turned + jnp.where(lane == 2, sums[:, RATES + 1 : RATES + 2], 0.0)
    pick = (iota((rows, EXTRA), 0) == iota((rows, EXTRA), 1)).astype(F32)
    turned = dot(turned, pick, ((0,), (0,)), lax.Precision.HIGHEST)
    small_ref[0:1, :] = turned[0:1, :] / gain_ref[...]
    small_ref[1:3, :] = turned[1:3, :]
    small_ref[3:4, :] = jnp.sum(bias, axis=0, keepdims=True)
    small_ref[4:8, :] = jnp.zeros((4, EXTRA), F32)


def unpack_in(got, w, rates, gain):
    rows = w.shape[0]
    gain = jnp.pad(gain.astype(F32)[None], ((0, 0), (0, EXTRA - rows)), constant_values=1.0)
    return pl.pallas_call(
        unpack_in_kernel,
        in_specs=[VMEM] * 4,
        out_specs=[VMEM] * 3,
        out_shape=[shape(w.shape, F32), shape(rates.shape, F32), shape((8, EXTRA), F32)],
        **settings(5, 16),
        name="unpack_in",
    )(got, w, rates, gain)


def unpack_gu_kernel(got_ref, w_ref, gain_ref, dw_ref, small_ref):
    rows, ff = w_ref.shape[0], w_ref.shape[1] // 2
    own = ff // TP
    along = jnp.zeros((rows, 1), F32)
    for t in range(TP):
        for half in range(2):
            at = half * ff + t * own
            piece = got_ref[t, :, half * own : (half + 1) * own].astype(F32)
            dw_ref[:, at : at + own] = piece
            along = along + jnp.sum(piece * w_ref[:, at : at + own].astype(F32), axis=1, keepdims=True)
    lane = iota((rows, EXTRA), 1)
    pick = (iota((rows, EXTRA), 0) == lane).astype(F32)
    turned = dot(jnp.where(lane == 0, along, 0.0), pick, ((0,), (0,)), lax.Precision.HIGHEST)
    small_ref[...] = turned[0:8, :] / gain_ref[...]


def unpack_gu(got, w, gain):
    rows = w.shape[0]
    gain = jnp.pad(gain.astype(F32)[None], ((0, 0), (0, EXTRA - rows)), constant_values=1.0)
    return pl.pallas_call(
        unpack_gu_kernel,
        in_specs=[VMEM] * 3,
        out_specs=[VMEM] * 2,
        out_shape=[shape(w.shape, F32), shape((8, EXTRA), F32)],
        **settings(3, 16),
        name="unpack_gu",
    )(got, w, gain)


def fold(block):
    cut = block.shape[0] // 2
    tail = jnp.concatenate([block[:cut, EXTRA:], block[cut:, EXTRA:]], axis=1)
    return jnp.concatenate([block[:, :EXTRA], tail], axis=0)


def unfold(block):
    rows = 2 * block.shape[0] // 3
    tail = block[rows:]
    tail = jnp.concatenate([tail[:, : BLOCK - EXTRA], tail[:, BLOCK - EXTRA :]], axis=0)
    return jnp.concatenate([block[:rows], tail], axis=1)


def split(field_in, count):
    terms = []
    for _ in range(count):
        terms.append(field_in.astype(BF16))
        field_in = field_in - terms[-1].astype(F32)
    return terms


def dot_split(field_in, picks, count):
    return sum(dot(term, picks) for term in split(field_in, count))


TAIL = 64
SPAN = BLOCK + TAIL
TERMS = 3


def tail_lane(h, term):
    return 8 * h + term


def constants():
    head = np.arange(BLOCK) // HEAD_DIM
    same = head[:, None] == head[None, :]
    extra = np.arange(EXTRA)
    key_lanes = extra[:, None] == OWN + head[None, :]
    value_lanes = extra[:, None] == 2 * OWN + head[None, :]
    to_query = np.zeros((TERMS, EXTRA, TAIL))
    to_key = np.zeros((TERMS, EXTRA, TAIL))
    from_tail = np.zeros((TAIL, EXTRA))
    for h in range(OWN):
        for term in range(TERMS):
            to_query[term, h, tail_lane(h, term)] = 1
            to_key[term, h, tail_lane(h, TERMS + term)] = -1
        from_tail[tail_lane(h, TERMS), h] = 1
    wide = np.concatenate([same, key_lanes, value_lanes], axis=0)
    tails = np.concatenate([to_query.reshape(-1, TAIL), to_key.reshape(-1, TAIL)], axis=0)
    backs = np.concatenate([key_lanes.T, value_lanes.T, from_tail], axis=0)
    return tuple(jnp.asarray(x, BF16) for x in (wide, tails, backs))


def places_of(lens_ref, bucket, rows):
    ends = []
    total = jnp.int32(0)
    for j in range(lens_ref.shape[1]):
        total = total + lens_ref[bucket, j]
        ends.append(total)

    def segment(place):
        seg = jnp.zeros(place.shape, jnp.int32)
        for end in ends:
            seg = seg + (end <= place).astype(jnp.int32)
        return seg

    col = iota((rows, 1), 0)
    row = iota((1, rows), 1)
    seg_col = segment(col)
    allowed = (col <= row) & (segment(row) == seg_col)
    live = (col < total).astype(F32)
    same_prev = ((col > 0) & (seg_col == segment(col - 1))).astype(F32)
    return allowed, live, same_prev


KEPT = ("qn", "kn", "rq", "rk", "ak", "av", "k", "v", "g")
KEPT_LOW = ("qx", "kx", "vb")


def front(proj, bias_ref, gains_ref, wide_ref, tails_ref, same_prev):
    rows = proj.shape[0]
    q = proj[:, 0:BLOCK]
    k = proj[:, BLOCK : 2 * BLOCK]
    v = proj[:, 2 * BLOCK : 3 * BLOCK]
    og = proj[:, 3 * BLOCK : CORE]
    rate = proj[:, CORE:WIDE] + bias_ref[0:1, :]
    sig = jax.nn.sigmoid(rate)
    log_keep = jnp.minimum(rate, 0.0) - jnp.log1p(jnp.exp(-jnp.abs(rate)))
    upto = (iota((rows, rows), 1) <= iota((rows, rows), 0)).astype(BF16)
    decay = sum(dot(upto, term) for term in split(log_keep, TERMS))
    same_head = wide_ref[0:BLOCK]
    ak = dot_split(sig, wide_ref[BLOCK : BLOCK + EXTRA], 2)
    av = dot_split(sig, wide_ref[BLOCK + EXTRA :], 2)
    ks = ak * shifted(k, same_prev) + (1.0 - ak) * k
    vs = av * shifted(v, same_prev) + (1.0 - av) * v

    def head_norm(u):
        factor = lax.rsqrt(dot_split(u * u, same_head, 2) * (1.0 / HEAD_DIM) + EPS)
        return u * factor, factor

    qn, rq = head_norm(q)
    kn, rk = head_norm(ks)
    q_gain, k_gain = gains_ref[0:1, 0:BLOCK], gains_ref[1:2, 0:BLOCK]
    qb = (qn * q_gain).astype(BF16) * jnp.asarray(HEAD_DIM**-0.5, BF16)
    kb = (kn * k_gain).astype(BF16)

    terms = split(decay, TERMS)
    lane = iota((1, TAIL), 1)
    ones_q = ((lane % 8 >= TERMS) & (lane % 8 < 2 * TERMS)).astype(F32)
    ones_k = (lane % 8 < TERMS).astype(F32)
    q_tail = ones_q + sum(dot(terms[t], tails_ref[t * EXTRA : (t + 1) * EXTRA]) for t in range(TERMS))
    k_tail = ones_k + sum(
        dot(terms[t], tails_ref[(TERMS + t) * EXTRA : (TERMS + t + 1) * EXTRA]) for t in range(TERMS)
    )
    qx = jnp.concatenate([qb, q_tail.astype(BF16)], axis=1)
    kx = jnp.concatenate([kb, k_tail.astype(BF16)], axis=1)
    return dict(
        qn=qn, kn=kn, rq=rq, rk=rk, ak=ak, av=av, k=k, v=v, g=jax.nn.sigmoid(og),
        qx=qx, kx=kx, vb=vs.astype(BF16), vs=vs, sig=sig,
    )


def shifted(array, same_prev):
    return pltpu.roll(array, 1, 0) * same_prev


def head_masks(rows):
    span = iota((rows, SPAN), 1)
    masks = []
    for h in range(OWN):
        feature = (span >= h * HEAD_DIM) & (span < (h + 1) * HEAD_DIM)
        masks.append(feature | ((span >= BLOCK + 8 * h) & (span < BLOCK + 8 * (h + 1))))
    return masks


def scores_of(qx, kx, mask, allowed):
    qh = jnp.where(mask, qx, jnp.zeros_like(qx))
    return jnp.where(allowed, dot(kx, qh, ((1,), (1,))), NEG), qh


def head_rows(h):
    return slice(h * HEAD_DIM, (h + 1) * HEAD_DIM)


def attn_fwd_kernel(
    lens_ref, spots_ref, near_ref, far_ref, w_ref, bias_ref, wide_ref, tails_ref,
    h1_ref, mixed_ref, att_ref, lse_ref, gains_ref, heads_ref, sig_ref, *kept_refs
):
    picks = (iota((8, EXTRA), 1) == GAIN_AT + iota((8, EXTRA), 0)) & (iota((8, EXTRA), 0) < 4)
    picks = picks.astype(BF16)
    gains = dot(picks, w_ref[:, CORE:WIDE], ((1,), (1,)))
    gains_ref[...] = gains
    at = pl.multiple_of(spots_ref[0] * BLOCK, BLOCK)
    heads = dot(picks, w_ref[pl.ds(at, BLOCK), CORE:WIDE], ((1,), (1,)))
    heads_ref[0:1, 0:BLOCK] = heads[1:2]
    heads_ref[1:2, 0:BLOCK] = heads[2:3]
    tok = jnp.where(pl.program_id(0) < 4, near_ref[...], far_ref[...]).astype(F32)
    h1 = (normed(tok)[0] * gains[0:1]).astype(BF16)
    h1_ref[...] = h1
    rows = h1.shape[0]
    allowed, live, same_prev = places_of(lens_ref, pl.program_id(0), rows)
    f = front(dot(h1, w_ref[...]), bias_ref, heads_ref, wide_ref, tails_ref, same_prev)
    sig_ref[...] = f["sig"]
    for name, ref in zip(KEPT + KEPT_LOW, kept_refs):
        ref[...] = f[name]
    vt = f["vs"].T.astype(BF16)
    att = []
    for h, mask in enumerate(head_masks(rows)):
        s, _ = scores_of(f["qx"], f["kx"], mask, allowed)
        top = jnp.max(s, axis=0, keepdims=True)
        e = jnp.exp(s - top)
        total = jnp.sum(e, axis=0, keepdims=True)
        prob = (e * (1.0 / total)).astype(BF16)
        att.append(dot(vt[head_rows(h)], prob))
        lse_ref[h : h + 1, :] = top + jnp.log(total)
    att = jnp.concatenate(att, axis=0).T
    att_ref[...] = att
    mixed_ref[0] = fold(att * f["g"] * live).astype(BF16)


def attn_bwd_kernel(
    lens_ref, spots_ref, gains_ref, wide_ref, backs_ref, w_ref, att_ref, lse_ref, dm_ref, sig_ref, *refs
):
    kept = KEPT + KEPT_LOW
    f = {name: ref[...] for name, ref in zip(kept, refs)}
    dp_ref, sums_ref, near_ref, far_ref = refs[len(kept) :]
    bucket = pl.program_id(0)
    rows = att_ref.shape[0]
    allowed, live, same_prev = places_of(lens_ref, bucket, rows)
    masks = head_masks(rows)
    same_head = wide_ref[0:BLOCK]
    q_gain, k_gain = gains_ref[0:1, 0:BLOCK], gains_ref[1:2, 0:BLOCK]
    dm = unfold(dm_ref[0].astype(F32)) * live
    g, vb = f["g"], f["vb"]
    dab = (dm * g).astype(BF16)
    dog = dm * att_ref[...] * g * (1.0 - g)
    kt = f["kx"][:, :BLOCK].astype(F32).T.astype(BF16)
    zero = jnp.zeros((rows, BLOCK), BF16)
    dkx = jnp.zeros((rows, SPAN), F32)
    dvb = jnp.zeros((rows, BLOCK), F32)
    tail = jnp.zeros((TAIL, rows), F32)
    dqt = []
    for h in range(OWN):
        s, qh = scores_of(f["qx"], f["kx"], masks[h], allowed)
        p = jnp.exp(s - lse_ref[h : h + 1, :])
        dab_h = jnp.where(masks[h][:, :BLOCK], dab, zero)
        dvb = dvb + dot(p.astype(BF16), dab_h)
        dp = dot(vb, dab_h, ((1,), (1,)))
        ds = p * (dp - jnp.sum(p * dp, axis=0, keepdims=True))
        dsb = ds.astype(BF16)
        dqt.append(dot(kt[head_rows(h)], dsb))
        dkx = dkx + dot(dsb, qh)
        along = jnp.sum(dsb.astype(F32), axis=0, keepdims=True)
        tail = jnp.where(iota((TAIL, rows), 0) == tail_lane(h, TERMS), along, tail)
    dqx = jnp.concatenate(dqt + [tail], axis=0).T
    dqb = dqx[:, :BLOCK] * HEAD_DIM**-0.5
    dkb = dkx[:, :BLOCK]

    def back(n, r, e):
        return r * (e - n * (dot_split(e * n, same_head, 2) * (1.0 / HEAD_DIM)))

    dq = back(f["qn"], f["rq"], dqb * q_gain)
    dks = back(f["kn"], f["rk"], dkb * k_gain)
    last = iota((rows, 1), 0) == rows - 1

    def mix_back(grad, rate, cur, prev):
        ahead = pltpu.roll(rate * grad * same_prev, rows - 1, 0)
        return (1.0 - rate) * grad + jnp.where(last, 0.0, ahead), grad * (prev - cur)

    dk, dak = mix_back(dks, f["ak"], f["k"], shifted(f["k"], same_prev))
    dv, dav = mix_back(dvb, f["av"], f["v"], shifted(f["v"], same_prev))

    onward = (iota((rows, rows), 1) >= iota((rows, rows), 0)).astype(BF16)
    keep = sum(dot(onward, term) for term in split(dqx[:, BLOCK:] - dkx[:, BLOCK:], TERMS))
    sig = sig_ref[...]
    drate = (
        dot_split(dak, backs_ref[0:BLOCK], 2)
        + dot_split(dav, backs_ref[BLOCK : 2 * BLOCK], 2)
        + dot_split(keep, backs_ref[2 * BLOCK :], 2)
    )
    lane = iota((rows, EXTRA), 1)
    drate = drate * (1.0 - sig) * jnp.where(lane < OWN, 1.0, sig)
    drate = jnp.where(lane < RATES, drate, 0.0)
    grads = jnp.concatenate([dq, dk, dv, dog, drate], axis=1).astype(BF16)
    dp_ref[...] = grads
    dh1 = dot(grads, w_ref[...], ((1,), (1,))).astype(BF16)

    @pl.when(bucket < 4)
    def _():
        near_ref[...] = dh1

    @pl.when(bucket >= 4)
    def _():
        far_ref[...] = dh1

    @pl.when(bucket == 0)
    def _():
        sums_ref[...] = jnp.zeros_like(sums_ref)

    sums_ref[0:1, 0:BLOCK] += jnp.sum(dqb * f["qn"], axis=0, keepdims=True)
    sums_ref[1:2, 0:BLOCK] += jnp.sum(dkb * f["kn"], axis=0, keepdims=True)
    sums_ref[2:3, 0:EXTRA] += jnp.sum(drate, axis=0, keepdims=True)


def rows_spec(rows, width):
    return pl.BlockSpec((rows, width), lambda i, lens, spots: (i, 0))


def whole_spec(dims):
    return pl.BlockSpec(dims, lambda i, lens, spots: (0,) * len(dims))


def spot_spec(rows):
    return pl.BlockSpec((1, rows * 3 // 2, EXTRA), lambda i, lens, spots: (spots[i], 0, 0))


def kept_specs(rows):
    return [rows_spec(rows, BLOCK) for _ in KEPT] + [rows_spec(rows, c) for c in (SPAN, SPAN, BLOCK)]


def attn_fwd(lens, spots, near, far, w, bias, wide, tails):
    buckets = lens.shape[0]
    width = near.shape[1]
    total = 2 * near.shape[0]
    rows = total // buckets
    return pl.pallas_call(
        attn_fwd_kernel,
        grid_spec=pltpu.PrefetchScalarGridSpec(
            num_scalar_prefetch=2,
            grid=(buckets,),
            in_specs=[
                near_spec(rows, width),
                far_spec(rows, width),
                whole_spec(w.shape),
                whole_spec(bias.shape),
                whole_spec(wide.shape),
                whole_spec(tails.shape),
            ],
            out_specs=[
                rows_spec(rows, width),
                spot_spec(rows),
                rows_spec(rows, BLOCK),
                rows_spec(8, rows),
                whole_spec((8, width)),
                whole_spec((8, 2 * EXTRA)),
                rows_spec(rows, EXTRA),
            ]
            + kept_specs(rows),
        ),
        out_shape=[
            shape((total, width), BF16),
            shape((buckets, rows * 3 // 2, EXTRA), BF16),
            shape((total, BLOCK), F32),
            shape((8 * buckets, rows), F32),
            shape((8, width), F32),
            shape((8, 2 * EXTRA), F32),
            shape((total, EXTRA), F32),
        ]
        + [shape((total, BLOCK), F32) for _ in KEPT]
        + [shape((total, c), BF16) for c in (SPAN, SPAN, BLOCK)],
        **settings(20, 60),
        name="attn_fwd",
    )(lens, spots, near, far, w, bias, wide, tails)


def near_spec(rows, width):
    return pl.BlockSpec((rows, width), lambda i, lens, spots: (jnp.minimum(i, 3), 0))


def far_spec(rows, width):
    return pl.BlockSpec((rows, width), lambda i, lens, spots: (jnp.maximum(i - 4, 0), 0))


def attn_bwd(lens, spots, gains, wide, backs, w, att, lse, dm, sig, *kept):
    buckets = lens.shape[0]
    total = att.shape[0]
    width = w.shape[0]
    rows = total // buckets
    return pl.pallas_call(
        attn_bwd_kernel,
        grid_spec=pltpu.PrefetchScalarGridSpec(
            num_scalar_prefetch=2,
            grid=(buckets,),
            in_specs=[whole_spec(x.shape) for x in (gains, wide, backs, w)]
            + [rows_spec(rows, BLOCK), rows_spec(8, rows), spot_spec(rows), rows_spec(rows, EXTRA)]
            + kept_specs(rows),
            out_specs=[
                rows_spec(rows, WIDE),
                whole_spec((8, 2 * EXTRA)),
                near_spec(rows, width),
                far_spec(rows, width),
            ],
        ),
        out_shape=[shape((total, WIDE), BF16), shape((8, 2 * EXTRA), F32)]
        + [shape((total // 2, width), BF16)] * 2,
        **settings(24, 60),
        name="attn_bwd",
    )(lens, spots, gains, wide, backs, w, att, lse, dm, sig, *kept)


def mid_fwd_kernel(spots_ref, got_ref, tok_ref, gain_ref, *refs):
    x2_ref, h2_ref = refs[TP:]
    acc = tok_ref[...].astype(F32)
    for i in range(TP):
        acc = acc + dot(unfold(got_ref[spots_ref[i]]), refs[i][...])
    x2_ref[...] = acc
    h2_ref[...] = (normed(acc)[0] * gain_ref[...]).astype(BF16)


def once(dims):
    return pl.BlockSpec(dims, lambda i: (0,) * len(dims))


def mix_specs(w):
    return [once((BLOCK, x.shape[1])) for x in w]


def mid_fwd(spots, got, w, tok, gain):
    rows, width = tok.shape
    return pl.pallas_call(
        mid_fwd_kernel,
        grid=(1,),
        in_specs=[SMEM, once(got.shape), once(tok.shape), once(gain.shape)] + mix_specs(w),
        out_specs=[once(tok.shape)] * 2,
        out_shape=[shape(tok.shape, F32), shape(tok.shape, BF16)],
        **settings(5, 40),
        name="mid_fwd",
    )(spots, got, tok, gain, *w)


def mid_bwd_kernel(spots_ref, a_ref, b_ref, c_ref, d_ref, x2_ref, cot_ref, gain_ref, got_ref, *refs):
    dx2_ref, dm_ref, near_ref, far_ref = refs[TP:]
    dh2 = a_ref[...] + b_ref[...].astype(F32) + c_ref[...].astype(F32) + d_ref[...].astype(F32)
    n2, r2 = normed(x2_ref[...])
    dx2 = cot_ref[...].astype(F32) + norm_back(n2, r2, dh2 * gain_ref[...])
    dx2_ref[...] = dx2
    dxb = dx2.astype(BF16)
    for i in range(TP):
        dm = dot(dxb, refs[i][...], ((1,), (1,)))
        dm_ref[spots_ref[i]] = fold(dm).astype(BF16)
        out_ref = near_ref if i < 4 else far_ref
        piece = dot(unfold(got_ref[spots_ref[i]]), dxb, ((0,), (0,)))
        out_ref[(i % 4) * BLOCK : (i % 4 + 1) * BLOCK, :] = piece.astype(BF16)


def mid_bwd(spots, parts, x2, cot, gain, got, w):
    rows, width = x2.shape
    arrays = (*parts, x2, cot, gain, got)
    outs = [
        shape((rows, width), F32),
        shape((TP, rows * 3 // 2, EXTRA), BF16),
        shape((4 * BLOCK, width), BF16),
        shape((4 * BLOCK, width), BF16),
    ]
    return pl.pallas_call(
        mid_bwd_kernel,
        grid=(1,),
        in_specs=[SMEM] + [once(x.shape) for x in arrays] + mix_specs(w),
        out_specs=[once(x.shape) for x in outs],
        out_shape=outs,
        **settings(9, 48),
        name="mid_bwd",
    )(spots, *arrays, *w)


def fold_cores(near, far):
    width = near.shape[1]
    rows = near.shape[0] // 4
    steps = 4

    def kernel(*refs):
        for i in range(4):
            both = refs[i][...].astype(F32) + refs[4 + i][...].astype(F32)
            refs[8 + i][...] = both.astype(refs[8 + i].dtype)

    def quarter(i):
        return pl.BlockSpec((rows // steps, width), lambda j: (i * steps + j, 0))

    return pl.pallas_call(
        kernel,
        grid=(steps,),
        in_specs=[quarter(i) for i in range(4)] * 2,
        out_specs=[pl.BlockSpec((rows // steps, width), lambda j: (j, 0))] * 4,
        out_shape=[shape((rows, width), F32)] + [shape((rows, width), BF16)] * 3,
        **settings(4, 32),
        name="fold_cores",
    )(near, near, near, near, far, far, far, far)


def last_norm(tok, gain, dx2, *parts):
    rows, width = tok.shape
    steps = 4

    def kernel(tok_ref, gain_ref, dx2_ref, *refs):
        n1, r1 = normed(tok_ref[...].astype(F32))
        refs[-1][...] = dx2_ref[...] + norm_back(n1, r1, total_of([x[...] for x in refs[:-1]]) * gain_ref[...])

    block = pl.BlockSpec((rows // steps, width), lambda i: (i, 0))
    return pl.pallas_call(
        kernel,
        grid=(steps,),
        in_specs=[block, once(gain.shape), block] + [block] * len(parts),
        out_specs=block,
        out_shape=shape((rows, width), F32),
        **settings(3, 24),
        name="last_norm",
    )(tok, gain, dx2, *parts)


def ffn_kernel(lens_ref, h2_ref, cot_ref, gu_ref, dn_ref, ab_ref, dgu_ref, *out_refs):
    rows, ff = h2_ref.shape[0], dn_ref.shape[0]
    total = jnp.int32(0)
    for j in range(lens_ref.shape[1]):
        total = total + lens_ref[pl.program_id(0), j]
    live = (iota((rows, 1), 0) < total).astype(F32)
    gu = dot(h2_ref[...], gu_ref[...])
    da = dot(cot_ref[...], dn_ref[...], ((1,), (1,))) * live
    gate, up = gu[:, :ff], gu[:, ff:]
    sg = jax.nn.sigmoid(gate)
    act = gate * sg
    ab = (act * up * live).astype(BF16)
    dgate = (da * up * sg * (1.0 + gate * (1.0 - sg))).astype(BF16)
    dup = (da * act).astype(BF16)
    ab_ref[...] = ab
    dgu_ref[:, :ff] = dgate
    dgu_ref[:, ff:] = dup
    dh2 = dot(dgate, gu_ref[:, :ff], ((1,), (1,))) + dot(dup, gu_ref[:, ff:], ((1,), (1,)))
    dh2 = dh2.astype(BF16)
    out = dot(ab, dn_ref[...]).astype(BF16)
    near = pl.program_id(0) < pl.num_programs(0) // 2

    @pl.when(near)
    def _():
        out_refs[0][...] = out
        out_refs[1][...] = dh2

    @pl.when(jnp.logical_not(near))
    def _():
        out_refs[2][...] = out
        out_refs[3][...] = dh2


def ffn(lens, h2, cot, gu, dn):
    buckets = lens.shape[0]
    half = buckets // 2
    total, width = h2.shape
    rows = total // buckets
    ff = dn.shape[0]

    def block(columns):
        return pl.BlockSpec((rows, columns), lambda i: (i, 0))

    def whole(dims):
        return pl.BlockSpec(dims, lambda i: (0, 0))

    near = pl.BlockSpec((rows, width), lambda i: (jnp.minimum(i, half - 1), 0))
    far = pl.BlockSpec((rows, width), lambda i: (jnp.maximum(i - half, 0), 0))
    return pl.pallas_call(
        ffn_kernel,
        grid=(buckets,),
        in_specs=[SMEM, block(width), block(width), whole(gu.shape), whole(dn.shape)],
        out_specs=[block(ff), block(2 * ff), near, near, far, far],
        out_shape=[shape((total, ff), BF16), shape((total, 2 * ff), BF16)] + [shape((total // 2, width), BF16)] * 4,
        **settings(4 * buckets, 40),
        name="ffn",
    )(lens, h2, cot, gu, dn)


def sum_of_dots(lefts, rights):
    return sum(dot(x[...], y[...], ((0,), (0,))) for x, y in zip(lefts, rights))


def grad_down(ab, cot):
    ff, width = ab[0].shape[1], cot[0].shape[1]
    steps = 4
    columns = width // steps
    count = len(ab)

    def kernel(*refs):
        refs[-1][...] = sum_of_dots(refs[:count], refs[count : 2 * count]).astype(BF16)

    return pl.pallas_call(
        kernel,
        grid=(steps,),
        in_specs=[pl.BlockSpec(x.shape, lambda i: (0, 0)) for x in ab]
        + [pl.BlockSpec((x.shape[0], columns), lambda i: (0, i)) for x in cot],
        out_specs=pl.BlockSpec((ff, columns), lambda i: (0, i)),
        out_shape=shape((ff, width), BF16),
        **settings(6, 60),
        name="grad_down",
    )(*ab, *cot)


def grad_gu(h2, dgu, share):
    width = h2[0].shape[1]
    own_rows = width // (TP * share)
    columns = dgu[0].shape[1]
    steps = TP // 2
    count = len(h2)

    def kernel(*refs):
        res = sum_of_dots(refs[:count], refs[count : 2 * count])
        for k in range(2):
            for z in range(share):
                at = (k * share + z) * own_rows
                refs[-1][z, k] = res[at : at + own_rows].astype(BF16)

    return pl.pallas_call(
        kernel,
        grid=(steps,),
        in_specs=[pl.BlockSpec((x.shape[0], width // steps), lambda i: (0, i)) for x in h2]
        + [pl.BlockSpec(x.shape, lambda i: (0, 0)) for x in dgu],
        out_specs=pl.BlockSpec((share, 2, own_rows, columns), lambda i: (0, i, 0, 0)),
        out_shape=shape((share, TP, own_rows, columns), BF16),
        **settings(11, 60),
        name="grad_gu",
    )(*h2, *dgu)


def grad_in(place, sums, left, right, share):
    own_rows = left.shape[1] // (TP * share)
    columns = right.shape[1]
    steps = TP // 2

    def kernel(place_ref, sums_ref, left_ref, right_ref, out_ref):
        res = dot(left_ref[...], right_ref[...], ((0,), (0,)))
        lane, row = iota((BLOCK, EXTRA), 1), iota((BLOCK, EXTRA), 0)
        turned = sums_ref[...].T[0:BLOCK]
        bias = jnp.where((lane == row % own_rows) & (lane < RATES), sums_ref[2:3, 0:EXTRA], 0.0)
        bias = jnp.sum(bias, axis=1, keepdims=True)
        for k in range(2):
            mine = (pl.program_id(0) * 2 + k == place_ref[0]).astype(F32)
            extra = res[k * BLOCK : (k + 1) * BLOCK, CORE:WIDE]
            extra = jnp.where(lane == RATES, turned[:, 0:1] * mine, extra)
            extra = jnp.where(lane == RATES + 1, turned[:, 1:2] * mine, extra)
            extra = jnp.where(lane == RATES + 2, bias, extra)
            for z in range(share):
                at = z * own_rows
                rest = k * BLOCK + at
                out_ref[z, k, :, :CORE] = res[rest : rest + own_rows, :CORE].astype(BF16)
                out_ref[z, k, :, CORE:] = extra[at : at + own_rows].astype(BF16)

    return pl.pallas_call(
        kernel,
        grid=(steps,),
        in_specs=[
            SMEM,
            pl.BlockSpec(sums.shape, lambda i: (0, 0)),
            pl.BlockSpec((left.shape[0], left.shape[1] // steps), lambda i: (0, i)),
            pl.BlockSpec(right.shape, lambda i: (0, 0)),
        ],
        out_specs=pl.BlockSpec((share, 2, own_rows, columns), lambda i: (0, i, 0, 0)),
        out_shape=shape((share, TP, own_rows, columns), BF16),
        **settings(11, 60),
        name="grad_in",
    )(place, sums, left, right)


def own_share(part):
    columns = part.shape[-1]
    summed = lax.psum_scatter(part.reshape(-1, columns), "sh", scatter_dimension=0, tiled=True)
    return summed.reshape(TP, -1, columns)


def swap(blocks):
    return lax.all_to_all(blocks, "tp", 0, 0, tiled=True)


def body(
    tokens,
    doc_lengths,
    norm_gain,
    w_attn_in,
    w_rates,
    rate_bias,
    q_gain,
    k_gain,
    w_out,
    ffn_gain,
    w_gate_up,
    w_down,
    cotangent,
):
    place = lax.axis_index("tp")
    share = lax.axis_size("sh")
    width = tokens.shape[1]
    own_rows = w_attn_in.shape[0]
    spots = place ^ jnp.array(OFFSETS, jnp.int32)

    gains = jnp.stack([norm_gain, q_gain, k_gain, ffn_gain])
    packed, w_mix = phase(pack_in(doc_lengths, w_attn_in, w_rates, gains), w_out)
    got_in = swap(packed)
    w_in = lax.all_gather(got_in, "sh", axis=1).reshape(width, WIDE)
    lens_all = got_in[:, 0, CORE + LENS_AT : CORE + LENS_AT + doc_lengths.shape[0]].astype(jnp.int32)
    lens = lens_all[spots]
    bias = lax.dynamic_index_in_dim(rate_bias.reshape(3, TP, OWN), place, 1, False).reshape(1, RATES)
    bias = jnp.pad(bias, ((0, 7), (0, EXTRA - RATES)))

    tok, w_gu, w_mix, _ = phase(tokens, w_gate_up, w_mix, got_in)
    two_four, w_mix = phase(sides(tok), gather_shares(w_mix))
    tok = join_rows(tok, *two_four, *diagonal(*two_four))
    tok, packed = phase(tok, pack_gu(w_gu))
    joined = join_ffn(swap(packed), w_down)
    far = flip(tok, 1)
    w_gu, w_dn = open_ffn(lax.all_gather(joined, "sh", axis=0), w_down.shape[0], width)

    wide, tails, backs = constants()
    beside = phase(join_rows(in_order(w_mix), cotangent), joined)[0]
    two_four = sides(beside)
    h1, mixed, att, lse, gains, gain_heads, *kept = attn_fwd(lens, spots, tok, far, w_in, bias, wide, tails)
    gain_one, gain_two = gains[0:1], gains[3:4]
    mixed, two_four = phase(mixed, two_four)
    near = [beside, *two_four]
    got_mixed, mix_six, far = phase(
        swap(mixed), diagonal(*[x[:BLOCK] for x in two_four]), [flip(x, 1) for x in near]
    )
    mix_six = jnp.concatenate(mix_six, axis=0)
    w_mix = [*near, mix_six, *far, flip(mix_six, 1)]
    x2, h2 = mid_fwd(spots, got_mixed, w_mix, tokens, gain_two)

    orders = (2, 4, 3, 5), (0, 1), (6, 7)
    lens_of = [jnp.stack([lens[OFFSETS.index(d)] for d in order]) for order in orders]
    h2, near, far = phase(h2, near, far)
    cot = [
        join_rows(*[(half[i], BLOCK) for half in (near, far) for i in (1, 2)]),
        join_rows((near[0], BLOCK), (far[0], BLOCK)),
    ]
    (two, four), one, cot = phase(sides(h2), flip(h2, 1), cot)
    six = diagonal(two, four)
    two, four, three, five, one = phase(two, four, flip(two, 1), flip(four, 1), one)
    h2 = [join_rows(two, four, three, five), join_rows(h2, one)]
    found = [ffn(lens_of[0], h2[0], cot[0], w_gu, w_dn)]
    found, six, h2[1], cot_six = phase(found, six, h2[1], diagonal(*[x[BLOCK:] for x in near[1:3]]))
    six, cot_six = [jnp.concatenate(x, axis=0) for x in (six, cot_six)]
    seven, cot_seven, far, more = phase(
        flip(six, 1),
        flip(cot_six, 1),
        [flip(x, 1) for x in found[0][4:]],
        ffn(lens_of[1], h2[1], cot[1], w_gu, w_dn),
    )
    found.append(more)
    layer_side, side = [[x.astype(BF16) for x in two_sums(*pair)] for pair in zip(found[0][2:4], far)]
    h2.append(join_rows(six, seven))
    cot.append(join_rows(cot_six, cot_seven))
    side, layer_side, h2[2], cot[2], one = phase(side, layer_side, h2[2], cot[2], found[1][5])
    side = flip(side[0], 2), flip(side[1], 4)
    one, more = phase(flip(one, 1), ffn(lens_of[2], h2[2], cot[2], w_gu, w_dn))
    found.append(more)
    ab, dgu, out_near, dh2_near, out_far, dh2_far = zip(*found)
    seven, dw_dn, side = phase(flip(dh2_far[2], 1), grad_down(ab, cot), side)
    dw_dn = lax.psum_scatter(dw_dn, "sh", scatter_dimension=0, tiled=True)
    low = (dh2_near[2].astype(F32) + seven.astype(F32)).astype(BF16)
    low, dgu, out_far = phase(low, dgu, out_far)
    own = dh2_near[1].astype(F32) + one.astype(F32)
    six, dw_gu, out_far, own = phase(flip(low, 6), grad_gu(h2, dgu, share), [flip(x, 1) for x in out_far[1:]], own)
    dw_gu = own_share(dw_gu)
    layer_six = (out_near[2].astype(F32) + out_far[1].astype(F32)).astype(BF16)
    dh2, layer_low = phase((own, *side, six), (*layer_side, layer_six))

    found, layer_low = phase(
        mid_bwd(spots, dh2, x2, cotangent, gain_two, got_mixed, w_mix), relay_six(layer_low)
    )
    dx2, dm, mix_near, mix_far = found
    mix_own, mix_low = both_cores(quarters(mix_near), quarters(flip(mix_far, 1)))
    got_dm, mix_own, mix_low, layer_low = phase(swap(dm), mix_own, mix_low, add_six(layer_low))
    layer, mix_low, found, dw_dn = phase(
        (flip(layer_low[0], 2), flip(layer_low[1], 4)),
        relay_six(mix_low),
        attn_bwd(lens, spots, gain_heads, wide, backs, w_in, att, lse, got_dm, *kept),
        dw_dn,
    )
    dp, sums, dh1_near, dh1_far = found

    mix_low = add_six(mix_low)
    mix = flip(mix_low[0], 2), flip(mix_low[1], 4)
    dh1_far, dw_in, dw_gu = phase(flip(dh1_far, 1), grad_in(place.reshape(1), sums, h1, dp, share), dw_gu)
    dw_in = own_share(dw_in)
    dh1_own, *dh1_low = fold_cores(dh1_near, dh1_far)
    dh1_low, mix = phase(relay_six(dh1_low), mix)
    layer_own = out_near[1].astype(F32) + out_far[0].astype(F32)
    layer_out = (x2 + total_of((layer_own, *layer))).astype(BF16)
    two, four = add_six(dh1_low)
    dh1, got_gu, dw_in, layer_out = phase((flip(two, 2), flip(four, 4)), swap(dw_gu), dw_in, layer_out)
    mix = to_shares(total_of((mix_own, *mix)).astype(BF16))
    d_tokens = last_norm(tokens, gain_one, dx2, dh1_own, *dh1)

    d_w_attn_in, d_w_rates, small = unpack_in(swap(dw_in), w_attn_in, w_rates, norm_gain)
    d_w_gate_up, small_gu = unpack_gu(got_gu, w_gate_up, ffn_gain)
    d_ffn_gain = small_gu[0, :own_rows]
    small, mix = phase(small, mix)
    d_w_out = total_of(mix)
    return (
        layer_out,
        d_tokens,
        small[0, :own_rows],
        d_w_attn_in,
        d_w_rates,
        small[3, : w_rates.shape[1]],
        small[1, :own_rows],
        small[2, :own_rows],
        d_w_out,
        d_ffn_gain,
        d_w_gate_up,
        dw_dn.astype(F32),
    )


def solution(mesh):
    devices = mesh.devices.reshape(TP, -1)
    grid = Mesh(devices, ("tp", "sh"))
    rows = P(("tp", "sh"), None)
    flat = P(("tp", "sh"))
    in_specs = (rows, flat, flat, rows, rows, P(), flat, flat, rows, flat, rows, rows, rows)
    out_specs = (rows, rows, flat, rows, rows, P(), flat, flat, rows, flat, rows, rows)
    return jax.shard_map(body, mesh=grid, in_specs=in_specs, out_specs=out_specs, check_vma=False)
```

```python
import jax
import jax.numpy as jnp
import numpy as np
from jax import lax
from jax.experimental import pallas as pl
from jax.experimental.pallas import tpu as pltpu
from jax.sharding import Mesh
from jax.sharding import PartitionSpec as P

HEADS = 24
HEAD_DIM = 64
EPS = 1e-06
NEG = -1e30
TP = 8
OWN = HEADS // TP
BLOCK = OWN * HEAD_DIM
CORE = 4 * BLOCK
EXTRA = 128
WIDE = CORE + EXTRA
RATES = 3 * OWN
GAIN_AT = RATES
LENS_AT = RATES + 4
OFFSETS = (0, 2, 4, 6, 1, 3, 5, 7)
F32 = jnp.float32
BF16 = jnp.bfloat16


def flip(array, offset):
    return lax.ppermute(array, "tp", [(i, i ^ offset) for i in range(TP)])


def sides(own):
    return flip(own, 2), flip(own, 4)


def diagonal(two, four):
    cut = two.shape[0] // 2
    return flip(two[:cut], 4), flip(four[cut:], 2)


def others(own):
    return [flip(own, d) for d in (2, 4, 6)]


def both_cores(near, far):
    sums = [x.astype(F32) + y.astype(F32) for x, y in zip(near, far)]
    return sums[0], [x.astype(BF16) for x in sums[1:]]


def two_sums(near, far):
    rows = near.shape[0] // 2
    return [near[i : i + rows].astype(F32) + far[i : i + rows].astype(F32) for i in (0, rows)]


def quarters(array):
    rows = array.shape[0] // 4
    return [array[i * rows : (i + 1) * rows] for i in range(4)]


def send(blocks):
    return [flip(x, d) for x, d in zip(blocks, (2, 4, 6))]


def relay_six(blocks):
    two, four, six = blocks
    cut = six.shape[0] // 2
    return two, four, flip(six[:cut], 2), flip(six[cut:], 4)


def add_six(blocks):
    two, four, over_two, over_four = blocks
    cut = over_two.shape[0]
    two = jnp.concatenate([two[:cut], (two[cut:].astype(F32) + over_four.astype(F32)).astype(BF16)], axis=0)
    four = jnp.concatenate([(four[:cut].astype(F32) + over_two.astype(F32)).astype(BF16), four[cut:]], axis=0)
    return two, four


def gather_shares(own):
    share = lax.axis_size("sh")
    return [own] + [lax.ppermute(own, "sh", [(i, (i + k) % share) for i in range(share)]) for k in range(1, share)]


def in_order(pieces):
    here = lax.axis_index("sh")
    share = len(pieces)
    out = jnp.zeros((share,) + pieces[0].shape, pieces[0].dtype)
    for k, piece in enumerate(pieces):
        out = lax.dynamic_update_index_in_dim(out, piece, (here - k) % share, 0)
    return out.reshape((-1,) + pieces[0].shape[1:])


def to_shares(part):
    share = lax.axis_size("sh")
    here = lax.axis_index("sh")
    blocks = part.reshape(share, -1, part.shape[1])
    picked = [lax.dynamic_index_in_dim(blocks, (here + k) % share, 0, False) for k in range(share)]
    return picked[:1] + [
        lax.ppermute(picked[k], "sh", [(i, (i + k) % share) for i in range(share)]) for k in range(1, share)
    ]


def total_of(parts):
    return sum(term.astype(F32) for term in parts)


def phase(*values):
    return lax.optimization_barrier(values)


def normed(field_in):
    factor = lax.rsqrt(jnp.mean(field_in * field_in, axis=-1, keepdims=True) + EPS)
    return field_in * factor, factor


def norm_back(normal, factor, grad_in):
    return factor * (grad_in - normal * jnp.mean(grad_in * normal, axis=-1, keepdims=True))


def dot(a, b, dims=((1,), (0,)), precision=None):
    return lax.dot_general(a, b, (dims, ((), ())), precision=precision, preferred_element_type=F32)


def iota(shape, dim):
    return lax.broadcasted_iota(jnp.int32, shape, dim)


def settings(us, mib):
    cost = pl.CostEstimate(flops=int(us * 1e7), bytes_accessed=int(us * 1e4), transcendentals=0)
    return dict(compiler_params=pltpu.CompilerParams(vmem_limit_bytes=mib * 2**20), cost_estimate=cost)


SMEM = pl.BlockSpec(memory_space=pltpu.SMEM)
VMEM = pl.BlockSpec(memory_space=pltpu.VMEM)


def shape(dims, dtype):
    return jax.ShapeDtypeStruct(dims, dtype)


def rate_picks(t, rows, columns, flipped=False):
    whole, own = iota((rows, columns), 1 if flipped else 0), iota((rows, columns), 0 if flipped else 1)
    kind, head = own // OWN, own % OWN
    return ((own < RATES) & (whole == kind * HEADS + t * OWN + head)).astype(BF16)


def pack_in_kernel(lens_ref, w_ref, rates_ref, gains_ref, out_ref):
    rows, width = w_ref.shape[0], w_ref.shape[1] // 4
    picks = (iota((4, EXTRA), 1) == GAIN_AT + iota((4, EXTRA), 0)).astype(BF16)
    beside = dot(gains_ref[...], picks, ((0,), (0,)))
    lane, row = iota((rows, EXTRA), 1), iota((rows, EXTRA), 0)
    for j in range(lens_ref.shape[0]):
        beside = jnp.where((lane == LENS_AT + j) & (row == 0), lens_ref[j].astype(F32), beside)
    for t in range(TP):
        for b in range(4):
            at = b * width + t * BLOCK
            out_ref[t, :, b * BLOCK : (b + 1) * BLOCK] = w_ref[:, at : at + BLOCK]
        rates = dot(rates_ref[...], rate_picks(t, rates_ref.shape[1], EXTRA))
        out_ref[t, :, CORE:WIDE] = (rates + beside).astype(BF16)


def pack_in(lens, w, rates, gains):
    return pl.pallas_call(
        pack_in_kernel,
        in_specs=[SMEM, VMEM, VMEM, VMEM],
        out_specs=VMEM,
        out_shape=shape((TP, w.shape[0], WIDE), BF16),
        **settings(3, 16),
        name="pack_in",
    )(lens, w, rates, gains)


def pack_gu_kernel(w_ref, out_ref):
    ff = w_ref.shape[1] // 2
    own = ff // TP
    for t in range(TP):
        out_ref[t, :, :own] = w_ref[:, t * own : (t + 1) * own]
        out_ref[t, :, own:] = w_ref[:, ff + t * own : ff + (t + 1) * own]


def pack_gu(w):
    return pl.pallas_call(
        pack_gu_kernel,
        in_specs=[VMEM],
        out_specs=VMEM,
        out_shape=shape((TP, w.shape[0], w.shape[1] // TP), BF16),
        **settings(2, 16),
        name="pack_gu",
    )(w)


def join_ffn(got, down):
    columns = got.shape[2]
    top, rows = got.shape[0] * got.shape[1], down.shape[0]
    half = rows // 2

    def kernel(got_ref, down_ref, out_ref):
        for t in range(TP):
            out_ref[t * got.shape[1] : (t + 1) * got.shape[1], :] = got_ref[t]
        out_ref[top : top + rows, :] = down_ref[:, :columns]
        out_ref[top + rows :, : columns // 2] = down_ref[:half, columns:]
        out_ref[top + rows :, columns // 2 :] = down_ref[half:, columns:]

    return pl.pallas_call(
        kernel,
        in_specs=[VMEM, VMEM],
        out_specs=VMEM,
        out_shape=shape((top + rows + half, columns), BF16),
        **settings(2, 16),
        name="join_ffn",
    )(got, down)


def open_ffn(joined, down_rows, width):
    share, _, columns = joined.shape
    own_rows = width // (TP * share)
    top = TP * own_rows
    half = down_rows // 2

    def kernel(in_ref, gu_ref, down_ref):
        for z in range(share):
            for t in range(TP):
                at = (t * share + z) * own_rows
                gu_ref[at : at + own_rows, :] = in_ref[z, t * own_rows : (t + 1) * own_rows, :]
            at = z * down_rows
            down_ref[at : at + down_rows, :columns] = in_ref[z, top : top + down_rows, :]
            down_ref[at : at + half, columns:] = in_ref[z, top + down_rows :, : columns // 2]
            down_ref[at + half : at + down_rows, columns:] = in_ref[z, top + down_rows :, columns // 2 :]

    return pl.pallas_call(
        kernel,
        in_specs=[VMEM],
        out_specs=[VMEM, VMEM],
        out_shape=[shape((width, columns), BF16), shape((share * down_rows, width), BF16)],
        **settings(4, 16),
        name="open_ffn",
    )(joined)


def join_lists(*lists):
    lists = [[x if isinstance(x, tuple) else (x, 0) for x in pieces] for pieces in lists]
    arrays = [x for pieces in lists for x, _ in pieces]

    def kernel(*refs):
        at = 0
        for pieces, out_ref in zip(lists, refs[len(arrays) :]):
            to = 0
            for (x, first), ref in zip(pieces, refs[at : at + len(pieces)]):
                more = x.shape[0] - first
                out_ref[to : to + more, :] = ref[first:, :]
                to += more
            at += len(pieces)

    totals = [(sum(x.shape[0] - first for x, first in pieces), pieces[0][0].shape[1]) for pieces in lists]
    return pl.pallas_call(
        kernel,
        in_specs=[VMEM] * len(arrays),
        out_specs=[VMEM] * len(lists),
        out_shape=[shape(x, BF16) for x in totals],
        **settings(2, 24),
        name="join_rows",
    )(*arrays)


def join_rows(*pieces):
    return join_lists(pieces)[0]


def unpack_in_kernel(got_ref, w_ref, rates_ref, gain_ref, dw_ref, drates_ref, small_ref):
    rows, width = w_ref.shape[0], w_ref.shape[1] // 4
    along = jnp.zeros((rows, 1), F32)
    drates = jnp.zeros((rows, EXTRA), F32)
    sums = jnp.zeros((rows, EXTRA), F32)
    bias = jnp.zeros((rows, EXTRA), F32)
    lane, row = iota((rows, EXTRA), 1), iota((rows, EXTRA), 0)
    for t in range(TP):
        for b in range(4):
            at = b * width + t * BLOCK
            piece = got_ref[t, :, b * BLOCK : (b + 1) * BLOCK].astype(F32)
            dw_ref[:, at : at + BLOCK] = piece
            along = along + jnp.sum(piece * w_ref[:, at : at + BLOCK].astype(F32), axis=1, keepdims=True)
        extra = got_ref[t, :, CORE:WIDE]
        drates = drates + dot(extra, rate_picks(t, EXTRA, EXTRA, True))
        extra = extra.astype(F32)
        sums = sums + extra
        spot = (row // OWN) * HEADS + t * OWN + row % OWN
        bias = bias + jnp.where((lane == spot) & (row < RATES), extra[:, RATES + 2 : RATES + 3], 0.0)
    columns = rates_ref.shape[1]
    drates_ref[...] = drates[:, :columns]
    along = along + jnp.sum(drates[:, :columns] * rates_ref[...].astype(F32), axis=1, keepdims=True)
    turned = jnp.where(lane == 0, along, 0.0) + jnp.where(lane == 1, sums[:, RATES : RATES + 1], 0.0)
    turned = turned + jnp.where(lane == 2, sums[:, RATES + 1 : RATES + 2], 0.0)
    pick = (iota((rows, EXTRA), 0) == iota((rows, EXTRA), 1)).astype(F32)
    turned = dot(turned, pick, ((0,), (0,)), lax.Precision.HIGHEST)
    small_ref[0:1, :] = turned[0:1, :] / gain_ref[...]
    small_ref[1:3, :] = turned[1:3, :]
    small_ref[3:4, :] = jnp.sum(bias, axis=0, keepdims=True)
    small_ref[4:8, :] = jnp.zeros((4, EXTRA), F32)


def unpack_in(got, w, rates, gain):
    rows = w.shape[0]
    gain = jnp.pad(gain.astype(F32)[None], ((0, 0), (0, EXTRA - rows)), constant_values=1.0)
    return pl.pallas_call(
        unpack_in_kernel,
        in_specs=[VMEM] * 4,
        out_specs=[VMEM] * 3,
        out_shape=[shape(w.shape, F32), shape(rates.shape, F32), shape((8, EXTRA), F32)],
        **settings(5, 16),
        name="unpack_in",
    )(got, w, rates, gain)


def unpack_gu_kernel(got_ref, w_ref, gain_ref, dw_ref, small_ref):
    rows, ff = w_ref.shape[0], w_ref.shape[1] // 2
    own = ff // TP
    along = jnp.zeros((rows, 1), F32)
    for t in range(TP):
        for half in range(2):
            at = half * ff + t * own
            piece = got_ref[t, :, half * own : (half + 1) * own].astype(F32)
            dw_ref[:, at : at + own] = piece
            along = along + jnp.sum(piece * w_ref[:, at : at + own].astype(F32), axis=1, keepdims=True)
    lane = iota((rows, EXTRA), 1)
    pick = (iota((rows, EXTRA), 0) == lane).astype(F32)
    turned = dot(jnp.where(lane == 0, along, 0.0), pick, ((0,), (0,)), lax.Precision.HIGHEST)
    small_ref[...] = turned[0:8, :] / gain_ref[...]


def unpack_gu(got, w, gain):
    rows = w.shape[0]
    gain = jnp.pad(gain.astype(F32)[None], ((0, 0), (0, EXTRA - rows)), constant_values=1.0)
    return pl.pallas_call(
        unpack_gu_kernel,
        in_specs=[VMEM] * 3,
        out_specs=[VMEM] * 2,
        out_shape=[shape(w.shape, F32), shape((8, EXTRA), F32)],
        **settings(3, 16),
        name="unpack_gu",
    )(got, w, gain)


def fold(block):
    cut = block.shape[0] // 2
    tail = jnp.concatenate([block[:cut, EXTRA:], block[cut:, EXTRA:]], axis=1)
    return jnp.concatenate([block[:, :EXTRA], tail], axis=0)


def unfold(block):
    rows = 2 * block.shape[0] // 3
    tail = block[rows:]
    tail = jnp.concatenate([tail[:, : BLOCK - EXTRA], tail[:, BLOCK - EXTRA :]], axis=0)
    return jnp.concatenate([block[:rows], tail], axis=1)


def split(field_in, count):
    terms = []
    for _ in range(count):
        terms.append(field_in.astype(BF16))
        field_in = field_in - terms[-1].astype(F32)
    return terms


def dot_split(field_in, picks, count):
    return sum(dot(term, picks) for term in split(field_in, count))


TAIL = 64
SPAN = BLOCK + TAIL
TERMS = 3


def tail_lane(h, term):
    return 8 * h + term


def constants():
    head = np.arange(BLOCK) // HEAD_DIM
    same = head[:, None] == head[None, :]
    extra = np.arange(EXTRA)
    key_lanes = extra[:, None] == OWN + head[None, :]
    value_lanes = extra[:, None] == 2 * OWN + head[None, :]
    to_query = np.zeros((TERMS, EXTRA, TAIL))
    to_key = np.zeros((TERMS, EXTRA, TAIL))
    from_tail = np.zeros((TAIL, EXTRA))
    for h in range(OWN):
        for term in range(TERMS):
            to_query[term, h, tail_lane(h, term)] = 1
            to_key[term, h, tail_lane(h, TERMS + term)] = -1
        from_tail[tail_lane(h, TERMS), h] = 1
    wide = np.concatenate([same, key_lanes, value_lanes], axis=0)
    tails = np.concatenate([to_query.reshape(-1, TAIL), to_key.reshape(-1, TAIL)], axis=0)
    backs = np.concatenate([key_lanes.T, value_lanes.T, from_tail], axis=0)
    return tuple(jnp.asarray(x, BF16) for x in (wide, tails, backs))


def places_of(lens_ref, bucket, rows):
    ends = []
    total = jnp.int32(0)
    for j in range(lens_ref.shape[1]):
        total = total + lens_ref[bucket, j]
        ends.append(total)

    def segment(place):
        seg = jnp.zeros(place.shape, jnp.int32)
        for end in ends:
            seg = seg + (end <= place).astype(jnp.int32)
        return seg

    col = iota((rows, 1), 0)
    row = iota((1, rows), 1)
    seg_col = segment(col)
    allowed = (col <= row) & (segment(row) == seg_col)
    live = (col < total).astype(F32)
    same_prev = ((col > 0) & (seg_col == segment(col - 1))).astype(F32)
    return allowed, live, same_prev


KEPT = ("qn", "kn", "rq", "rk", "ak", "av", "k", "v", "g")
KEPT_LOW = ("qx", "kx", "vb")


def front(proj, bias_ref, gains_ref, wide_ref, tails_ref, same_prev):
    rows = proj.shape[0]
    q = proj[:, 0:BLOCK]
    k = proj[:, BLOCK : 2 * BLOCK]
    v = proj[:, 2 * BLOCK : 3 * BLOCK]
    og = proj[:, 3 * BLOCK : CORE]
    rate = proj[:, CORE:WIDE] + bias_ref[0:1, :]
    sig = jax.nn.sigmoid(rate)
    log_keep = jnp.minimum(rate, 0.0) - jnp.log1p(jnp.exp(-jnp.abs(rate)))
    upto = (iota((rows, rows), 1) <= iota((rows, rows), 0)).astype(BF16)
    decay = sum(dot(upto, term) for term in split(log_keep, TERMS))
    same_head = wide_ref[0:BLOCK]
    ak = dot_split(sig, wide_ref[BLOCK : BLOCK + EXTRA], 2)
    av = dot_split(sig, wide_ref[BLOCK + EXTRA :], 2)
    ks = ak * shifted(k, same_prev) + (1.0 - ak) * k
    vs = av * shifted(v, same_prev) + (1.0 - av) * v

    def head_norm(u):
        factor = lax.rsqrt(dot_split(u * u, same_head, 2) * (1.0 / HEAD_DIM) + EPS)
        return u * factor, factor

    qn, rq = head_norm(q)
    kn, rk = head_norm(ks)
    q_gain, k_gain = gains_ref[0:1, 0:BLOCK], gains_ref[1:2, 0:BLOCK]
    qb = (qn * q_gain).astype(BF16) * jnp.asarray(HEAD_DIM**-0.5, BF16)
    kb = (kn * k_gain).astype(BF16)

    terms = split(decay, TERMS)
    lane = iota((1, TAIL), 1)
    ones_q = ((lane % 8 >= TERMS) & (lane % 8 < 2 * TERMS)).astype(F32)
    ones_k = (lane % 8 < TERMS).astype(F32)
    q_tail = ones_q + sum(dot(terms[t], tails_ref[t * EXTRA : (t + 1) * EXTRA]) for t in range(TERMS))
    k_tail = ones_k + sum(
        dot(terms[t], tails_ref[(TERMS + t) * EXTRA : (TERMS + t + 1) * EXTRA]) for t in range(TERMS)
    )
    qx = jnp.concatenate([qb, q_tail.astype(BF16)], axis=1)
    kx = jnp.concatenate([kb, k_tail.astype(BF16)], axis=1)
    return dict(
        qn=qn, kn=kn, rq=rq, rk=rk, ak=ak, av=av, k=k, v=v, g=jax.nn.sigmoid(og),
        qx=qx, kx=kx, vb=vs.astype(BF16), vs=vs, sig=sig,
    )


def shifted(array, same_prev):
    return pltpu.roll(array, 1, 0) * same_prev


def head_masks(rows):
    span = iota((rows, SPAN), 1)
    masks = []
    for h in range(OWN):
        feature = (span >= h * HEAD_DIM) & (span < (h + 1) * HEAD_DIM)
        masks.append(feature | ((span >= BLOCK + 8 * h) & (span < BLOCK + 8 * (h + 1))))
    return masks


def scores_of(qx, kx, mask, allowed):
    qh = jnp.where(mask, qx, jnp.zeros_like(qx))
    return jnp.where(allowed, dot(kx, qh, ((1,), (1,))), NEG), qh


def head_rows(h):
    return slice(h * HEAD_DIM, (h + 1) * HEAD_DIM)


def attn_fwd_kernel(
    lens_ref, spots_ref, near_ref, far_ref, w_ref, bias_ref, wide_ref, tails_ref,
    h1_ref, mixed_ref, att_ref, lse_ref, gains_ref, heads_ref, sig_ref, *kept_refs
):
    picks = (iota((8, EXTRA), 1) == GAIN_AT + iota((8, EXTRA), 0)) & (iota((8, EXTRA), 0) < 4)
    picks = picks.astype(BF16)
    gains = dot(picks, w_ref[:, CORE:WIDE], ((1,), (1,)))
    gains_ref[...] = gains
    at = pl.multiple_of(spots_ref[0] * BLOCK, BLOCK)
    heads = dot(picks, w_ref[pl.ds(at, BLOCK), CORE:WIDE], ((1,), (1,)))
    heads_ref[0:1, 0:BLOCK] = heads[1:2]
    heads_ref[1:2, 0:BLOCK] = heads[2:3]
    tok = jnp.where(pl.program_id(0) < 4, near_ref[...], far_ref[...]).astype(F32)
    h1 = (normed(tok)[0] * gains[0:1]).astype(BF16)
    h1_ref[...] = h1
    rows = h1.shape[0]
    allowed, live, same_prev = places_of(lens_ref, pl.program_id(0), rows)
    f = front(dot(h1, w_ref[...]), bias_ref, heads_ref, wide_ref, tails_ref, same_prev)
    sig_ref[...] = f["sig"]
    for name, ref in zip(KEPT + KEPT_LOW, kept_refs):
        ref[...] = f[name]
    vt = f["vs"].T.astype(BF16)
    att = []
    for h, mask in enumerate(head_masks(rows)):
        s, _ = scores_of(f["qx"], f["kx"], mask, allowed)
        top = jnp.max(s, axis=0, keepdims=True)
        e = jnp.exp(s - top)
        total = jnp.sum(e, axis=0, keepdims=True)
        prob = (e * (1.0 / total)).astype(BF16)
        att.append(dot(vt[head_rows(h)], prob))
        lse_ref[h : h + 1, :] = top + jnp.log(total)
    att = jnp.concatenate(att, axis=0).T
    att_ref[...] = att
    mixed_ref[0] = fold(att * f["g"] * live).astype(BF16)


def attn_bwd_kernel(
    lens_ref, spots_ref, gains_ref, wide_ref, backs_ref, w_ref, att_ref, lse_ref, dm_ref, sig_ref, *refs
):
    kept = KEPT + KEPT_LOW
    f = {name: ref[...] for name, ref in zip(kept, refs)}
    dp_ref, sums_ref, near_ref, far_ref = refs[len(kept) :]
    bucket = pl.program_id(0)
    rows = att_ref.shape[0]
    allowed, live, same_prev = places_of(lens_ref, bucket, rows)
    masks = head_masks(rows)
    same_head = wide_ref[0:BLOCK]
    q_gain, k_gain = gains_ref[0:1, 0:BLOCK], gains_ref[1:2, 0:BLOCK]
    dm = unfold(dm_ref[0].astype(F32)) * live
    g, vb = f["g"], f["vb"]
    dab = (dm * g).astype(BF16)
    dog = dm * att_ref[...] * g * (1.0 - g)
    kt = f["kx"][:, :BLOCK].astype(F32).T.astype(BF16)
    zero = jnp.zeros((rows, BLOCK), BF16)
    dkx = jnp.zeros((rows, SPAN), F32)
    dvb = jnp.zeros((rows, BLOCK), F32)
    tail = jnp.zeros((TAIL, rows), F32)
    dqt = []
    for h in range(OWN):
        s, qh = scores_of(f["qx"], f["kx"], masks[h], allowed)
        p = jnp.exp(s - lse_ref[h : h + 1, :])
        dab_h = jnp.where(masks[h][:, :BLOCK], dab, zero)
        dvb = dvb + dot(p.astype(BF16), dab_h)
        dp = dot(vb, dab_h, ((1,), (1,)))
        ds = p * (dp - jnp.sum(p * dp, axis=0, keepdims=True))
        dsb = ds.astype(BF16)
        dqt.append(dot(kt[head_rows(h)], dsb))
        dkx = dkx + dot(dsb, qh)
        along = jnp.sum(dsb.astype(F32), axis=0, keepdims=True)
        tail = jnp.where(iota((TAIL, rows), 0) == tail_lane(h, TERMS), along, tail)
    dqx = jnp.concatenate(dqt + [tail], axis=0).T
    dqb = dqx[:, :BLOCK] * HEAD_DIM**-0.5
    dkb = dkx[:, :BLOCK]

    def back(n, r, e):
        return r * (e - n * (dot_split(e * n, same_head, 2) * (1.0 / HEAD_DIM)))

    dq = back(f["qn"], f["rq"], dqb * q_gain)
    dks = back(f["kn"], f["rk"], dkb * k_gain)
    last = iota((rows, 1), 0) == rows - 1

    def mix_back(grad, rate, cur, prev):
        ahead = pltpu.roll(rate * grad * same_prev, rows - 1, 0)
        return (1.0 - rate) * grad + jnp.where(last, 0.0, ahead), grad * (prev - cur)

    dk, dak = mix_back(dks, f["ak"], f["k"], shifted(f["k"], same_prev))
    dv, dav = mix_back(dvb, f["av"], f["v"], shifted(f["v"], same_prev))

    onward = (iota((rows, rows), 1) >= iota((rows, rows), 0)).astype(BF16)
    keep = sum(dot(onward, term) for term in split(dqx[:, BLOCK:] - dkx[:, BLOCK:], TERMS))
    sig = sig_ref[...]
    drate = (
        dot_split(dak, backs_ref[0:BLOCK], 2)
        + dot_split(dav, backs_ref[BLOCK : 2 * BLOCK], 2)
        + dot_split(keep, backs_ref[2 * BLOCK :], 2)
    )
    lane = iota((rows, EXTRA), 1)
    drate = drate * (1.0 - sig) * jnp.where(lane < OWN, 1.0, sig)
    drate = jnp.where(lane < RATES, drate, 0.0)
    grads = jnp.concatenate([dq, dk, dv, dog, drate], axis=1).astype(BF16)
    dp_ref[...] = grads
    dh1 = dot(grads, w_ref[...], ((1,), (1,))).astype(BF16)

    @pl.when(bucket < 4)
    def _():
        near_ref[...] = dh1

    @pl.when(bucket >= 4)
    def _():
        far_ref[...] = dh1

    @pl.when(bucket == 0)
    def _():
        sums_ref[...] = jnp.zeros_like(sums_ref)

    sums_ref[0:1, 0:BLOCK] += jnp.sum(dqb * f["qn"], axis=0, keepdims=True)
    sums_ref[1:2, 0:BLOCK] += jnp.sum(dkb * f["kn"], axis=0, keepdims=True)
    sums_ref[2:3, 0:EXTRA] += jnp.sum(drate, axis=0, keepdims=True)


def rows_spec(rows, width):
    return pl.BlockSpec((rows, width), lambda i, lens, spots: (i, 0))


def whole_spec(dims):
    return pl.BlockSpec(dims, lambda i, lens, spots: (0,) * len(dims))


def spot_spec(rows):
    return pl.BlockSpec((1, rows * 3 // 2, EXTRA), lambda i, lens, spots: (spots[i], 0, 0))


def kept_specs(rows):
    return [rows_spec(rows, BLOCK) for _ in KEPT] + [rows_spec(rows, c) for c in (SPAN, SPAN, BLOCK)]


def attn_fwd(lens, spots, near, far, w, bias, wide, tails):
    buckets = lens.shape[0]
    width = near.shape[1]
    total = 2 * near.shape[0]
    rows = total // buckets
    return pl.pallas_call(
        attn_fwd_kernel,
        grid_spec=pltpu.PrefetchScalarGridSpec(
            num_scalar_prefetch=2,
            grid=(buckets,),
            in_specs=[
                near_spec(rows, width),
                far_spec(rows, width),
                whole_spec(w.shape),
                whole_spec(bias.shape),
                whole_spec(wide.shape),
                whole_spec(tails.shape),
            ],
            out_specs=[
                rows_spec(rows, width),
                spot_spec(rows),
                rows_spec(rows, BLOCK),
                rows_spec(8, rows),
                whole_spec((8, width)),
                whole_spec((8, 2 * EXTRA)),
                rows_spec(rows, EXTRA),
            ]
            + kept_specs(rows),
        ),
        out_shape=[
            shape((total, width), BF16),
            shape((buckets, rows * 3 // 2, EXTRA), BF16),
            shape((total, BLOCK), F32),
            shape((8 * buckets, rows), F32),
            shape((8, width), F32),
            shape((8, 2 * EXTRA), F32),
            shape((total, EXTRA), F32),
        ]
        + [shape((total, BLOCK), F32) for _ in KEPT]
        + [shape((total, c), BF16) for c in (SPAN, SPAN, BLOCK)],
        **settings(20, 60),
        name="attn_fwd",
    )(lens, spots, near, far, w, bias, wide, tails)


def near_spec(rows, width):
    return pl.BlockSpec((rows, width), lambda i, lens, spots: (jnp.minimum(i, 3), 0))


def far_spec(rows, width):
    return pl.BlockSpec((rows, width), lambda i, lens, spots: (jnp.maximum(i - 4, 0), 0))


def attn_bwd(lens, spots, gains, wide, backs, w, att, lse, dm, sig, *kept):
    buckets = lens.shape[0]
    total = att.shape[0]
    width = w.shape[0]
    rows = total // buckets
    return pl.pallas_call(
        attn_bwd_kernel,
        grid_spec=pltpu.PrefetchScalarGridSpec(
            num_scalar_prefetch=2,
            grid=(buckets,),
            in_specs=[whole_spec(x.shape) for x in (gains, wide, backs, w)]
            + [rows_spec(rows, BLOCK), rows_spec(8, rows), spot_spec(rows), rows_spec(rows, EXTRA)]
            + kept_specs(rows),
            out_specs=[
                rows_spec(rows, WIDE),
                whole_spec((8, 2 * EXTRA)),
                near_spec(rows, width),
                far_spec(rows, width),
            ],
        ),
        out_shape=[shape((total, WIDE), BF16), shape((8, 2 * EXTRA), F32)]
        + [shape((total // 2, width), BF16)] * 2,
        **settings(24, 60),
        name="attn_bwd",
    )(lens, spots, gains, wide, backs, w, att, lse, dm, sig, *kept)


def mid_fwd_kernel(spots_ref, got_ref, tok_ref, gain_ref, *refs):
    x2_ref, h2_ref = refs[TP:]
    acc = tok_ref[...].astype(F32)
    for i in range(TP):
        acc = acc + dot(unfold(got_ref[spots_ref[i]]), refs[i][...])
    x2_ref[...] = acc
    h2_ref[...] = (normed(acc)[0] * gain_ref[...]).astype(BF16)


def once(dims):
    return pl.BlockSpec(dims, lambda i: (0,) * len(dims))


def mix_specs(w):
    return [once((BLOCK, x.shape[1])) for x in w]


def mid_fwd(spots, got, w, tok, gain):
    rows, width = tok.shape
    return pl.pallas_call(
        mid_fwd_kernel,
        grid=(1,),
        in_specs=[SMEM, once(got.shape), once(tok.shape), once(gain.shape)] + mix_specs(w),
        out_specs=[once(tok.shape)] * 2,
        out_shape=[shape(tok.shape, F32), shape(tok.shape, BF16)],
        **settings(5, 40),
        name="mid_fwd",
    )(spots, got, tok, gain, *w)


def mid_bwd_kernel(spots_ref, a_ref, b_ref, c_ref, d_ref, x2_ref, cot_ref, gain_ref, got_ref, *refs):
    dx2_ref, dm_ref, near_ref, far_ref = refs[TP:]
    dh2 = a_ref[...] + b_ref[...].astype(F32) + c_ref[...].astype(F32) + d_ref[...].astype(F32)
    n2, r2 = normed(x2_ref[...])
    dx2 = cot_ref[...].astype(F32) + norm_back(n2, r2, dh2 * gain_ref[...])
    dx2_ref[...] = dx2
    dxb = dx2.astype(BF16)
    for i in range(TP):
        dm = dot(dxb, refs[i][...], ((1,), (1,)))
        dm_ref[spots_ref[i]] = fold(dm).astype(BF16)
        out_ref = near_ref if i < 4 else far_ref
        piece = dot(unfold(got_ref[spots_ref[i]]), dxb, ((0,), (0,)))
        out_ref[(i % 4) * BLOCK : (i % 4 + 1) * BLOCK, :] = piece.astype(BF16)


def mid_bwd(spots, parts, x2, cot, gain, got, w):
    rows, width = x2.shape
    arrays = (*parts, x2, cot, gain, got)
    outs = [
        shape((rows, width), F32),
        shape((TP, rows * 3 // 2, EXTRA), BF16),
        shape((4 * BLOCK, width), BF16),
        shape((4 * BLOCK, width), BF16),
    ]
    return pl.pallas_call(
        mid_bwd_kernel,
        grid=(1,),
        in_specs=[SMEM] + [once(x.shape) for x in arrays] + mix_specs(w),
        out_specs=[once(x.shape) for x in outs],
        out_shape=outs,
        **settings(9, 48),
        name="mid_bwd",
    )(spots, *arrays, *w)


def fold_cores(near, far):
    width = near.shape[1]
    rows = near.shape[0] // 4
    steps = 4

    def kernel(*refs):
        for i in range(4):
            both = refs[i][...].astype(F32) + refs[4 + i][...].astype(F32)
            refs[8 + i][...] = both.astype(refs[8 + i].dtype)

    def quarter(i):
        return pl.BlockSpec((rows // steps, width), lambda j: (i * steps + j, 0))

    return pl.pallas_call(
        kernel,
        grid=(steps,),
        in_specs=[quarter(i) for i in range(4)] * 2,
        out_specs=[pl.BlockSpec((rows // steps, width), lambda j: (j, 0))] * 4,
        out_shape=[shape((rows, width), F32)] + [shape((rows, width), BF16)] * 3,
        **settings(4, 32),
        name="fold_cores",
    )(near, near, near, near, far, far, far, far)


def last_norm(tok, gain, dx2, *parts):
    rows, width = tok.shape
    steps = 4

    def kernel(tok_ref, gain_ref, dx2_ref, *refs):
        n1, r1 = normed(tok_ref[...].astype(F32))
        refs[-1][...] = dx2_ref[...] + norm_back(n1, r1, total_of([x[...] for x in refs[:-1]]) * gain_ref[...])

    block = pl.BlockSpec((rows // steps, width), lambda i: (i, 0))
    return pl.pallas_call(
        kernel,
        grid=(steps,),
        in_specs=[block, once(gain.shape), block] + [block] * len(parts),
        out_specs=block,
        out_shape=shape((rows, width), F32),
        **settings(3, 24),
        name="last_norm",
    )(tok, gain, dx2, *parts)


def ffn_kernel(lens_ref, h2_ref, cot_ref, gu_ref, dn_ref, ab_ref, dgu_ref, *out_refs):
    rows, ff = h2_ref.shape[0], dn_ref.shape[0]
    total = jnp.int32(0)
    for j in range(lens_ref.shape[1]):
        total = total + lens_ref[pl.program_id(0), j]
    live = (iota((rows, 1), 0) < total).astype(F32)
    gu = dot(h2_ref[...], gu_ref[...])
    da = dot(cot_ref[...], dn_ref[...], ((1,), (1,))) * live
    gate, up = gu[:, :ff], gu[:, ff:]
    sg = jax.nn.sigmoid(gate)
    act = gate * sg
    ab = (act * up * live).astype(BF16)
    dgate = (da * up * sg * (1.0 + gate * (1.0 - sg))).astype(BF16)
    dup = (da * act).astype(BF16)
    ab_ref[...] = ab
    dgu_ref[:, :ff] = dgate
    dgu_ref[:, ff:] = dup
    dh2 = dot(dgate, gu_ref[:, :ff], ((1,), (1,))) + dot(dup, gu_ref[:, ff:], ((1,), (1,)))
    dh2 = dh2.astype(BF16)
    out = dot(ab, dn_ref[...]).astype(BF16)
    near = pl.program_id(0) < pl.num_programs(0) // 2

    @pl.when(near)
    def _():
        out_refs[0][...] = out
        out_refs[1][...] = dh2

    @pl.when(jnp.logical_not(near))
    def _():
        out_refs[2][...] = out
        out_refs[3][...] = dh2


def ffn(lens, h2, cot, gu, dn):
    buckets = lens.shape[0]
    half = buckets // 2
    total, width = h2.shape
    rows = total // buckets
    ff = dn.shape[0]

    def block(columns):
        return pl.BlockSpec((rows, columns), lambda i: (i, 0))

    def whole(dims):
        return pl.BlockSpec(dims, lambda i: (0, 0))

    near = pl.BlockSpec((rows, width), lambda i: (jnp.minimum(i, half - 1), 0))
    far = pl.BlockSpec((rows, width), lambda i: (jnp.maximum(i - half, 0), 0))
    return pl.pallas_call(
        ffn_kernel,
        grid=(buckets,),
        in_specs=[SMEM, block(width), block(width), whole(gu.shape), whole(dn.shape)],
        out_specs=[block(ff), block(2 * ff), near, near, far, far],
        out_shape=[shape((total, ff), BF16), shape((total, 2 * ff), BF16)] + [shape((total // 2, width), BF16)] * 4,
        **settings(4 * buckets, 34),
        name="ffn",
    )(lens, h2, cot, gu, dn)


def sum_of_dots(lefts, rights):
    return sum(dot(x[...], y[...], ((0,), (0,))) for x, y in zip(lefts, rights))


def grad_down(ab, cot):
    ff, width = ab[0].shape[1], cot[0].shape[1]
    steps = 4
    columns = width // steps
    count = len(ab)

    def kernel(*refs):
        refs[-1][...] = sum_of_dots(refs[:count], refs[count : 2 * count]).astype(BF16)

    return pl.pallas_call(
        kernel,
        grid=(steps,),
        in_specs=[pl.BlockSpec(x.shape, lambda i: (0, 0)) for x in ab]
        + [pl.BlockSpec((x.shape[0], columns), lambda i: (0, i)) for x in cot],
        out_specs=pl.BlockSpec((ff, columns), lambda i: (0, i)),
        out_shape=shape((ff, width), BF16),
        **settings(6, 24),
        name="grad_down",
    )(*ab, *cot)


def grad_gu(h2, dgu, share):
    width = h2[0].shape[1]
    own_rows = width // (TP * share)
    columns = dgu[0].shape[1]
    steps = TP // 2
    count = len(h2)

    def kernel(*refs):
        res = sum_of_dots(refs[:count], refs[count : 2 * count])
        for k in range(2):
            for z in range(share):
                at = (k * share + z) * own_rows
                refs[-1][z, k] = res[at : at + own_rows].astype(BF16)

    return pl.pallas_call(
        kernel,
        grid=(steps,),
        in_specs=[pl.BlockSpec((x.shape[0], width // steps), lambda i: (0, i)) for x in h2]
        + [pl.BlockSpec(x.shape, lambda i: (0, 0)) for x in dgu],
        out_specs=pl.BlockSpec((share, 2, own_rows, columns), lambda i: (0, i, 0, 0)),
        out_shape=shape((share, TP, own_rows, columns), BF16),
        **settings(11, 36),
        name="grad_gu",
    )(*h2, *dgu)


def grad_in(place, sums, left, right, share):
    own_rows = left.shape[1] // (TP * share)
    columns = right.shape[1]
    steps = TP // 2

    def kernel(place_ref, sums_ref, left_ref, right_ref, out_ref):
        res = dot(left_ref[...], right_ref[...], ((0,), (0,)))
        lane, row = iota((BLOCK, EXTRA), 1), iota((BLOCK, EXTRA), 0)
        turned = sums_ref[...].T[0:BLOCK]
        bias = jnp.where((lane == row % own_rows) & (lane < RATES), sums_ref[2:3, 0:EXTRA], 0.0)
        bias = jnp.sum(bias, axis=1, keepdims=True)
        for k in range(2):
            mine = (pl.program_id(0) * 2 + k == place_ref[0]).astype(F32)
            extra = res[k * BLOCK : (k + 1) * BLOCK, CORE:WIDE]
            extra = jnp.where(lane == RATES, turned[:, 0:1] * mine, extra)
            extra = jnp.where(lane == RATES + 1, turned[:, 1:2] * mine, extra)
            extra = jnp.where(lane == RATES + 2, bias, extra)
            for z in range(share):
                at = z * own_rows
                rest = k * BLOCK + at
                out_ref[z, k, :, :CORE] = res[rest : rest + own_rows, :CORE].astype(BF16)
                out_ref[z, k, :, CORE:] = extra[at : at + own_rows].astype(BF16)

    return pl.pallas_call(
        kernel,
        grid=(steps,),
        in_specs=[
            SMEM,
            pl.BlockSpec(sums.shape, lambda i: (0, 0)),
            pl.BlockSpec((left.shape[0], left.shape[1] // steps), lambda i: (0, i)),
            pl.BlockSpec(right.shape, lambda i: (0, 0)),
        ],
        out_specs=pl.BlockSpec((share, 2, own_rows, columns), lambda i: (0, i, 0, 0)),
        out_shape=shape((share, TP, own_rows, columns), BF16),
        **settings(11, 60),
        name="grad_in",
    )(place, sums, left, right)


def own_share(part):
    columns = part.shape[-1]
    summed = lax.psum_scatter(part.reshape(-1, columns), "sh", scatter_dimension=0, tiled=True)
    return summed.reshape(TP, -1, columns)


def swap(blocks):
    return lax.all_to_all(blocks, "tp", 0, 0, tiled=True)


def body(
    tokens,
    doc_lengths,
    norm_gain,
    w_attn_in,
    w_rates,
    rate_bias,
    q_gain,
    k_gain,
    w_out,
    ffn_gain,
    w_gate_up,
    w_down,
    cotangent,
):
    place = lax.axis_index("tp")
    share = lax.axis_size("sh")
    width = tokens.shape[1]
    own_rows = w_attn_in.shape[0]
    spots = place ^ jnp.array(OFFSETS, jnp.int32)

    gains = jnp.stack([norm_gain, q_gain, k_gain, ffn_gain])
    packed, w_mix = phase(pack_in(doc_lengths, w_attn_in, w_rates, gains), w_out)
    got_in = swap(packed)
    w_in = lax.all_gather(got_in, "sh", axis=1).reshape(width, WIDE)
    lens_all = got_in[:, 0, CORE + LENS_AT : CORE + LENS_AT + doc_lengths.shape[0]].astype(jnp.int32)
    lens = lens_all[spots]
    bias = lax.dynamic_index_in_dim(rate_bias.reshape(3, TP, OWN), place, 1, False).reshape(1, RATES)
    bias = jnp.pad(bias, ((0, 7), (0, EXTRA - RATES)))

    tok, w_gu, w_mix, _ = phase(tokens, w_gate_up, w_mix, got_in)
    two_four, w_mix = phase(sides(tok), gather_shares(w_mix))
    tok = join_rows(tok, *two_four, *diagonal(*two_four))
    tok, packed = phase(tok, pack_gu(w_gu))
    joined = join_ffn(swap(packed), w_down)
    far = flip(tok, 1)
    w_gu, w_dn = open_ffn(lax.all_gather(joined, "sh", axis=0), w_down.shape[0], width)

    wide, tails, backs = constants()
    beside = phase(join_rows(in_order(w_mix), cotangent), joined)[0]
    two_four = sides(beside)
    h1, mixed, att, lse, gains, gain_heads, *kept = attn_fwd(lens, spots, tok, far, w_in, bias, wide, tails)
    gain_one, gain_two = gains[0:1], gains[3:4]
    mixed, two_four = phase(mixed, two_four)
    near = [beside, *two_four]
    got_mixed, mix_six, far = phase(
        swap(mixed), diagonal(*[x[:BLOCK] for x in two_four]), [flip(x, 1) for x in near]
    )
    mix_six = jnp.concatenate(mix_six, axis=0)
    w_mix = [*near, mix_six, *far, flip(mix_six, 1)]
    x2, h2 = mid_fwd(spots, got_mixed, w_mix, tokens, gain_two)

    orders = (2, 4, 3, 5), (0, 1), (6, 7)
    lens_of = [jnp.stack([lens[OFFSETS.index(d)] for d in order]) for order in orders]
    h2, near, far = phase(h2, near, far)
    cot = [
        join_rows(*[(half[i], BLOCK) for half in (near, far) for i in (1, 2)]),
        join_rows((near[0], BLOCK), (far[0], BLOCK)),
    ]
    (two, four), one, cot = phase(sides(h2), flip(h2, 1), cot)
    six = diagonal(two, four)
    two, four, three, five, one = phase(two, four, flip(two, 1), flip(four, 1), one)
    h2 = [join_rows(two, four, three, five), join_rows(h2, one)]
    found = [ffn(lens_of[0], h2[0], cot[0], w_gu, w_dn)]
    found, six, h2[1], cot_six = phase(found, six, h2[1], diagonal(*[x[BLOCK:] for x in near[1:3]]))
    six, cot_six = join_lists(six, cot_six)
    seven, cot_seven, far, more = phase(
        flip(six, 1),
        flip(cot_six, 1),
        [flip(x, 1) for x in found[0][4:]],
        ffn(lens_of[1], h2[1], cot[1], w_gu, w_dn),
    )
    found.append(more)
    side = [x.astype(BF16) for x in two_sums(found[0][3], far[1])]
    h2.append(join_rows(six, seven))
    cot.append(join_rows(cot_six, cot_seven))
    side, h2[2], cot[2], one = phase(side, h2[2], cot[2], found[1][5])
    side = flip(side[0], 2), flip(side[1], 4)
    one, more = phase(flip(one, 1), ffn(lens_of[2], h2[2], cot[2], w_gu, w_dn))
    found.append(more)
    ab, dgu, out_near, dh2_near, out_far, dh2_far = zip(*found)
    seven, dw_dn, side = phase(flip(dh2_far[2], 1), grad_down(ab, cot), side)
    dw_dn = lax.psum_scatter(dw_dn, "sh", scatter_dimension=0, tiled=True)
    low = (dh2_near[2].astype(F32) + seven.astype(F32)).astype(BF16)
    low, dgu, out_far, far = phase(low, dgu, out_far, far)
    own = dh2_near[1].astype(F32) + one.astype(F32)
    six, dw_gu, out_far, own = phase(flip(low, 6), grad_gu(h2, dgu, share), [flip(x, 1) for x in out_far[1:]], own)
    dw_gu = own_share(dw_gu)
    layer_side = [x.astype(BF16) for x in two_sums(out_near[0], far[0])]
    layer_six = (out_near[2].astype(F32) + out_far[1].astype(F32)).astype(BF16)
    dh2, layer_low = phase((own, *side, six), (*layer_side, layer_six))

    found, layer_low = phase(
        mid_bwd(spots, dh2, x2, cotangent, gain_two, got_mixed, w_mix), relay_six(layer_low)
    )
    dx2, dm, mix_near, mix_far = found
    mix_own, mix_low = both_cores(quarters(mix_near), quarters(flip(mix_far, 1)))
    got_dm, mix_own, mix_low, layer_low = phase(swap(dm), mix_own, mix_low, add_six(layer_low))
    layer, mix_low, found, dw_dn = phase(
        (flip(layer_low[0], 2), flip(layer_low[1], 4)),
        relay_six(mix_low),
        attn_bwd(lens, spots, gain_heads, wide, backs, w_in, att, lse, got_dm, *kept),
        dw_dn,
    )
    dp, sums, dh1_near, dh1_far = found

    mix_low = add_six(mix_low)
    mix = flip(mix_low[0], 2), flip(mix_low[1], 4)
    dh1_far, dw_in, dw_gu = phase(flip(dh1_far, 1), grad_in(place.reshape(1), sums, h1, dp, share), dw_gu)
    dw_in = own_share(dw_in)
    dh1_own, *dh1_low = fold_cores(dh1_near, dh1_far)
    dh1_low, mix = phase(relay_six(dh1_low), mix)
    layer_own = out_near[1].astype(F32) + out_far[0].astype(F32)
    layer_out = (x2 + total_of((layer_own, *layer))).astype(BF16)
    two, four = add_six(dh1_low)
    mix = total_of((mix_own, *mix)).astype(BF16)
    dh1, got_gu, dw_in, layer_out, mix = phase(
        (flip(two, 2), flip(four, 4)), swap(dw_gu), dw_in, layer_out, mix
    )
    mix = to_shares(mix)
    d_tokens = last_norm(tokens, gain_one, dx2, dh1_own, *dh1)

    d_w_attn_in, d_w_rates, small = unpack_in(swap(dw_in), w_attn_in, w_rates, norm_gain)
    d_w_gate_up, small_gu = unpack_gu(got_gu, w_gate_up, ffn_gain)
    d_ffn_gain = small_gu[0, :own_rows]
    small, mix = phase(small, mix)
    d_w_out = total_of(mix)
    return (
        layer_out,
        d_tokens,
        small[0, :own_rows],
        d_w_attn_in,
        d_w_rates,
        small[3, : w_rates.shape[1]],
        small[1, :own_rows],
        small[2, :own_rows],
        d_w_out,
        d_ffn_gain,
        d_w_gate_up,
        dw_dn.astype(F32),
    )


def solution(mesh):
    devices = mesh.devices.reshape(TP, -1)
    grid = Mesh(devices, ("tp", "sh"))
    rows = P(("tp", "sh"), None)
    flat = P(("tp", "sh"))
    in_specs = (rows, flat, flat, rows, rows, P(), flat, flat, rows, flat, rows, rows, rows)
    out_specs = (rows, rows, flat, rows, rows, P(), flat, flat, rows, flat, rows, rows)
    return jax.shard_map(body, mesh=grid, in_specs=in_specs, out_specs=out_specs, check_vma=False)
```

```python
import jax
import jax.numpy as jnp
import numpy as np
from jax import lax
from jax.experimental import pallas as pl
from jax.experimental.pallas import tpu as pltpu
from jax.sharding import Mesh
from jax.sharding import PartitionSpec as P

HEADS = 24
HEAD_DIM = 64
EPS = 1e-06
NEG = -1e30
TP = 8
OWN = HEADS // TP
BLOCK = OWN * HEAD_DIM
CORE = 4 * BLOCK
EXTRA = 128
WIDE = CORE + EXTRA
RATES = 3 * OWN
GAIN_AT = RATES
LENS_AT = RATES + 4
OFFSETS = (0, 2, 4, 6, 1, 3, 5, 7)
F32 = jnp.float32
BF16 = jnp.bfloat16


def flip(array, offset):
    return lax.ppermute(array, "tp", [(i, i ^ offset) for i in range(TP)])


def sides(own):
    return flip(own, 2), flip(own, 4)


def diagonal(two, four):
    cut = two.shape[0] // 2
    return flip(two[:cut], 4), flip(four[cut:], 2)


def others(own):
    return [flip(own, d) for d in (2, 4, 6)]


def both_cores(near, far):
    sums = [x.astype(F32) + y.astype(F32) for x, y in zip(near, far)]
    return sums[0], [x.astype(BF16) for x in sums[1:]]


def two_sums(near, far):
    rows = near.shape[0] // 2
    return [near[i : i + rows].astype(F32) + far[i : i + rows].astype(F32) for i in (0, rows)]


def quarters(array):
    rows = array.shape[0] // 4
    return [array[i * rows : (i + 1) * rows] for i in range(4)]


def send(blocks):
    return [flip(x, d) for x, d in zip(blocks, (2, 4, 6))]


def relay_six(blocks):
    two, four, six = blocks
    cut = six.shape[0] // 2
    return two, four, flip(six[:cut], 2), flip(six[cut:], 4)


def add_six(blocks):
    two, four, over_two, over_four = blocks
    cut = over_two.shape[0]
    two = jnp.concatenate([two[:cut], (two[cut:].astype(F32) + over_four.astype(F32)).astype(BF16)], axis=0)
    four = jnp.concatenate([(four[:cut].astype(F32) + over_two.astype(F32)).astype(BF16), four[cut:]], axis=0)
    return two, four


def gather_shares(own):
    share = lax.axis_size("sh")
    return [own] + [lax.ppermute(own, "sh", [(i, (i + k) % share) for i in range(share)]) for k in range(1, share)]


def in_order(pieces):
    here = lax.axis_index("sh")
    share = len(pieces)
    out = jnp.zeros((share,) + pieces[0].shape, pieces[0].dtype)
    for k, piece in enumerate(pieces):
        out = lax.dynamic_update_index_in_dim(out, piece, (here - k) % share, 0)
    return out.reshape((-1,) + pieces[0].shape[1:])


def to_shares(part):
    share = lax.axis_size("sh")
    here = lax.axis_index("sh")
    blocks = part.reshape(share, -1, part.shape[1])
    picked = [lax.dynamic_index_in_dim(blocks, (here + k) % share, 0, False) for k in range(share)]
    return picked[:1] + [
        lax.ppermute(picked[k], "sh", [(i, (i + k) % share) for i in range(share)]) for k in range(1, share)
    ]


def total_of(parts):
    return sum(term.astype(F32) for term in parts)


def phase(*values):
    return lax.optimization_barrier(values)


def normed(field_in):
    factor = lax.rsqrt(jnp.mean(field_in * field_in, axis=-1, keepdims=True) + EPS)
    return field_in * factor, factor


def norm_back(normal, factor, grad_in):
    return factor * (grad_in - normal * jnp.mean(grad_in * normal, axis=-1, keepdims=True))


def dot(a, b, dims=((1,), (0,)), precision=None):
    return lax.dot_general(a, b, (dims, ((), ())), precision=precision, preferred_element_type=F32)


def iota(shape, dim):
    return lax.broadcasted_iota(jnp.int32, shape, dim)


def settings(us, mib):
    cost = pl.CostEstimate(flops=int(us * 1e7), bytes_accessed=int(us * 1e4), transcendentals=0)
    return dict(compiler_params=pltpu.CompilerParams(vmem_limit_bytes=mib * 2**20), cost_estimate=cost)


SMEM = pl.BlockSpec(memory_space=pltpu.SMEM)
VMEM = pl.BlockSpec(memory_space=pltpu.VMEM)


def shape(dims, dtype):
    return jax.ShapeDtypeStruct(dims, dtype)


def rate_picks(t, rows, columns, flipped=False):
    whole, own = iota((rows, columns), 1 if flipped else 0), iota((rows, columns), 0 if flipped else 1)
    kind, head = own // OWN, own % OWN
    return ((own < RATES) & (whole == kind * HEADS + t * OWN + head)).astype(BF16)


def pack_in_kernel(lens_ref, w_ref, rates_ref, gains_ref, out_ref):
    rows, width = w_ref.shape[0], w_ref.shape[1] // 4
    picks = (iota((4, EXTRA), 1) == GAIN_AT + iota((4, EXTRA), 0)).astype(BF16)
    beside = dot(gains_ref[...], picks, ((0,), (0,)))
    lane, row = iota((rows, EXTRA), 1), iota((rows, EXTRA), 0)
    for j in range(lens_ref.shape[0]):
        beside = jnp.where((lane == LENS_AT + j) & (row == 0), lens_ref[j].astype(F32), beside)
    for t in range(TP):
        for b in range(4):
            at = b * width + t * BLOCK
            out_ref[t, :, b * BLOCK : (b + 1) * BLOCK] = w_ref[:, at : at + BLOCK]
        rates = dot(rates_ref[...], rate_picks(t, rates_ref.shape[1], EXTRA))
        out_ref[t, :, CORE:WIDE] = (rates + beside).astype(BF16)


def pack_in(lens, w, rates, gains):
    return pl.pallas_call(
        pack_in_kernel,
        in_specs=[SMEM, VMEM, VMEM, VMEM],
        out_specs=VMEM,
        out_shape=shape((TP, w.shape[0], WIDE), BF16),
        **settings(3, 16),
        name="pack_in",
    )(lens, w, rates, gains)


def pack_gu_kernel(w_ref, out_ref):
    ff = w_ref.shape[1] // 2
    own = ff // TP
    for t in range(TP):
        out_ref[t, :, :own] = w_ref[:, t * own : (t + 1) * own]
        out_ref[t, :, own:] = w_ref[:, ff + t * own : ff + (t + 1) * own]


def pack_gu(w):
    return pl.pallas_call(
        pack_gu_kernel,
        in_specs=[VMEM],
        out_specs=VMEM,
        out_shape=shape((TP, w.shape[0], w.shape[1] // TP), BF16),
        **settings(2, 16),
        name="pack_gu",
    )(w)


def join_ffn(got, down):
    columns = got.shape[2]
    top, rows = got.shape[0] * got.shape[1], down.shape[0]
    half = rows // 2

    def kernel(got_ref, down_ref, out_ref):
        for t in range(TP):
            out_ref[t * got.shape[1] : (t + 1) * got.shape[1], :] = got_ref[t]
        out_ref[top : top + rows, :] = down_ref[:, :columns]
        out_ref[top + rows :, : columns // 2] = down_ref[:half, columns:]
        out_ref[top + rows :, columns // 2 :] = down_ref[half:, columns:]

    return pl.pallas_call(
        kernel,
        in_specs=[VMEM, VMEM],
        out_specs=VMEM,
        out_shape=shape((top + rows + half, columns), BF16),
        **settings(2, 16),
        name="join_ffn",
    )(got, down)


def open_ffn(joined, down_rows, width):
    share, _, columns = joined.shape
    own_rows = width // (TP * share)
    top = TP * own_rows
    half = down_rows // 2

    def kernel(in_ref, gu_ref, down_ref):
        for z in range(share):
            for t in range(TP):
                at = (t * share + z) * own_rows
                gu_ref[at : at + own_rows, :] = in_ref[z, t * own_rows : (t + 1) * own_rows, :]
            at = z * down_rows
            down_ref[at : at + down_rows, :columns] = in_ref[z, top : top + down_rows, :]
            down_ref[at : at + half, columns:] = in_ref[z, top + down_rows :, : columns // 2]
            down_ref[at + half : at + down_rows, columns:] = in_ref[z, top + down_rows :, columns // 2 :]

    return pl.pallas_call(
        kernel,
        in_specs=[VMEM],
        out_specs=[VMEM, VMEM],
        out_shape=[shape((width, columns), BF16), shape((share * down_rows, width), BF16)],
        **settings(4, 16),
        name="open_ffn",
    )(joined)


def join_lists(*lists):
    lists = [[x if isinstance(x, tuple) else (x, 0) for x in pieces] for pieces in lists]
    arrays = [x for pieces in lists for x, _ in pieces]

    def kernel(*refs):
        at = 0
        for pieces, out_ref in zip(lists, refs[len(arrays) :]):
            to = 0
            for (x, first), ref in zip(pieces, refs[at : at + len(pieces)]):
                more = x.shape[0] - first
                out_ref[to : to + more, :] = ref[first:, :]
                to += more
            at += len(pieces)

    totals = [(sum(x.shape[0] - first for x, first in pieces), pieces[0][0].shape[1]) for pieces in lists]
    return pl.pallas_call(
        kernel,
        in_specs=[VMEM] * len(arrays),
        out_specs=[VMEM] * len(lists),
        out_shape=[shape(x, BF16) for x in totals],
        **settings(2, 24),
        name="join_rows",
    )(*arrays)


def join_rows(*pieces):
    return join_lists(pieces)[0]


def unpack_in_kernel(got_ref, w_ref, rates_ref, gain_ref, dw_ref, drates_ref, small_ref):
    rows, width = w_ref.shape[0], w_ref.shape[1] // 4
    along = jnp.zeros((rows, 1), F32)
    drates = jnp.zeros((rows, EXTRA), F32)
    sums = jnp.zeros((rows, EXTRA), F32)
    bias = jnp.zeros((rows, EXTRA), F32)
    lane, row = iota((rows, EXTRA), 1), iota((rows, EXTRA), 0)
    for t in range(TP):
        for b in range(4):
            at = b * width + t * BLOCK
            piece = got_ref[t, :, b * BLOCK : (b + 1) * BLOCK].astype(F32)
            dw_ref[:, at : at + BLOCK] = piece
            along = along + jnp.sum(piece * w_ref[:, at : at + BLOCK].astype(F32), axis=1, keepdims=True)
        extra = got_ref[t, :, CORE:WIDE]
        drates = drates + dot(extra, rate_picks(t, EXTRA, EXTRA, True))
        extra = extra.astype(F32)
        sums = sums + extra
        spot = (row // OWN) * HEADS + t * OWN + row % OWN
        bias = bias + jnp.where((lane == spot) & (row < RATES), extra[:, RATES + 2 : RATES + 3], 0.0)
    columns = rates_ref.shape[1]
    drates_ref[...] = drates[:, :columns]
    along = along + jnp.sum(drates[:, :columns] * rates_ref[...].astype(F32), axis=1, keepdims=True)
    turned = jnp.where(lane == 0, along, 0.0) + jnp.where(lane == 1, sums[:, RATES : RATES + 1], 0.0)
    turned = turned + jnp.where(lane == 2, sums[:, RATES + 1 : RATES + 2], 0.0)
    pick = (iota((rows, EXTRA), 0) == iota((rows, EXTRA), 1)).astype(F32)
    turned = dot(turned, pick, ((0,), (0,)), lax.Precision.HIGHEST)
    small_ref[0:1, :] = turned[0:1, :] / gain_ref[...]
    small_ref[1:3, :] = turned[1:3, :]
    small_ref[3:4, :] = jnp.sum(bias, axis=0, keepdims=True)
    small_ref[4:8, :] = jnp.zeros((4, EXTRA), F32)


def unpack_in(got, w, rates, gain):
    rows = w.shape[0]
    gain = jnp.pad(gain.astype(F32)[None], ((0, 0), (0, EXTRA - rows)), constant_values=1.0)
    return pl.pallas_call(
        unpack_in_kernel,
        in_specs=[VMEM] * 4,
        out_specs=[VMEM] * 3,
        out_shape=[shape(w.shape, F32), shape(rates.shape, F32), shape((8, EXTRA), F32)],
        **settings(5, 16),
        name="unpack_in",
    )(got, w, rates, gain)


def unpack_gu_kernel(got_ref, w_ref, gain_ref, dw_ref, small_ref):
    rows, ff = w_ref.shape[0], w_ref.shape[1] // 2
    own = ff // TP
    along = jnp.zeros((rows, 1), F32)
    for t in range(TP):
        for half in range(2):
            at = half * ff + t * own
            piece = got_ref[t, :, half * own : (half + 1) * own].astype(F32)
            dw_ref[:, at : at + own] = piece
            along = along + jnp.sum(piece * w_ref[:, at : at + own].astype(F32), axis=1, keepdims=True)
    lane = iota((rows, EXTRA), 1)
    pick = (iota((rows, EXTRA), 0) == lane).astype(F32)
    turned = dot(jnp.where(lane == 0, along, 0.0), pick, ((0,), (0,)), lax.Precision.HIGHEST)
    small_ref[...] = turned[0:8, :] / gain_ref[...]


def unpack_gu(got, w, gain):
    rows = w.shape[0]
    gain = jnp.pad(gain.astype(F32)[None], ((0, 0), (0, EXTRA - rows)), constant_values=1.0)
    return pl.pallas_call(
        unpack_gu_kernel,
        in_specs=[VMEM] * 3,
        out_specs=[VMEM] * 2,
        out_shape=[shape(w.shape, F32), shape((8, EXTRA), F32)],
        **settings(3, 16),
        name="unpack_gu",
    )(got, w, gain)


def fold(block):
    cut = block.shape[0] // 2
    tail = jnp.concatenate([block[:cut, EXTRA:], block[cut:, EXTRA:]], axis=1)
    return jnp.concatenate([block[:, :EXTRA], tail], axis=0)


def unfold(block):
    rows = 2 * block.shape[0] // 3
    tail = block[rows:]
    tail = jnp.concatenate([tail[:, : BLOCK - EXTRA], tail[:, BLOCK - EXTRA :]], axis=0)
    return jnp.concatenate([block[:rows], tail], axis=1)


def split(field_in, count):
    terms = []
    for _ in range(count):
        terms.append(field_in.astype(BF16))
        field_in = field_in - terms[-1].astype(F32)
    return terms


def dot_split(field_in, picks, count):
    return sum(dot(term, picks) for term in split(field_in, count))


TAIL = 64
SPAN = BLOCK + TAIL
TERMS = 3


def tail_lane(h, term):
    return 8 * h + term


def constants():
    head = np.arange(BLOCK) // HEAD_DIM
    same = head[:, None] == head[None, :]
    extra = np.arange(EXTRA)
    key_lanes = extra[:, None] == OWN + head[None, :]
    value_lanes = extra[:, None] == 2 * OWN + head[None, :]
    to_query = np.zeros((TERMS, EXTRA, TAIL))
    to_key = np.zeros((TERMS, EXTRA, TAIL))
    from_tail = np.zeros((TAIL, EXTRA))
    for h in range(OWN):
        for term in range(TERMS):
            to_query[term, h, tail_lane(h, term)] = 1
            to_key[term, h, tail_lane(h, TERMS + term)] = -1
        from_tail[tail_lane(h, TERMS), h] = 1
    wide = np.concatenate([same, key_lanes, value_lanes], axis=0)
    tails = np.concatenate([to_query.reshape(-1, TAIL), to_key.reshape(-1, TAIL)], axis=0)
    backs = np.concatenate([key_lanes.T, value_lanes.T, from_tail], axis=0)
    return tuple(jnp.asarray(x, BF16) for x in (wide, tails, backs))


def places_of(lens_ref, bucket, rows):
    ends = []
    total = jnp.int32(0)
    for j in range(lens_ref.shape[1]):
        total = total + lens_ref[bucket, j]
        ends.append(total)

    def segment(place):
        seg = jnp.zeros(place.shape, jnp.int32)
        for end in ends:
            seg = seg + (end <= place).astype(jnp.int32)
        return seg

    col = iota((rows, 1), 0)
    row = iota((1, rows), 1)
    seg_col = segment(col)
    allowed = (col <= row) & (segment(row) == seg_col)
    live = (col < total).astype(F32)
    same_prev = ((col > 0) & (seg_col == segment(col - 1))).astype(F32)
    return allowed, live, same_prev


KEPT = ("qn", "kn", "rq", "rk", "ak", "av", "k", "v", "g")
KEPT_LOW = ("qx", "kx", "vb")


def front(proj, bias_ref, gains_ref, wide_ref, tails_ref, same_prev):
    rows = proj.shape[0]
    q = proj[:, 0:BLOCK]
    k = proj[:, BLOCK : 2 * BLOCK]
    v = proj[:, 2 * BLOCK : 3 * BLOCK]
    og = proj[:, 3 * BLOCK : CORE]
    rate = proj[:, CORE:WIDE] + bias_ref[0:1, :]
    sig = jax.nn.sigmoid(rate)
    log_keep = jnp.minimum(rate, 0.0) - jnp.log1p(jnp.exp(-jnp.abs(rate)))
    upto = (iota((rows, rows), 1) <= iota((rows, rows), 0)).astype(BF16)
    decay = sum(dot(upto, term) for term in split(log_keep, TERMS))
    same_head = wide_ref[0:BLOCK]
    ak = dot_split(sig, wide_ref[BLOCK : BLOCK + EXTRA], 2)
    av = dot_split(sig, wide_ref[BLOCK + EXTRA :], 2)
    ks = ak * shifted(k, same_prev) + (1.0 - ak) * k
    vs = av * shifted(v, same_prev) + (1.0 - av) * v

    def head_norm(u):
        factor = lax.rsqrt(dot_split(u * u, same_head, 2) * (1.0 / HEAD_DIM) + EPS)
        return u * factor, factor

    qn, rq = head_norm(q)
    kn, rk = head_norm(ks)
    q_gain, k_gain = gains_ref[0:1, 0:BLOCK], gains_ref[1:2, 0:BLOCK]
    qb = (qn * q_gain).astype(BF16) * jnp.asarray(HEAD_DIM**-0.5, BF16)
    kb = (kn * k_gain).astype(BF16)

    terms = split(decay, TERMS)
    lane = iota((1, TAIL), 1)
    ones_q = ((lane % 8 >= TERMS) & (lane % 8 < 2 * TERMS)).astype(F32)
    ones_k = (lane % 8 < TERMS).astype(F32)
    q_tail = ones_q + sum(dot(terms[t], tails_ref[t * EXTRA : (t + 1) * EXTRA]) for t in range(TERMS))
    k_tail = ones_k + sum(
        dot(terms[t], tails_ref[(TERMS + t) * EXTRA : (TERMS + t + 1) * EXTRA]) for t in range(TERMS)
    )
    qx = jnp.concatenate([qb, q_tail.astype(BF16)], axis=1)
    kx = jnp.concatenate([kb, k_tail.astype(BF16)], axis=1)
    return dict(
        qn=qn, kn=kn, rq=rq, rk=rk, ak=ak, av=av, k=k, v=v, g=jax.nn.sigmoid(og),
        qx=qx, kx=kx, vb=vs.astype(BF16), vs=vs, sig=sig,
    )


def shifted(array, same_prev):
    return pltpu.roll(array, 1, 0) * same_prev


def head_masks(rows):
    span = iota((rows, SPAN), 1)
    masks = []
    for h in range(OWN):
        feature = (span >= h * HEAD_DIM) & (span < (h + 1) * HEAD_DIM)
        masks.append(feature | ((span >= BLOCK + 8 * h) & (span < BLOCK + 8 * (h + 1))))
    return masks


def scores_of(qx, kx, mask, allowed):
    qh = jnp.where(mask, qx, jnp.zeros_like(qx))
    return jnp.where(allowed, dot(kx, qh, ((1,), (1,))), NEG), qh


def head_rows(h):
    return slice(h * HEAD_DIM, (h + 1) * HEAD_DIM)


def attn_fwd_kernel(
    lens_ref, spots_ref, near_ref, far_ref, w_ref, bias_ref, wide_ref, tails_ref,
    h1_ref, mixed_ref, att_ref, lse_ref, gains_ref, heads_ref, sig_ref, *kept_refs
):
    picks = (iota((8, EXTRA), 1) == GAIN_AT + iota((8, EXTRA), 0)) & (iota((8, EXTRA), 0) < 4)
    picks = picks.astype(BF16)
    gains = dot(picks, w_ref[:, CORE:WIDE], ((1,), (1,)))
    gains_ref[...] = gains
    at = pl.multiple_of(spots_ref[0] * BLOCK, BLOCK)
    heads = dot(picks, w_ref[pl.ds(at, BLOCK), CORE:WIDE], ((1,), (1,)))
    heads_ref[0:1, 0:BLOCK] = heads[1:2]
    heads_ref[1:2, 0:BLOCK] = heads[2:3]
    tok = jnp.where(pl.program_id(0) < 4, near_ref[...], far_ref[...]).astype(F32)
    h1 = (normed(tok)[0] * gains[0:1]).astype(BF16)
    h1_ref[...] = h1
    rows = h1.shape[0]
    allowed, live, same_prev = places_of(lens_ref, pl.program_id(0), rows)
    f = front(dot(h1, w_ref[...]), bias_ref, heads_ref, wide_ref, tails_ref, same_prev)
    sig_ref[...] = f["sig"]
    for name, ref in zip(KEPT + KEPT_LOW, kept_refs):
        ref[...] = f[name]
    vt = f["vs"].T.astype(BF16)
    att = []
    for h, mask in enumerate(head_masks(rows)):
        s, _ = scores_of(f["qx"], f["kx"], mask, allowed)
        top = jnp.max(s, axis=0, keepdims=True)
        e = jnp.exp(s - top)
        total = jnp.sum(e, axis=0, keepdims=True)
        prob = (e * (1.0 / total)).astype(BF16)
        att.append(dot(vt[head_rows(h)], prob))
        lse_ref[h : h + 1, :] = top + jnp.log(total)
    att = jnp.concatenate(att, axis=0).T
    att_ref[...] = att
    mixed_ref[0] = fold(att * f["g"] * live).astype(BF16)


def attn_bwd_kernel(
    lens_ref, spots_ref, gains_ref, wide_ref, backs_ref, w_ref, att_ref, lse_ref, dm_ref, sig_ref, *refs
):
    kept = KEPT + KEPT_LOW
    f = {name: ref[...] for name, ref in zip(kept, refs)}
    dp_ref, sums_ref, near_ref, far_ref = refs[len(kept) :]
    bucket = pl.program_id(0)
    rows = att_ref.shape[0]
    allowed, live, same_prev = places_of(lens_ref, bucket, rows)
    masks = head_masks(rows)
    same_head = wide_ref[0:BLOCK]
    q_gain, k_gain = gains_ref[0:1, 0:BLOCK], gains_ref[1:2, 0:BLOCK]
    dm = unfold(dm_ref[0].astype(F32)) * live
    g, vb = f["g"], f["vb"]
    dab = (dm * g).astype(BF16)
    dog = dm * att_ref[...] * g * (1.0 - g)
    kt = f["kx"][:, :BLOCK].astype(F32).T.astype(BF16)
    zero = jnp.zeros((rows, BLOCK), BF16)
    dkx = jnp.zeros((rows, SPAN), F32)
    dvb = jnp.zeros((rows, BLOCK), F32)
    tail = jnp.zeros((TAIL, rows), F32)
    dqt = []
    for h in range(OWN):
        s, qh = scores_of(f["qx"], f["kx"], masks[h], allowed)
        p = jnp.exp(s - lse_ref[h : h + 1, :])
        dab_h = jnp.where(masks[h][:, :BLOCK], dab, zero)
        dvb = dvb + dot(p.astype(BF16), dab_h)
        dp = dot(vb, dab_h, ((1,), (1,)))
        ds = p * (dp - jnp.sum(p * dp, axis=0, keepdims=True))
        dsb = ds.astype(BF16)
        dqt.append(dot(kt[head_rows(h)], dsb))
        dkx = dkx + dot(dsb, qh)
        along = jnp.sum(dsb.astype(F32), axis=0, keepdims=True)
        tail = jnp.where(iota((TAIL, rows), 0) == tail_lane(h, TERMS), along, tail)
    dqx = jnp.concatenate(dqt + [tail], axis=0).T
    dqb = dqx[:, :BLOCK] * HEAD_DIM**-0.5
    dkb = dkx[:, :BLOCK]

    def back(n, r, e):
        return r * (e - n * (dot_split(e * n, same_head, 2) * (1.0 / HEAD_DIM)))

    dq = back(f["qn"], f["rq"], dqb * q_gain)
    dks = back(f["kn"], f["rk"], dkb * k_gain)
    last = iota((rows, 1), 0) == rows - 1

    def mix_back(grad, rate, cur, prev):
        ahead = pltpu.roll(rate * grad * same_prev, rows - 1, 0)
        return (1.0 - rate) * grad + jnp.where(last, 0.0, ahead), grad * (prev - cur)

    dk, dak = mix_back(dks, f["ak"], f["k"], shifted(f["k"], same_prev))
    dv, dav = mix_back(dvb, f["av"], f["v"], shifted(f["v"], same_prev))

    onward = (iota((rows, rows), 1) >= iota((rows, rows), 0)).astype(BF16)
    keep = sum(dot(onward, term) for term in split(dqx[:, BLOCK:] - dkx[:, BLOCK:], TERMS))
    sig = sig_ref[...]
    drate = (
        dot_split(dak, backs_ref[0:BLOCK], 2)
        + dot_split(dav, backs_ref[BLOCK : 2 * BLOCK], 2)
        + dot_split(keep, backs_ref[2 * BLOCK :], 2)
    )
    lane = iota((rows, EXTRA), 1)
    drate = drate * (1.0 - sig) * jnp.where(lane < OWN, 1.0, sig)
    drate = jnp.where(lane < RATES, drate, 0.0)
    grads = jnp.concatenate([dq, dk, dv, dog, drate], axis=1).astype(BF16)
    dp_ref[...] = grads
    dh1 = dot(grads, w_ref[...], ((1,), (1,))).astype(BF16)

    @pl.when(bucket < 4)
    def _():
        near_ref[...] = dh1

    @pl.when(bucket >= 4)
    def _():
        far_ref[...] = dh1

    @pl.when(bucket == 0)
    def _():
        sums_ref[...] = jnp.zeros_like(sums_ref)

    sums_ref[0:1, 0:BLOCK] += jnp.sum(dqb * f["qn"], axis=0, keepdims=True)
    sums_ref[1:2, 0:BLOCK] += jnp.sum(dkb * f["kn"], axis=0, keepdims=True)
    sums_ref[2:3, 0:EXTRA] += jnp.sum(drate, axis=0, keepdims=True)


def rows_spec(rows, width):
    return pl.BlockSpec((rows, width), lambda i, lens, spots: (i, 0))


def whole_spec(dims):
    return pl.BlockSpec(dims, lambda i, lens, spots: (0,) * len(dims))


def spot_spec(rows):
    return pl.BlockSpec((1, rows * 3 // 2, EXTRA), lambda i, lens, spots: (spots[i], 0, 0))


def kept_specs(rows):
    return [rows_spec(rows, BLOCK) for _ in KEPT] + [rows_spec(rows, c) for c in (SPAN, SPAN, BLOCK)]


def attn_fwd(lens, spots, near, far, w, bias, wide, tails):
    buckets = lens.shape[0]
    width = near.shape[1]
    total = 2 * near.shape[0]
    rows = total // buckets
    return pl.pallas_call(
        attn_fwd_kernel,
        grid_spec=pltpu.PrefetchScalarGridSpec(
            num_scalar_prefetch=2,
            grid=(buckets,),
            in_specs=[
                near_spec(rows, width),
                far_spec(rows, width),
                whole_spec(w.shape),
                whole_spec(bias.shape),
                whole_spec(wide.shape),
                whole_spec(tails.shape),
            ],
            out_specs=[
                rows_spec(rows, width),
                spot_spec(rows),
                rows_spec(rows, BLOCK),
                rows_spec(8, rows),
                whole_spec((8, width)),
                whole_spec((8, 2 * EXTRA)),
                rows_spec(rows, EXTRA),
            ]
            + kept_specs(rows),
        ),
        out_shape=[
            shape((total, width), BF16),
            shape((buckets, rows * 3 // 2, EXTRA), BF16),
            shape((total, BLOCK), F32),
            shape((8 * buckets, rows), F32),
            shape((8, width), F32),
            shape((8, 2 * EXTRA), F32),
            shape((total, EXTRA), F32),
        ]
        + [shape((total, BLOCK), F32) for _ in KEPT]
        + [shape((total, c), BF16) for c in (SPAN, SPAN, BLOCK)],
        **settings(20, 60),
        name="attn_fwd",
    )(lens, spots, near, far, w, bias, wide, tails)


def near_spec(rows, width):
    return pl.BlockSpec((rows, width), lambda i, lens, spots: (jnp.minimum(i, 3), 0))


def far_spec(rows, width):
    return pl.BlockSpec((rows, width), lambda i, lens, spots: (jnp.maximum(i - 4, 0), 0))


def attn_bwd(lens, spots, gains, wide, backs, w, att, lse, dm, sig, *kept):
    buckets = lens.shape[0]
    total = att.shape[0]
    width = w.shape[0]
    rows = total // buckets
    return pl.pallas_call(
        attn_bwd_kernel,
        grid_spec=pltpu.PrefetchScalarGridSpec(
            num_scalar_prefetch=2,
            grid=(buckets,),
            in_specs=[whole_spec(x.shape) for x in (gains, wide, backs, w)]
            + [rows_spec(rows, BLOCK), rows_spec(8, rows), spot_spec(rows), rows_spec(rows, EXTRA)]
            + kept_specs(rows),
            out_specs=[
                rows_spec(rows, WIDE),
                whole_spec((8, 2 * EXTRA)),
                near_spec(rows, width),
                far_spec(rows, width),
            ],
        ),
        out_shape=[shape((total, WIDE), BF16), shape((8, 2 * EXTRA), F32)]
        + [shape((total // 2, width), BF16)] * 2,
        **settings(24, 60),
        name="attn_bwd",
    )(lens, spots, gains, wide, backs, w, att, lse, dm, sig, *kept)


def mid_fwd_kernel(spots_ref, got_ref, tok_ref, gain_ref, *refs):
    x2_ref, h2_ref = refs[TP:]
    acc = tok_ref[...].astype(F32)
    for i in range(TP):
        acc = acc + dot(unfold(got_ref[spots_ref[i]]), refs[i][...])
    x2_ref[...] = acc
    h2_ref[...] = (normed(acc)[0] * gain_ref[...]).astype(BF16)


def once(dims):
    return pl.BlockSpec(dims, lambda i: (0,) * len(dims))


def mix_specs(w):
    return [once((BLOCK, x.shape[1])) for x in w]


def mid_fwd(spots, got, w, tok, gain):
    rows, width = tok.shape
    return pl.pallas_call(
        mid_fwd_kernel,
        grid=(1,),
        in_specs=[SMEM, once(got.shape), once(tok.shape), once(gain.shape)] + mix_specs(w),
        out_specs=[once(tok.shape)] * 2,
        out_shape=[shape(tok.shape, F32), shape(tok.shape, BF16)],
        **settings(5, 40),
        name="mid_fwd",
    )(spots, got, tok, gain, *w)


def mid_bwd_kernel(spots_ref, a_ref, b_ref, c_ref, d_ref, x2_ref, cot_ref, gain_ref, got_ref, *refs):
    dx2_ref, dm_ref, near_ref, far_ref = refs[TP:]
    dh2 = a_ref[...] + b_ref[...].astype(F32) + c_ref[...].astype(F32) + d_ref[...].astype(F32)
    n2, r2 = normed(x2_ref[...])
    dx2 = cot_ref[...].astype(F32) + norm_back(n2, r2, dh2 * gain_ref[...])
    dx2_ref[...] = dx2
    dxb = dx2.astype(BF16)
    for i in range(TP):
        dm = dot(dxb, refs[i][...], ((1,), (1,)))
        dm_ref[spots_ref[i]] = fold(dm).astype(BF16)
        out_ref = near_ref if i < 4 else far_ref
        piece = dot(unfold(got_ref[spots_ref[i]]), dxb, ((0,), (0,)))
        out_ref[(i % 4) * BLOCK : (i % 4 + 1) * BLOCK, :] = piece.astype(BF16)


def mid_bwd(spots, parts, x2, cot, gain, got, w):
    rows, width = x2.shape
    arrays = (*parts, x2, cot, gain, got)
    outs = [
        shape((rows, width), F32),
        shape((TP, rows * 3 // 2, EXTRA), BF16),
        shape((4 * BLOCK, width), BF16),
        shape((4 * BLOCK, width), BF16),
    ]
    return pl.pallas_call(
        mid_bwd_kernel,
        grid=(1,),
        in_specs=[SMEM] + [once(x.shape) for x in arrays] + mix_specs(w),
        out_specs=[once(x.shape) for x in outs],
        out_shape=outs,
        **settings(9, 48),
        name="mid_bwd",
    )(spots, *arrays, *w)


def fold_cores(near, far):
    width = near.shape[1]
    rows = near.shape[0] // 4
    steps = 4

    def kernel(*refs):
        for i in range(4):
            both = refs[i][...].astype(F32) + refs[4 + i][...].astype(F32)
            refs[8 + i][...] = both.astype(refs[8 + i].dtype)

    def quarter(i):
        return pl.BlockSpec((rows // steps, width), lambda j: (i * steps + j, 0))

    return pl.pallas_call(
        kernel,
        grid=(steps,),
        in_specs=[quarter(i) for i in range(4)] * 2,
        out_specs=[pl.BlockSpec((rows // steps, width), lambda j: (j, 0))] * 4,
        out_shape=[shape((rows, width), F32)] + [shape((rows, width), BF16)] * 3,
        **settings(4, 32),
        name="fold_cores",
    )(near, near, near, near, far, far, far, far)


def last_norm(tok, gain, dx2, *parts):
    rows, width = tok.shape
    steps = 4

    def kernel(tok_ref, gain_ref, dx2_ref, *refs):
        n1, r1 = normed(tok_ref[...].astype(F32))
        refs[-1][...] = dx2_ref[...] + norm_back(n1, r1, total_of([x[...] for x in refs[:-1]]) * gain_ref[...])

    block = pl.BlockSpec((rows // steps, width), lambda i: (i, 0))
    return pl.pallas_call(
        kernel,
        grid=(steps,),
        in_specs=[block, once(gain.shape), block] + [block] * len(parts),
        out_specs=block,
        out_shape=shape((rows, width), F32),
        **settings(3, 24),
        name="last_norm",
    )(tok, gain, dx2, *parts)


def ffn_kernel(lens_ref, h2_ref, cot_ref, gu_ref, dn_ref, ab_ref, dgu_ref, *out_refs):
    rows, ff = h2_ref.shape[0], dn_ref.shape[0]
    total = jnp.int32(0)
    for j in range(lens_ref.shape[1]):
        total = total + lens_ref[pl.program_id(0), j]
    live = (iota((rows, 1), 0) < total).astype(F32)
    gu = dot(h2_ref[...], gu_ref[...])
    da = dot(cot_ref[...], dn_ref[...], ((1,), (1,))) * live
    gate, up = gu[:, :ff], gu[:, ff:]
    sg = jax.nn.sigmoid(gate)
    act = gate * sg
    ab = (act * up * live).astype(BF16)
    dgate = (da * up * sg * (1.0 + gate * (1.0 - sg))).astype(BF16)
    dup = (da * act).astype(BF16)
    ab_ref[...] = ab
    dgu_ref[:, :ff] = dgate
    dgu_ref[:, ff:] = dup
    dh2 = dot(dgate, gu_ref[:, :ff], ((1,), (1,))) + dot(dup, gu_ref[:, ff:], ((1,), (1,)))
    dh2 = dh2.astype(BF16)
    out = dot(ab, dn_ref[...]).astype(BF16)
    near = pl.program_id(0) < pl.num_programs(0) // 2

    @pl.when(near)
    def _():
        out_refs[0][...] = out
        out_refs[1][...] = dh2

    @pl.when(jnp.logical_not(near))
    def _():
        out_refs[2][...] = out
        out_refs[3][...] = dh2


def ffn(lens, h2, cot, gu, dn):
    buckets = lens.shape[0]
    half = buckets // 2
    total, width = h2.shape
    rows = total // buckets
    ff = dn.shape[0]

    def block(columns):
        return pl.BlockSpec((rows, columns), lambda i: (i, 0))

    def whole(dims):
        return pl.BlockSpec(dims, lambda i: (0, 0))

    near = pl.BlockSpec((rows, width), lambda i: (jnp.minimum(i, half - 1), 0))
    far = pl.BlockSpec((rows, width), lambda i: (jnp.maximum(i - half, 0), 0))
    return pl.pallas_call(
        ffn_kernel,
        grid=(buckets,),
        in_specs=[SMEM, block(width), block(width), whole(gu.shape), whole(dn.shape)],
        out_specs=[block(ff), block(2 * ff), near, near, far, far],
        out_shape=[shape((total, ff), BF16), shape((total, 2 * ff), BF16)] + [shape((total // 2, width), BF16)] * 4,
        **settings(4 * buckets, 34),
        name="ffn",
    )(lens, h2, cot, gu, dn)


def sum_of_dots(lefts, rights):
    return sum(dot(x[...], y[...], ((0,), (0,))) for x, y in zip(lefts, rights))


def grad_down(ab, cot):
    ff, width = ab[0].shape[1], cot[0].shape[1]
    steps = 4
    columns = width // steps
    count = len(ab)

    def kernel(*refs):
        refs[-1][...] = sum_of_dots(refs[:count], refs[count : 2 * count]).astype(BF16)

    return pl.pallas_call(
        kernel,
        grid=(steps,),
        in_specs=[pl.BlockSpec(x.shape, lambda i: (0, 0)) for x in ab]
        + [pl.BlockSpec((x.shape[0], columns), lambda i: (0, i)) for x in cot],
        out_specs=pl.BlockSpec((ff, columns), lambda i: (0, i)),
        out_shape=shape((ff, width), BF16),
        **settings(6, 24),
        name="grad_down",
    )(*ab, *cot)


def grad_gu(h2, dgu, share):
    width = h2[0].shape[1]
    own_rows = width // (TP * share)
    columns = dgu[0].shape[1]
    steps = TP // 2
    count = len(h2)

    def kernel(*refs):
        res = sum_of_dots(refs[:count], refs[count : 2 * count])
        for k in range(2):
            for z in range(share):
                at = (k * share + z) * own_rows
                refs[-1][z, k] = res[at : at + own_rows].astype(BF16)

    return pl.pallas_call(
        kernel,
        grid=(steps,),
        in_specs=[pl.BlockSpec((x.shape[0], width // steps), lambda i: (0, i)) for x in h2]
        + [pl.BlockSpec(x.shape, lambda i: (0, 0)) for x in dgu],
        out_specs=pl.BlockSpec((share, 2, own_rows, columns), lambda i: (0, i, 0, 0)),
        out_shape=shape((share, TP, own_rows, columns), BF16),
        **settings(11, 36),
        name="grad_gu",
    )(*h2, *dgu)


def grad_in(place, sums, left, right, share):
    own_rows = left.shape[1] // (TP * share)
    columns = right.shape[1]
    steps = TP // 2

    def kernel(place_ref, sums_ref, left_ref, right_ref, out_ref):
        res = dot(left_ref[...], right_ref[...], ((0,), (0,)))
        lane, row = iota((BLOCK, EXTRA), 1), iota((BLOCK, EXTRA), 0)
        turned = sums_ref[...].T[0:BLOCK]
        bias = jnp.where((lane == row % own_rows) & (lane < RATES), sums_ref[2:3, 0:EXTRA], 0.0)
        bias = jnp.sum(bias, axis=1, keepdims=True)
        for k in range(2):
            mine = (pl.program_id(0) * 2 + k == place_ref[0]).astype(F32)
            extra = res[k * BLOCK : (k + 1) * BLOCK, CORE:WIDE]
            extra = jnp.where(lane == RATES, turned[:, 0:1] * mine, extra)
            extra = jnp.where(lane == RATES + 1, turned[:, 1:2] * mine, extra)
            extra = jnp.where(lane == RATES + 2, bias, extra)
            for z in range(share):
                at = z * own_rows
                rest = k * BLOCK + at
                out_ref[z, k, :, :CORE] = res[rest : rest + own_rows, :CORE].astype(BF16)
                out_ref[z, k, :, CORE:] = extra[at : at + own_rows].astype(BF16)

    return pl.pallas_call(
        kernel,
        grid=(steps,),
        in_specs=[
            SMEM,
            pl.BlockSpec(sums.shape, lambda i: (0, 0)),
            pl.BlockSpec((left.shape[0], left.shape[1] // steps), lambda i: (0, i)),
            pl.BlockSpec(right.shape, lambda i: (0, 0)),
        ],
        out_specs=pl.BlockSpec((share, 2, own_rows, columns), lambda i: (0, i, 0, 0)),
        out_shape=shape((share, TP, own_rows, columns), BF16),
        **settings(11, 60),
        name="grad_in",
    )(place, sums, left, right)


def own_share(part):
    columns = part.shape[-1]
    summed = lax.psum_scatter(part.reshape(-1, columns), "sh", scatter_dimension=0, tiled=True)
    return summed.reshape(TP, -1, columns)


def swap(blocks):
    return lax.all_to_all(blocks, "tp", 0, 0, tiled=True)


def body(
    tokens,
    doc_lengths,
    norm_gain,
    w_attn_in,
    w_rates,
    rate_bias,
    q_gain,
    k_gain,
    w_out,
    ffn_gain,
    w_gate_up,
    w_down,
    cotangent,
):
    place = lax.axis_index("tp")
    share = lax.axis_size("sh")
    width = tokens.shape[1]
    own_rows = w_attn_in.shape[0]
    spots = place ^ jnp.array(OFFSETS, jnp.int32)

    gains = jnp.stack([norm_gain, q_gain, k_gain, ffn_gain])
    packed, w_mix = phase(pack_in(doc_lengths, w_attn_in, w_rates, gains), w_out)
    got_in = swap(packed)
    w_in = lax.all_gather(got_in, "sh", axis=1).reshape(width, WIDE)
    lens_all = got_in[:, 0, CORE + LENS_AT : CORE + LENS_AT + doc_lengths.shape[0]].astype(jnp.int32)
    lens = lens_all[spots]
    bias = lax.dynamic_index_in_dim(rate_bias.reshape(3, TP, OWN), place, 1, False).reshape(1, RATES)
    bias = jnp.pad(bias, ((0, 7), (0, EXTRA - RATES)))

    tok, w_gu, w_mix, _ = phase(tokens, w_gate_up, w_mix, got_in)
    two_four, w_mix = phase(sides(tok), gather_shares(w_mix))
    tok = join_rows(tok, *two_four, *diagonal(*two_four))
    tok, packed = phase(tok, pack_gu(w_gu))
    joined = join_ffn(swap(packed), w_down)
    far = flip(tok, 1)
    w_gu, w_dn = open_ffn(lax.all_gather(joined, "sh", axis=0), w_down.shape[0], width)

    wide, tails, backs = constants()
    beside = phase(join_rows(in_order(w_mix), cotangent), joined)[0]
    two_four = sides(beside)
    h1, mixed, att, lse, gains, gain_heads, *kept = attn_fwd(lens, spots, tok, far, w_in, bias, wide, tails)
    gain_one, gain_two = gains[0:1], gains[3:4]
    mixed, two_four = phase(mixed, two_four)
    near = [beside, *two_four]
    got_mixed, mix_six, far = phase(
        swap(mixed), diagonal(*[x[:BLOCK] for x in two_four]), [flip(x, 1) for x in near]
    )
    mix_six = jnp.concatenate(mix_six, axis=0)
    w_mix = [*near, mix_six, *far, flip(mix_six, 1)]
    x2, h2 = mid_fwd(spots, got_mixed, w_mix, tokens, gain_two)

    orders = (2, 4, 3, 5), (0, 1), (6, 7)
    lens_of = [jnp.stack([lens[OFFSETS.index(d)] for d in order]) for order in orders]
    h2, near, far = phase(h2, near, far)
    cot = [
        join_rows(*[(half[i], BLOCK) for half in (near, far) for i in (1, 2)]),
        join_rows((near[0], BLOCK), (far[0], BLOCK)),
    ]
    (two, four), one, cot = phase(sides(h2), flip(h2, 1), cot)
    six = diagonal(two, four)
    two, four, three, five, one = phase(two, four, flip(two, 1), flip(four, 1), one)
    h2 = [join_rows(two, four, three, five), join_rows(h2, one)]
    found = [ffn(lens_of[0], h2[0], cot[0], w_gu, w_dn)]
    found, six, h2[1], cot_six = phase(found, six, h2[1], diagonal(*[x[BLOCK:] for x in near[1:3]]))
    six, cot_six = join_lists(six, cot_six)
    seven, cot_seven, far, more = phase(
        flip(six, 1),
        flip(cot_six, 1),
        [flip(x, 1) for x in found[0][4:]],
        ffn(lens_of[1], h2[1], cot[1], w_gu, w_dn),
    )
    found.append(more)
    side = [x.astype(BF16) for x in two_sums(found[0][3], far[1])]
    h2.append(join_rows(six, seven))
    cot.append(join_rows(cot_six, cot_seven))
    side, h2[2], cot[2], one = phase(side, h2[2], cot[2], found[1][5])
    side = flip(side[0], 2), flip(side[1], 4)
    one, more = phase(flip(one, 1), ffn(lens_of[2], h2[2], cot[2], w_gu, w_dn))
    found.append(more)
    ab, dgu, out_near, dh2_near, out_far, dh2_far = zip(*found)
    seven, dw_dn, side = phase(flip(dh2_far[2], 1), grad_down(ab, cot), side)
    dw_dn = lax.psum_scatter(dw_dn, "sh", scatter_dimension=0, tiled=True)
    low = (dh2_near[2].astype(F32) + seven.astype(F32)).astype(BF16)
    low, dgu, out_far, far = phase(low, dgu, out_far, far)
    own = dh2_near[1].astype(F32) + one.astype(F32)
    six, dw_gu, out_far, own = phase(flip(low, 6), grad_gu(h2, dgu, share), [flip(x, 1) for x in out_far[1:]], own)
    dw_gu = own_share(dw_gu)
    layer_side = [x.astype(BF16) for x in two_sums(out_near[0], far[0])]
    layer_six = (out_near[2].astype(F32) + out_far[1].astype(F32)).astype(BF16)
    dh2, layer_low = phase((own, *side, six), (*layer_side, layer_six))

    found, layer_low = phase(
        mid_bwd(spots, dh2, x2, cotangent, gain_two, got_mixed, w_mix), relay_six(layer_low)
    )
    dx2, dm, mix_near, mix_far = found
    mix_own, mix_low = both_cores(quarters(mix_near), quarters(flip(mix_far, 1)))
    got_dm, mix_own, mix_low, layer_low = phase(swap(dm), mix_own, mix_low, add_six(layer_low))
    layer, mix_low, found, dw_dn = phase(
        (flip(layer_low[0], 2), flip(layer_low[1], 4)),
        relay_six(mix_low),
        attn_bwd(lens, spots, gain_heads, wide, backs, w_in, att, lse, got_dm, *kept),
        dw_dn,
    )
    dp, sums, dh1_near, dh1_far = found

    dh1_far, dw_in, dw_gu, mix_low = phase(
        flip(dh1_far, 1), grad_in(place.reshape(1), sums, h1, dp, share), dw_gu, add_six(mix_low)
    )
    mix = flip(mix_low[0], 2), flip(mix_low[1], 4)
    dw_in = own_share(dw_in)
    dh1_own, *dh1_low = fold_cores(dh1_near, dh1_far)
    dh1_low, mix = phase(relay_six(dh1_low), mix)
    layer_own = out_near[1].astype(F32) + out_far[0].astype(F32)
    layer_out = (x2 + total_of((layer_own, *layer))).astype(BF16)
    two, four = add_six(dh1_low)
    mix = total_of((mix_own, *mix)).astype(BF16)
    dh1, got_gu, dw_in, layer_out, mix = phase(
        (flip(two, 2), flip(four, 4)), swap(dw_gu), dw_in, layer_out, mix
    )
    mix = to_shares(mix)
    d_tokens = last_norm(tokens, gain_one, dx2, dh1_own, *dh1)

    d_w_attn_in, d_w_rates, small = unpack_in(swap(dw_in), w_attn_in, w_rates, norm_gain)
    d_w_gate_up, small_gu = unpack_gu(got_gu, w_gate_up, ffn_gain)
    d_ffn_gain = small_gu[0, :own_rows]
    small, mix = phase(small, mix)
    d_w_out = total_of(mix)
    return (
        layer_out,
        d_tokens,
        small[0, :own_rows],
        d_w_attn_in,
        d_w_rates,
        small[3, : w_rates.shape[1]],
        small[1, :own_rows],
        small[2, :own_rows],
        d_w_out,
        d_ffn_gain,
        d_w_gate_up,
        dw_dn.astype(F32),
    )


def solution(mesh):
    devices = mesh.devices.reshape(TP, -1)
    grid = Mesh(devices, ("tp", "sh"))
    rows = P(("tp", "sh"), None)
    flat = P(("tp", "sh"))
    in_specs = (rows, flat, flat, rows, rows, P(), flat, flat, rows, flat, rows, rows, rows)
    out_specs = (rows, rows, flat, rows, rows, P(), flat, flat, rows, flat, rows, rows)
    return jax.shard_map(body, mesh=grid, in_specs=in_specs, out_specs=out_specs, check_vma=False)
```
